32 devices in a mesh: gx: 4 (over z), gy: 4 (over x, core), gz: 2 (over y).
Axes of the slice: x: 2, y: 2, z: 4, core: 2. Of those that a mesh axis runs over, the one named last changes fastest.
Arguments:
- terminal_adjoint: float32 [5, 32, 32, 256], P(None, 'gx', 'gy', 'gz'), may hold values from -6 to 6
- density: float32 [32, 32, 256], P('gx', 'gy', 'gz'), may hold values from 0.7 to 1.5
- velocity: float32 [3, 32, 32, 256], P(None, 'gx', 'gy', 'gz'), may hold values from -0.5 to 0.5
- stiffness: float32 [32, 32, 256], P('gx', 'gy', 'gz'), may hold values from 0.6 to 1.6
- sponge: float32 [32, 32, 256], P('gx', 'gy', 'gz'), may hold values from 0.1 to 3
- source_shape: float32 [32, 32, 256], P('gx', 'gy', 'gz'), may hold values from -0.1875 to 0.1875
- brick_level: int32 [4, 4, 2], replicated, may hold values from 0 to 1
- brick_patch: int32 [4, 4, 2], replicated, may hold values from 0 to 31, as said below
- patch_owner: int32 [32], replicated, may hold values from 0 to 31, as said below
Outputs:
- adjoint: float32 [5, 32, 32, 256], P(None, 'gx', 'gy', 'gz')
- patch_gradient: float32 [32, 40], P(('gx', 'gy', 'gz'))
The draws below stay inside these ranges and needn't reach their ends.
Inputs may be any that keep to these rules, and one draw needn't show every extreme that they name: `brick_patch`: each brick names one patch; a patch may be named by several bricks or by none. `patch_owner`: every device owns exactly one patch.
All inputs are finite; a program needn't handle non-finite values.
Results may differ from the reference program's by a relative error of at most 0.00013.
Values sent between devices are 32-bit elements; how exact they have to be, the bound alone decides.
No kernel may reach another device: no remote copies, remote signals or barrier semaphores. Data moves between devices by JAX's collectives and lax.ppermute only.
A program may use at most 64 MiB of HBM per device.

```python
import math
import jax
import jax.numpy as jnp

CX = 8
CY = 8
CZ = 128
BX = 8
BY = 8
BZ = 16
STEPS = 1
NX = 32
NY = 32
NZ = 256
PATCHES = 32
KBLOCK = 40
N_GX = 4
N_GY = 4
N_GZ = 2


def joint_routing(key):
    owner = jax.random.permutation(jax.random.fold_in(key, 11), PATCHES).astype(jnp.int32)
    device_patch = jnp.zeros((PATCHES,), jnp.int32).at[owner].set(jnp.arange(PATCHES, dtype=jnp.int32))
    bricks = jnp.arange(PATCHES, dtype=jnp.int32)
    kinds = jax.random.randint(jax.random.fold_in(key, 12), (PATCHES,), 0, 4)
    random_target = jax.random.randint(jax.random.fold_in(key, 13), (PATCHES,), 0, PATCHES)
    half_count = PATCHES // 2
    target = jnp.where(kinds == 0, bricks, jnp.where(kinds == 1, (bricks + half_count) % PATCHES, jnp.where(kinds == 2, (bricks + 1) % PATCHES, random_target)))
    target = target.at[half_count].set(0).at[1].set(0).at[2].set(3)
    return (owner, device_patch[target].astype(jnp.int32))


def draw_patch_owner(key, part):
    owner, patches = joint_routing(key)
    return owner


def draw_brick_patch(key, part):
    owner, patches = joint_routing(key)
    return patches.reshape(N_GX, N_GY, N_GZ)


def set_ends(result, key, smallest, high):
    index_at = [jax.random.randint(jax.random.fold_in(key, axis), (), 0, length) for axis, length in enumerate(result.shape)]
    main_axis = result.shape.index(max(result.shape))
    next_to = index_at[:main_axis] + [(index_at[main_axis] + 1) % result.shape[main_axis]] + index_at[main_axis + 1:]
    return result.at[tuple(index_at)].set(smallest).at[tuple(next_to)].set(high)


def levels(key, extent, shards, low, largest):
    gain, own = 1.0, jax.random.fold_in(key, 6)
    for axis_at, parts in shards:
        steps = jnp.exp(jax.random.uniform(jax.random.fold_in(own, axis_at), (parts,), jnp.float32, low / len(shards), largest / len(shards)))
        gain = gain * jnp.repeat(steps, extent[axis_at] // parts).reshape([-1 if axis == axis_at else 1 for axis in range(len(extent))])
    return gain


def gaussian(rng, dims, scale, limit, cuts=(), kind=jnp.bfloat16):
    drawn = jax.random.normal(rng, dims, jnp.float32) * scale
    if len(cuts) > 0:
        drawn = levels(rng, dims, cuts, -0.22, 0.18) * drawn
    return jnp.clip(drawn, min=-limit, max=limit).astype(kind)


def setup_inputs(seed: int = 0) -> dict:
    arg_keys = jax.random.split(jax.random.key(seed), 10)
    terminal_adjoint = gaussian(arg_keys[0], (5, NX, NY, NZ), 1.0, 6.0, ((1, 4), (2, 4), (3, 2)), jnp.float32)
    density = jnp.clip(jnp.exp(math.log(1.5) - 0.7621401 * jax.random.uniform(arg_keys[1], (NX, NY, NZ), jnp.float32) ** levels(arg_keys[1], (NX, NY, NZ), ((0, 4), (1, 4), (2, 2)), -0.2, 0.2)), 0.7, 1.5)
    velocity = jnp.clip(jax.random.uniform(arg_keys[2], (3, NX, NY, NZ), jnp.float32, -0.5, 0.5) * levels(arg_keys[2], (3, NX, NY, NZ), ((1, 4), (2, 4), (3, 2)), -0.4, 0.0), -0.5, 0.5)
    stiffness = jnp.clip(jnp.exp(math.log(1.6) - 0.98082923 * jax.random.uniform(arg_keys[3], (NX, NY, NZ), jnp.float32) ** levels(arg_keys[3], (NX, NY, NZ), ((0, 4), (1, 4), (2, 2)), -0.2, 0.2)), 0.6, 1.6)
    sponge = jnp.clip(jnp.exp(math.log(3.0) - 3.4011974 * jax.random.uniform(arg_keys[4], (NX, NY, NZ), jnp.float32) ** levels(arg_keys[4], (NX, NY, NZ), ((0, 4), (1, 4), (2, 2)), -0.2, 0.2)), 0.1, 3.0)
    source_shape = gaussian(arg_keys[5], (NX, NY, NZ), (BX * BY * BZ) ** -0.5, 0.1875, ((0, 4), (1, 4), (2, 2)), jnp.float32)
    brick_level = set_ends(jax.random.randint(arg_keys[6], (N_GX, N_GY, N_GZ), 0, 2), jax.random.fold_in(arg_keys[6], 1), 0, 1).astype(jnp.int32)
    brick_patch = draw_brick_patch(jax.random.fold_in(arg_keys[9], 71), 0)
    patch_owner = draw_patch_owner(jax.random.fold_in(arg_keys[9], 71), 0)
    return {"terminal_adjoint": terminal_adjoint, "density": density, "velocity": velocity, "stiffness": stiffness, "sponge": sponge, "source_shape": source_shape, "brick_level": brick_level, "brick_patch": brick_patch, "patch_owner": patch_owner}


step_length = 0.14
third = 1.0 / 3.0
two_thirds = 2.0 / 3.0


def transposed_flux(adjoint, density, velocity, stiffness, direction):
    along_speed = velocity[direction]
    components = [along_speed * adjoint[component] for component in range(5)]
    velocity_row = 1 + direction
    components[velocity_row] = components[velocity_row] + density * adjoint[0] + stiffness * adjoint[4]
    components[4] = components[4] + adjoint[velocity_row] / density
    return jnp.stack(components)


def half_inverse_field(brick_level):
    scaled = 0.5 * jnp.exp2(brick_level.astype(jnp.float32))
    spread = jnp.broadcast_to(scaled[:, None, :, None, :, None], (N_GX, CX, N_GY, CY, N_GZ, CZ))
    return spread.reshape(NX, NY, NZ)


def operate(adjoint, density, velocity, stiffness, half_inverse, sponge):
    summed = None
    for direction in range(3):
        partials = half_inverse * transposed_flux(adjoint, density, velocity, stiffness, direction)
        pad_widths = [(0, 0), (0, 0), (0, 0), (0, 0)]
        pad_widths[direction + 1] = (1, 1)
        padded = jnp.pad(partials, pad_widths)
        upper_cut = [slice(None), slice(None), slice(None), slice(None)]
        lower_cut = [slice(None), slice(None), slice(None), slice(None)]
        upper_cut[direction + 1] = slice(2, None)
        lower_cut[direction + 1] = slice(None, -2)
        difference = padded[tuple(upper_cut)] - padded[tuple(lower_cut)]
        summed = difference if summed is None else summed + difference
    return summed - sponge * adjoint


def restrict(adjoint, source_shape):
    weighted = adjoint * source_shape
    boxed = weighted.reshape(5, N_GX, CX // BX, BX, N_GY, CY // BY, BY, N_GZ, CZ // BZ, BZ)
    boxed = jnp.sum(boxed, axis=(3, 6, 9))
    return jnp.transpose(boxed, (1, 3, 5, 0, 2, 4, 6)).reshape(N_GX * N_GY * N_GZ, KBLOCK)


def reference(terminal_adjoint, density, velocity, stiffness, sponge, source_shape, brick_level, brick_patch, patch_owner):
    half_inverse = half_inverse_field(brick_level)
    adjoint = terminal_adjoint

    def apply_op(field_now):
        return operate(field_now, density, velocity, stiffness, half_inverse, sponge)

    blocks = jnp.zeros((PATCHES, KBLOCK), jnp.float32)
    for step_index in range(STEPS):
        section_one = adjoint + step_length * apply_op(adjoint)
        section_two = 0.75 * adjoint + 0.25 * (section_one + step_length * apply_op(section_one))
        adjoint = third * adjoint + two_thirds * (section_two + step_length * apply_op(section_two))
        blocks = blocks + step_length * restrict(adjoint, source_shape)
    patch_sums = jax.ops.segment_sum(blocks, brick_patch.reshape(-1).astype(jnp.int32), num_segments=PATCHES)
    patch_gradient = jnp.zeros_like(patch_sums).at[patch_owner.astype(jnp.int32)].set(patch_sums)
    return adjoint, patch_gradient
```

```python
import jax
import jax.numpy as jnp
from jax import lax
from jax.sharding import PartitionSpec as P

BX = 8
BY = 8
BZ = 16


step_length = 0.14
third = 1.0 / 3.0
two_thirds = 2.0 / 3.0


def with_halo(block, sides, width):
    for axis, dim in sides:
        count = lax.axis_size(axis)
        forward = [(i, i + 1) for i in range(count - 1)]
        backward = [(target, source) for source, target in forward]
        low = lax.ppermute(
            lax.slice_in_dim(block, block.shape[dim] - width, None, axis=dim), axis, forward
        )
        high = lax.ppermute(lax.slice_in_dim(block, 0, width, axis=dim), axis, backward)
        block = jnp.concatenate([low, block, high], axis=dim)
    return block


def transposed_flux(adjoint, density, velocity, stiffness, direction):
    along_speed = velocity[direction]
    components = [along_speed * adjoint[component] for component in range(5)]
    velocity_row = 1 + direction
    components[velocity_row] = (
        components[velocity_row] + density * adjoint[0] + stiffness * adjoint[4]
    )
    components[4] = components[4] + adjoint[velocity_row] / density
    return jnp.stack(components)


def apply_faces(adjoint, density, velocity, stiffness, half_inverse, sponge):
    partials = half_inverse * transposed_flux(adjoint, density, velocity, stiffness, 0)
    padded = with_halo(partials, (("gx", 1),), 1)
    summed = padded[:, 2:] - padded[:, :-2]
    partials = half_inverse * transposed_flux(adjoint, density, velocity, stiffness, 1)
    padded = with_halo(partials, (("gy", 2),), 1)
    summed = summed + (padded[:, :, 2:] - padded[:, :, :-2])
    partials = half_inverse * transposed_flux(adjoint, density, velocity, stiffness, 2)
    padded = with_halo(partials, (("gz", 3),), 1)
    summed = summed + (padded[:, :, :, 2:] - padded[:, :, :, :-2])
    return summed - sponge * adjoint


def body(
    terminal_adjoint,
    density,
    velocity,
    stiffness,
    sponge,
    source_shape,
    brick_level,
    brick_patch,
    patch_owner,
):
    index_x = lax.axis_index("gx")
    index_y = lax.axis_index("gy")
    index_z = lax.axis_index("gz")
    count_y = lax.axis_size("gy")
    count_z = lax.axis_size("gz")
    cells_x, cells_y, cells_z = density.shape
    own_brick = (index_x * count_y + index_y) * count_z + index_z
    own_patch = brick_patch[index_x, index_y, index_z]
    target = patch_owner[own_patch]
    devices = patch_owner.shape[0]
    own_level = brick_level[index_x, index_y, index_z]
    half_inverse = 0.5 * jnp.exp2(own_level.astype(jnp.float32))

    def apply_op(field_now):
        return apply_faces(field_now, density, velocity, stiffness, half_inverse, sponge)

    adjoint = terminal_adjoint
    section_one = adjoint + step_length * apply_op(adjoint)
    section_two = 0.75 * adjoint + 0.25 * (section_one + step_length * apply_op(section_one))
    adjoint = third * adjoint + two_thirds * (section_two + step_length * apply_op(section_two))
    weighted = adjoint * source_shape
    boxed = weighted.reshape(5, cells_x // BX, BX, cells_y // BY, BY, cells_z // BZ, BZ)
    block_now = step_length * jnp.sum(boxed, axis=(2, 4, 6)).reshape(1, -1)
    rows = jnp.arange(devices, dtype=jnp.int32)[:, None]
    outgoing = jnp.where(rows == target, block_now, 0.0)
    incoming = lax.all_to_all(outgoing, ("gx", "gy", "gz"), 0, 0, tiled=True)
    gradient = jnp.sum(incoming, axis=0, keepdims=True)
    return (adjoint, gradient)


def solution(mesh):
    in_specs = (
        P(None, "gx", "gy", "gz"),
        P("gx", "gy", "gz"),
        P(None, "gx", "gy", "gz"),
        P("gx", "gy", "gz"),
        P("gx", "gy", "gz"),
        P("gx", "gy", "gz"),
        P(),
        P(),
        P(),
    )
    out_specs = (P(None, "gx", "gy", "gz"), P(("gx", "gy", "gz"), None))
    return jax.shard_map(body, mesh=mesh, in_specs=in_specs, out_specs=out_specs, check_vma=False)
```

```python
import jax
import jax.numpy as jnp
from jax import lax
from jax.sharding import PartitionSpec as P

BX = 8
BY = 8
BZ = 16

AXES = ("gx", "gy", "gz")

step_length = 0.14
third = 1.0 / 3.0
two_thirds = 2.0 / 3.0


def pairings(sizes, axis, near_axis):
    size = sizes[axis]
    first, second = [], []
    for x in range(sizes[0]):
        for y in range(sizes[1]):
            for z in range(sizes[2]):
                here = [x, y, z]
                index = (x * sizes[1] + y) * sizes[2] + z
                place = here[axis]
                other = list(here)
                other[axis] = place ^ 1
                first.append((index, (other[0] * sizes[1] + other[1]) * sizes[2] + other[2]))
                other = list(here)
                if 0 < place < size - 1:
                    other[axis] = place + 1 if place % 2 else place - 1
                else:
                    other[near_axis] = here[near_axis] ^ 1
                second.append((index, (other[0] * sizes[1] + other[1]) * sizes[2] + other[2]))
    return first, second if size > 2 else None


def send_faces(low_face, high_face, position, permutations):
    even = position % 2 == 0
    first = lax.ppermute(jnp.where(even, high_face, low_face), AXES, permutations[0])
    second = None
    if permutations[1] is not None:
        second = lax.ppermute(jnp.where(even, low_face, high_face), AXES, permutations[1])
    return first, second


def sort_faces(received, position, size):
    first, second = received
    even = position % 2 == 0
    zero = jnp.zeros_like(first)
    if second is None:
        return jnp.where(even, zero, first), jnp.where(even, first, zero)
    below = jnp.where(position == 0, zero, jnp.where(even, second, first))
    above = jnp.where(position == size - 1, zero, jnp.where(even, first, second))
    return below, above


def transposed_flux(adjoint, density, velocity, stiffness, direction):
    along_speed = velocity[direction]
    components = [along_speed * adjoint[component] for component in range(5)]
    velocity_row = 1 + direction
    components[velocity_row] = (
        components[velocity_row] + density * adjoint[0] + stiffness * adjoint[4]
    )
    components[4] = components[4] + adjoint[velocity_row] / density
    return jnp.stack(components)


def body(
    terminal_adjoint,
    density,
    velocity,
    stiffness,
    sponge,
    source_shape,
    brick_level,
    brick_patch,
    patch_owner,
):
    sizes = tuple(lax.axis_size(axis) for axis in AXES)
    position = tuple(lax.axis_index(axis) for axis in AXES)
    cells_x, cells_y, cells_z = density.shape
    here = jnp.ones(sizes, bool)
    for axis in range(3):
        here = here & (lax.broadcasted_iota(jnp.int32, sizes, axis) == position[axis])
    own_level = jnp.sum(jnp.where(here, brick_level, 0))
    own_patch = jnp.sum(jnp.where(here, brick_patch, 0))
    devices = patch_owner.shape[0]
    target = jnp.sum(jnp.where(jnp.arange(devices) == own_patch, patch_owner, 0))
    half_inverse = 0.5 * jnp.exp2(own_level.astype(jnp.float32))
    permutations = (
        pairings(sizes, 0, 1),
        pairings(sizes, 1, 2),
        pairings(sizes, 2, 1),
    )

    def apply_op(adjoint):
        partials = [
            half_inverse * transposed_flux(adjoint, density, velocity, stiffness, direction)
            for direction in range(3)
        ]
        received = []
        for direction in range(3):
            block, dim = partials[direction], direction + 1
            low_face = lax.slice_in_dim(block, 0, 1, axis=dim)
            high_face = lax.slice_in_dim(block, block.shape[dim] - 1, None, axis=dim)
            received.append(
                send_faces(low_face, high_face, position[direction], permutations[direction])
            )
        summed = None
        for direction in range(3):
            dim = direction + 1
            below, above = sort_faces(received[direction], position[direction], sizes[direction])
            padded = jnp.concatenate([below, partials[direction], above], axis=dim)
            count = padded.shape[dim]
            difference = lax.slice_in_dim(padded, 2, None, axis=dim) - lax.slice_in_dim(
                padded, 0, count - 2, axis=dim
            )
            summed = difference if summed is None else summed + difference
        return summed - sponge * adjoint

    adjoint = terminal_adjoint
    section_one = adjoint + step_length * apply_op(adjoint)
    section_two = 0.75 * adjoint + 0.25 * (section_one + step_length * apply_op(section_one))
    adjoint = third * adjoint + two_thirds * (section_two + step_length * apply_op(section_two))
    weighted = adjoint * source_shape
    boxed = weighted.reshape(5, cells_x // BX, BX, cells_y // BY, BY, cells_z // BZ, BZ)
    block_now = step_length * jnp.sum(boxed, axis=(2, 4, 6)).reshape(1, -1)
    rows = jnp.arange(devices, dtype=jnp.int32)[:, None]
    outgoing = jnp.where(rows == target, block_now, 0.0)
    incoming = lax.all_to_all(outgoing, AXES, 0, 0, tiled=True)
    gradient = jnp.sum(incoming, axis=0, keepdims=True)
    return (adjoint, gradient)


def solution(mesh):
    in_specs = (
        P(None, "gx", "gy", "gz"),
        P("gx", "gy", "gz"),
        P(None, "gx", "gy", "gz"),
        P("gx", "gy", "gz"),
        P("gx", "gy", "gz"),
        P("gx", "gy", "gz"),
        P(),
        P(),
        P(),
    )
    out_specs = (P(None, "gx", "gy", "gz"), P(("gx", "gy", "gz"), None))
    return jax.shard_map(body, mesh=mesh, in_specs=in_specs, out_specs=out_specs, check_vma=False)
```

```python
import functools

import jax
import jax.numpy as jnp
from jax import lax
from jax.experimental import pallas as pl
from jax.experimental.pallas import tpu as pltpu
from jax.sharding import PartitionSpec as P

CX = 8
CY = 8
CZ = 128
BZ = 16
BOXES = CZ // BZ

AXES = ("gx", "gy", "gz")

step_length = 0.14
third = 1.0 / 3.0
two_thirds = 2.0 / 3.0

FULL = (CX, CY, CZ)
TILE = (CY, CZ)


def pairings(sizes, axis, near_axis):
    size = sizes[axis]
    first, second = [], []
    for x in range(sizes[0]):
        for y in range(sizes[1]):
            for z in range(sizes[2]):
                here = [x, y, z]
                index = (x * sizes[1] + y) * sizes[2] + z
                place = here[axis]
                other = list(here)
                other[axis] = place ^ 1
                first.append((index, (other[0] * sizes[1] + other[1]) * sizes[2] + other[2]))
                other = list(here)
                if 0 < place < size - 1:
                    other[axis] = place + 1 if place % 2 else place - 1
                else:
                    other[near_axis] = here[near_axis] ^ 1
                second.append((index, (other[0] * sizes[1] + other[1]) * sizes[2] + other[2]))
    return first, second if size > 2 else None


def positions():
    return [lax.axis_index(axis) for axis in AXES]


def own_half_inverse(level_ref):
    here = positions()
    level = level_ref[here[0], here[1], here[2]]
    return 0.5 * lax.shift_left(jnp.int32(1), level).astype(jnp.float32)


def load(ref):
    return [ref[component] for component in range(5)]


def transposed_partials(adjoint, density, velocity_ref, stiffness, half_inverse, direction):
    along_speed = half_inverse * velocity_ref[direction]
    components = [along_speed * component for component in adjoint]
    row = 1 + direction
    components[row] = components[row] + half_inverse * (
        density * adjoint[0] + stiffness * adjoint[4]
    )
    components[4] = components[4] + (half_inverse * adjoint[row]) / density
    return components


def all_partials(adjoint, density_ref, velocity_ref, stiffness_ref, half_inverse):
    density, stiffness = density_ref[...], stiffness_ref[...]
    return [
        transposed_partials(adjoint, density, velocity_ref, stiffness, half_inverse, direction)
        for direction in range(3)
    ]


def rows_of(block, row):
    return jnp.concatenate([block[x, row : row + 1, :] for x in range(CX)], axis=0)


def pack_x(fields, position, out_first, out_second):
    even = position % 2 == 0
    for index, field in enumerate(fields):
        low, high = field[0], field[CX - 1]
        out_first[index] = jnp.where(even, high, low)
        if out_second is not None:
            out_second[index] = jnp.where(even, low, high)


def pack_y(fields, position, out_first, out_second):
    even = position % 2 == 0
    faces = []
    for index, field in enumerate(fields):
        low, high = rows_of(field, 0), rows_of(field, CY - 1)
        out_first[index] = jnp.where(even, high, low)
        if out_second is not None:
            out_second[index] = jnp.where(even, low, high)
        faces.append((low, high))
    return faces


def pack_z(fields):
    lanes = lax.broadcasted_iota(jnp.int32, TILE, 1) // 2
    packed = jnp.zeros(TILE, jnp.float32)
    for index, field in enumerate(fields):
        for x in range(CX):
            k = index * CX + x
            packed = jnp.where(lanes == k, pltpu.roll(field[x], (2 * k + 1) % CZ, 1), packed)
    return packed


def sort_pair(first, second, position, size):
    even = position % 2 == 0
    zero = jnp.zeros_like(first)
    if second is None:
        return jnp.where(even, zero, first), jnp.where(even, first, zero)
    below = jnp.where(position == 0, zero, jnp.where(even, second, first))
    above = jnp.where(position == size - 1, zero, jnp.where(even, first, second))
    return below, above


def pair_of(refs, index):
    first, second = refs
    return first[index], None if second is None else second[index]


def lane_halo(z_refs, position, size):
    below, above = sort_pair(
        z_refs[0][...], None if z_refs[1] is None else z_refs[1][...], position, size
    )
    lanes = lax.broadcasted_iota(jnp.int32, TILE, 1)
    return jnp.where(lanes % 2 == 0, pltpu.roll(above, CZ - 1, 1), pltpu.roll(below, 1, 1))


def halo_of(x_refs, y_refs, z_halo, component, sizes):
    here = positions()
    x_below, x_above = sort_pair(*pair_of(x_refs, component), here[0], sizes[0])
    y_below, y_above = sort_pair(*pair_of(y_refs, component), here[1], sizes[1])
    spread = lambda rows: jnp.stack(
        [jnp.broadcast_to(rows[x : x + 1], TILE) for x in range(CX)]
    )
    z_both = jnp.stack(
        [pltpu.roll(z_halo, (CZ - 1 - 2 * (component * CX + x)) % CZ, 1) for x in range(CX)]
    )
    return x_below, x_above, spread(y_below), spread(y_above), z_both


def differences(partials, component, halo):
    part_x, part_y, part_z = (partials[direction][component] for direction in range(3))
    rows = lax.broadcasted_iota(jnp.int32, FULL, 1)
    lanes = lax.broadcasted_iota(jnp.int32, FULL, 2)
    if halo is None:
        zero = jnp.zeros(TILE, jnp.float32)
        x_below, x_above, y_below, y_above, z_both = zero, zero, 0.0, 0.0, 0.0
    else:
        x_below, x_above, y_below, y_above, z_both = halo
    after = jnp.concatenate([part_x[1:], x_above[None]], axis=0)
    before = jnp.concatenate([x_below[None], part_x[:-1]], axis=0)
    total = after - before
    after = jnp.where(rows == CY - 1, y_above, pltpu.roll(part_y, CY - 1, 1))
    before = jnp.where(rows == 0, y_below, pltpu.roll(part_y, 1, 1))
    total = total + (after - before)
    after = jnp.where(lanes == CZ - 1, z_both, pltpu.roll(part_z, CZ - 1, 2))
    before = jnp.where(lanes == 0, z_both, pltpu.roll(part_z, 1, 2))
    return total + (after - before)


def split(refs, sizes, count):
    refs, out = list(refs), []
    for axis in range(3):
        first = refs.pop(0)
        out.append((first, refs.pop(0) if sizes[axis] > 2 else None))
    assert len(refs) == count
    return out, refs


def send_all(partials, extra, out_x, out_y, out_z):
    here = positions()
    pack_x(partials[0] + extra, here[0], *out_x)
    faces = pack_y(partials[1] + extra, here[1], *out_y)
    packed = pack_z(partials[2] + extra)
    for ref in out_z[:1]:
        ref[...] = packed
    return faces, packed


def first_kernel(sizes, level, adjoint, density, velocity, stiffness, source, *outs):
    half_inverse = own_half_inverse(level)
    partials = all_partials(load(adjoint), density, velocity, stiffness, half_inverse)
    out_x, out_y, out_z = message_outs(outs, sizes)[0]
    send_all(partials, [source[...]], out_x, out_y, out_z)


def message_outs(refs, sizes):
    refs, out = list(refs), []
    for axis in range(2):
        first = refs.pop(0)
        out.append((first, refs.pop(0) if sizes[axis] > 2 else None))
    out.append((refs.pop(0),))
    return out, refs


def second_kernel(sizes, level, adjoint, density, velocity, stiffness, sponge, *refs):
    received, outs = split(refs, sizes, len(refs) - sum(2 if s > 2 else 1 for s in sizes))
    half_inverse = own_half_inverse(level)
    here = positions()
    old = load(adjoint)
    partials = all_partials(old, density, velocity, stiffness, half_inverse)
    z_halo = lane_halo(received[2], here[2], sizes[2])
    section, outs = outs[0], outs[1:]
    new = []
    for component in range(5):
        halo = halo_of(received[0], received[1], z_halo, component, sizes)
        change = differences(partials, component, halo) - sponge[...] * old[component]
        value = old[component] + step_length * change
        section[component] = value
        new.append(value)
    partials = all_partials(new, density, velocity, stiffness, half_inverse)
    send_all(partials, [], *message_outs(outs, sizes)[0])


def sublane_total(tile):
    for shift in (4, 2, 1):
        tile = tile + pltpu.roll(tile, shift, 0)
    return tile


def box_row(tiles):
    sublanes = lax.broadcasted_iota(jnp.int32, TILE, 0)
    lanes = lax.broadcasted_iota(jnp.int32, TILE, 1)
    rows = jnp.zeros(TILE, jnp.float32)
    for component, tile in enumerate(tiles):
        rows = jnp.where(sublanes == component, sublane_total(tile), rows)
    for shift in (1, 2, 4, 8):
        rows = rows + pltpu.roll(rows, CZ - shift, 1)
    placed = jnp.zeros(TILE, jnp.float32)
    for component in range(5):
        placed = jnp.where(
            (sublanes == component) & (lanes % BZ == component),
            pltpu.roll(rows, component, 1),
            placed,
        )
    return sublane_total(placed)


def lane_row(product, box):
    lanes = lax.broadcasted_iota(jnp.int32, TILE, 1)
    rows = sublane_total(product)
    for shift in (1, 2, 4, 8):
        rows = rows + pltpu.roll(rows, CZ - shift, 1)
    placed = jnp.zeros(TILE, jnp.float32)
    for component in range(5):
        want = box * BZ + component
        placed = jnp.where(
            lanes == want, pltpu.roll(rows, (want - 2 * CX * component) % CZ, 1), placed
        )
    return placed


def third_kernel(
    sizes, level, patches, owners, adjoint, density, velocity, stiffness, sponge, source, section, *refs
):
    received, rest = split(refs, sizes, len(refs) - sum(2 if s > 2 else 1 for s in sizes))
    (sources_x, sources_y, sources_z), outs = split(
        rest, sizes, len(rest) - sum(2 if s > 2 else 1 for s in sizes)
    )
    half_inverse = own_half_inverse(level)
    here = positions()
    base, old = load(adjoint), load(section)
    partials = all_partials(old, density, velocity, stiffness, half_inverse)
    z_halo = lane_halo(received[2], here[2], sizes[2])
    partial_out, table_out, outs = outs[0], outs[1], outs[2:]
    new = []
    for component in range(5):
        halo = halo_of(received[0], received[1], z_halo, component, sizes)
        change = differences(partials, component, halo) - sponge[...] * old[component]
        new.append(0.75 * base[component] + 0.25 * (old[component] + step_length * change))
    partials = all_partials(new, density, velocity, stiffness, half_inverse)
    faces_y, packed_z = send_all(partials, [], *message_outs(outs, sizes)[0])
    shape = source[...]
    own = []
    for component in range(5):
        change = differences(partials, component, None) - sponge[...] * new[component]
        value = third * base[component] + two_thirds * (new[component] + step_length * change)
        partial_out[component] = value
        own.append(jnp.sum(value * shape, axis=0))
    weight = two_thirds * step_length
    x_below, x_above = sort_pair(*pair_of(sources_x, 5), here[0], sizes[0])
    y_below, y_above = sort_pair(*pair_of(sources_y, 5), here[1], sizes[1])
    first, second = sources_z
    z_below, z_above = sort_pair(
        first[...], None if second is None else second[...], here[2], sizes[2]
    )
    lanes = lax.broadcasted_iota(jnp.int32, TILE, 1)
    aligned_above = jnp.zeros(TILE, jnp.float32)
    aligned_below = jnp.zeros(TILE, jnp.float32)
    for component in range(5):
        group = lanes // (2 * CX) == component
        shift = 2 * CX * (component - 5)
        aligned_above = jnp.where(
            group & (lanes % 2 == 0), pltpu.roll(z_above, (shift - 1) % CZ, 1), aligned_above
        )
        aligned_below = jnp.where(
            group & (lanes % 2 == 1), pltpu.roll(z_below, (shift + 1) % CZ, 1), aligned_below
        )
    contributions = [
        ((0, 0, 0), box_row(own)),
        ((1, 0, 0), -weight * box_row([x_above * partials[0][f][CX - 1] for f in range(5)])),
        ((-1, 0, 0), weight * box_row([x_below * partials[0][f][0] for f in range(5)])),
        ((0, 1, 0), -weight * box_row([y_above * faces_y[f][1] for f in range(5)])),
        ((0, -1, 0), weight * box_row([y_below * faces_y[f][0] for f in range(5)])),
        ((0, 0, 1), -weight * lane_row(aligned_above * packed_z, 0)),
        ((0, 0, -1), weight * lane_row(aligned_below * packed_z, BOXES - 1)),
    ]
    targets = []
    for offset, row in contributions:
        place = [
            jnp.clip(here[axis] + offset[axis], 0, sizes[axis] - 1) for axis in range(3)
        ]
        targets.append(owners[patches[place[0], place[1], place[2]]])
    sublanes = lax.broadcasted_iota(jnp.int32, TILE, 0)
    rows_total = table_out.shape[0]
    for start in range(0, rows_total, CY):
        table = jnp.zeros(TILE, jnp.float32)
        for (offset, row), target in zip(contributions, targets):
            table = table + jnp.where(sublanes + start == target, step_length * row, 0.0)
        table_out[start : start + CY, :] = table


def last_kernel(sizes, partial, table, *refs):
    received, (out, gradient) = split(refs, sizes, 2)
    here = positions()
    weight = two_thirds * step_length
    z_halo = lane_halo(received[2], here[2], sizes[2])
    rows = lax.broadcasted_iota(jnp.int32, FULL, 1)
    lanes = lax.broadcasted_iota(jnp.int32, FULL, 2)
    for component in range(5):
        x_below, x_above, y_below, y_above, z_both = halo_of(
            received[0], received[1], z_halo, component, sizes
        )
        change = jnp.where(rows == CY - 1, y_above, 0.0) - jnp.where(rows == 0, y_below, 0.0)
        change = change + jnp.where(lanes == CZ - 1, z_both, 0.0)
        change = change - jnp.where(lanes == 0, z_both, 0.0)
        value = partial[component] + weight * change
        out[component] = value
        out[component, CX - 1] = value[CX - 1] + weight * x_above
        out[component, 0] = value[0] - weight * x_below
    total = jnp.zeros(TILE, jnp.float32)
    for start in range(0, table.shape[0], CY):
        total = total + table[start : start + CY, :]
    total = sublane_total(total)
    tile_lanes = lax.broadcasted_iota(jnp.int32, TILE, 1)
    result = jnp.zeros(TILE, jnp.float32)
    for component in range(5):
        for box in range(BOXES):
            want = component * BOXES + box
            have = box * BZ + component
            result = jnp.where(tile_lanes == want, pltpu.roll(total, (want - have) % CZ, 1), result)
    gradient[...] = result[0:1, : 5 * BOXES]


def call(kernel, sizes, tables, arrays, out_shapes):
    vmem = pl.BlockSpec(memory_space=pltpu.VMEM)
    smem = pl.BlockSpec(memory_space=pltpu.SMEM)
    return pl.pallas_call(
        functools.partial(kernel, sizes),
        out_shape=[jax.ShapeDtypeStruct(shape, jnp.float32) for shape in out_shapes],
        in_specs=[smem] * len(tables) + [vmem] * len(arrays),
        out_specs=[vmem] * len(out_shapes),
        compiler_params=pltpu.CompilerParams(vmem_limit_bytes=32 * 1024 * 1024),
    )(*tables, *arrays)


def body(
    terminal_adjoint,
    density,
    velocity,
    stiffness,
    sponge,
    source_shape,
    brick_level,
    brick_patch,
    patch_owner,
):
    sizes = tuple(lax.axis_size(axis) for axis in AXES)
    permutations = (
        pairings(sizes, 0, 1),
        pairings(sizes, 1, 2),
        pairings(sizes, 2, 1),
    )
    devices = patch_owner.shape[0]
    state = (5,) + FULL

    def message_shapes(fields):
        shapes = []
        for axis in range(2):
            shapes += [(fields,) + TILE] * (2 if sizes[axis] > 2 else 1)
        return shapes + [TILE]

    def exchange(messages):
        messages = list(messages)
        sends = []
        for axis in range(2):
            for permutation in permutations[axis]:
                if permutation is not None:
                    sends.append((messages.pop(0), permutation))
        packed = messages.pop(0)
        for permutation in permutations[2]:
            if permutation is not None:
                sends.append((packed, permutation))
        return [lax.ppermute(message, AXES, permutation) for message, permutation in sends]

    mean = (density, velocity, stiffness)
    sent = call(
        first_kernel,
        sizes,
        (brick_level,),
        (terminal_adjoint, *mean, source_shape),
        message_shapes(6),
    )
    received_one = exchange(sent)
    section, *sent = call(
        second_kernel,
        sizes,
        (brick_level,),
        (terminal_adjoint, *mean, sponge, *received_one),
        [state] + message_shapes(5),
    )
    received = exchange(sent)
    partial, table, *sent = call(
        third_kernel,
        sizes,
        (brick_level, brick_patch, patch_owner),
        (terminal_adjoint, *mean, sponge, source_shape, section, *received, *received_one),
        [state, (devices, CZ)] + message_shapes(5),
    )
    received = exchange(sent)
    table = lax.all_to_all(table.reshape(devices, 1, CZ), AXES, 0, 0, tiled=True)
    adjoint, gradient = call(
        last_kernel,
        sizes,
        (),
        (partial, table.reshape(devices, CZ), *received),
        [state, (1, 5 * BOXES)],
    )
    return adjoint, gradient


def solution(mesh):
    in_specs = (
        P(None, "gx", "gy", "gz"),
        P("gx", "gy", "gz"),
        P(None, "gx", "gy", "gz"),
        P("gx", "gy", "gz"),
        P("gx", "gy", "gz"),
        P("gx", "gy", "gz"),
        P(),
        P(),
        P(),
    )
    out_specs = (P(None, "gx", "gy", "gz"), P(("gx", "gy", "gz"), None))
    return jax.shard_map(body, mesh=mesh, in_specs=in_specs, out_specs=out_specs, check_vma=False)
```

```python
import functools

import jax
import jax.numpy as jnp
from jax import lax
from jax.experimental import pallas as pl
from jax.experimental.pallas import tpu as pltpu
from jax.sharding import PartitionSpec as P

CX = 8
CY = 8
CZ = 128
BZ = 16
BOXES = CZ // BZ
ROWS = CX * CY

AXES = ("gx", "gy", "gz")

step_length = 0.14
third = 1.0 / 3.0
two_thirds = 2.0 / 3.0

TILE = (CY, CZ)
FLAT = (ROWS, CZ)
STATE = (5,) + FLAT


def pairings(sizes, axis, near_axis):
    size = sizes[axis]
    first, second = [], []
    for x in range(sizes[0]):
        for y in range(sizes[1]):
            for z in range(sizes[2]):
                here = [x, y, z]
                index = (x * sizes[1] + y) * sizes[2] + z
                place = here[axis]
                other = list(here)
                other[axis] = place ^ 1
                first.append((index, (other[0] * sizes[1] + other[1]) * sizes[2] + other[2]))
                other = list(here)
                if 0 < place < size - 1 or near_axis == axis:
                    other[axis] = (place + (1 if place % 2 else -1)) % size
                else:
                    other[near_axis] = here[near_axis] ^ 1
                second.append((index, (other[0] * sizes[1] + other[1]) * sizes[2] + other[2]))
    return first, second if size > 2 else None


def positions():
    return [lax.axis_index(axis) for axis in AXES]


def tile_at(x):
    return slice(x * CY, (x + 1) * CY)


def row_at(y):
    return pl.ds(y, CX, stride=CY)


def partials_of(adjoint, speed, density, stiffness, inverse, direction):
    components = [speed * component for component in adjoint]
    row = 1 + direction
    components[row] = components[row] + (density * adjoint[0] + stiffness * adjoint[4])
    components[4] = components[4] + adjoint[row] * inverse
    return components


def faces_at(state, scaled, rows, direction):
    adjoint = [state[component, rows, :] for component in range(5)]
    return partials_of(
        adjoint,
        scaled[direction, rows, :],
        scaled[3, rows, :],
        scaled[4, rows, :],
        scaled[5, rows, :],
        direction,
    )


def pack_lanes(fields):
    lanes = lax.broadcasted_iota(jnp.int32, TILE, 1) // 2
    packed = jnp.zeros(TILE, jnp.float32)
    for index, field in enumerate(fields):
        for x in range(CX):
            k = index * CX + x
            packed = jnp.where(lanes == k, pltpu.roll(field[x], (2 * k + 1) % CZ, 1), packed)
    return packed


def put_pair(low, high, position, outs):
    even = position % 2 == 0
    for index, (below, above) in enumerate(zip(low, high)):
        outs[0][index] = jnp.where(even, above, below)
        if outs[1] is not None:
            outs[1][index] = jnp.where(even, below, above)


def put_messages(state, scaled, source, outs):
    here = positions()
    x_low = faces_at(state, scaled, tile_at(0), 0)
    x_high = faces_at(state, scaled, tile_at(CX - 1), 0)
    y_low = faces_at(state, scaled, row_at(0), 1)
    y_high = faces_at(state, scaled, row_at(CY - 1), 1)
    z_tiles = [faces_at(state, scaled, tile_at(x), 2) for x in range(CX)]
    z_fields = [[z_tiles[x][component] for x in range(CX)] for component in range(5)]
    if source is None:
        extra = [[]] * 4
    else:
        rows = (tile_at(0), tile_at(CX - 1), row_at(0), row_at(CY - 1))
        extra = [[source[row, :]] for row in rows]
        z_fields.append([source[tile_at(x), :] for x in range(CX)])
    put_pair(x_low + extra[0], x_high + extra[1], here[0], outs[0])
    put_pair(y_low + extra[2], y_high + extra[3], here[1], outs[1])
    packed = pack_lanes(z_fields)
    outs[2][0][...] = packed
    return x_low, x_high, y_low, y_high, packed


def sort_pair(first, second, position, size):
    even = position % 2 == 0
    zero = jnp.zeros_like(first)
    if second is None:
        return jnp.where(even, zero, first), jnp.where(even, first, zero)
    below = jnp.where(position == 0, zero, jnp.where(even, second, first))
    above = jnp.where(position == size - 1, zero, jnp.where(even, first, second))
    return below, above


def sorted_field(refs, index, position, size):
    first, second = refs
    return sort_pair(first[index], None if second is None else second[index], position, size)


def sorted_lanes(refs, position, size):
    first, second = refs
    return sort_pair(first[...], None if second is None else second[...], position, size)


def add_halo(base, received, weight, sizes, out):
    here = positions()
    lanes = lax.broadcasted_iota(jnp.int32, TILE, 1)
    edges = (lanes == 0) | (lanes == CZ - 1)
    z_below, z_above = sorted_lanes(received[2], here[2], sizes[2])
    z_halo = weight * jnp.where(
        lanes % 2 == 0, pltpu.roll(z_above, CZ - 1, 1), -pltpu.roll(z_below, 1, 1)
    )
    for component in range(5):
        x_below, x_above = sorted_field(received[0], component, here[0], sizes[0])
        y_below, y_above = sorted_field(received[1], component, here[1], sizes[1])
        for x in range(CX):
            k = component * CX + x
            value = base[component, tile_at(x), :]
            value = value + jnp.where(edges, pltpu.roll(z_halo, (CZ - 1 - 2 * k) % CZ, 1), 0.0)
            if x == 0:
                value = value - weight * x_below
            if x == CX - 1:
                value = value + weight * x_above
            out[component, tile_at(x), :] = value
        out[component, row_at(0), :] = out[component, row_at(0), :] - weight * y_below
        out[component, row_at(CY - 1), :] = out[component, row_at(CY - 1), :] + weight * y_above


ORDER = ((1, 0), (2, 0), (0, 1), (0, 0), (1, 1), (2, 1))


def message_keys(sizes, sent):
    keys = [key for key in ORDER if key[1] == 0 or sizes[key[0]] > 2]
    return [key for key in keys if not (sent and key == (2, 1))]


def split(refs, sizes, sent=False):
    refs, out = list(refs), [[None, None] for axis in range(3)]
    for axis, which in message_keys(sizes, sent):
        out[axis][which] = refs.pop(0)
    return out, refs


def first_kernel(sizes, level, adjoint, density, velocity, stiffness, source, scaled, *refs):
    outs, scratch = split(refs, sizes, True)
    adjoint_now, density_now, velocity_now, stiffness_now, source_now, arrived = scratch
    pairs = (
        (density, density_now),
        (velocity, velocity_now),
        (stiffness, stiffness_now),
        (adjoint, adjoint_now),
        (source, source_now),
    )
    copies = [
        pltpu.make_async_copy(there, here, arrived.at[index])
        for index, (there, here) in enumerate(pairs)
    ]
    for copy in copies:
        copy.start()
    here = positions()
    own_level = level[here[0], here[2], here[1]]
    half_inverse = 0.5 * lax.shift_left(jnp.int32(1), own_level).astype(jnp.float32)
    for copy in copies:
        copy.wait()
    for direction in range(3):
        scaled[direction] = half_inverse * velocity_now[direction]
    scaled[3] = half_inverse * density_now[...]
    scaled[4] = half_inverse * stiffness_now[...]
    scaled[5] = half_inverse / density_now[...]
    put_messages(adjoint_now, scaled, source_now, outs)


def own_kernel(weights, scaled, sponge, *refs):
    keep, blend = weights
    start, state, out = refs if keep else (None,) + refs
    rows = lax.broadcasted_iota(jnp.int32, TILE, 0)
    lanes = lax.broadcasted_iota(jnp.int32, TILE, 1)
    tiles = [
        [faces_at(state, scaled, tile_at(x), direction) for direction in range(3)]
        for x in range(CX)
    ]
    for x in range(CX):
        damp = sponge[tile_at(x), :]
        for component in range(5):
            total = None
            if x < CX - 1:
                total = tiles[x + 1][0][component]
            if x > 0:
                before = tiles[x - 1][0][component]
                total = -before if total is None else total - before
            part = tiles[x][1][component]
            total = total + jnp.where(rows == CY - 1, 0.0, pltpu.roll(part, CY - 1, 0))
            total = total - jnp.where(rows == 0, 0.0, pltpu.roll(part, 1, 0))
            part = tiles[x][2][component]
            total = total + jnp.where(lanes == CZ - 1, 0.0, pltpu.roll(part, CZ - 1, 1))
            total = total - jnp.where(lanes == 0, 0.0, pltpu.roll(part, 1, 1))
            value = state[component, tile_at(x), :]
            value = blend * (value + step_length * (total - damp * value))
            if keep:
                value = value + keep * start[component, tile_at(x), :]
            out[component, tile_at(x), :] = value


def shape_kernel(source, scaled, sponge, start, shapes, sums):
    rows = lax.broadcasted_iota(jnp.int32, TILE, 0)
    lanes = lax.broadcasted_iota(jnp.int32, TILE, 1)
    outer = step_length * two_thirds
    inner = outer * step_length
    totals = [None] * 5
    for x in range(CX):
        at = tile_at(x)
        shape = source[at, :]
        along_x = jnp.zeros(TILE, jnp.float32)
        if x > 0:
            along_x = along_x + source[tile_at(x - 1), :]
        if x < CX - 1:
            along_x = along_x - source[tile_at(x + 1), :]
        along_y = jnp.where(rows == 0, 0.0, pltpu.roll(shape, 1, 0)) - jnp.where(
            rows == CY - 1, 0.0, pltpu.roll(shape, CY - 1, 0)
        )
        before = inner * jnp.where(lanes == 0, 0.0, pltpu.roll(shape, 1, 1))
        after = inner * jnp.where(lanes == CZ - 1, 0.0, pltpu.roll(shape, CZ - 1, 1))
        along_x, along_y = inner * along_x, inner * along_y
        own = outer * shape * (1.0 - step_length * sponge[at, :])
        own = own + scaled[0, at, :] * along_x + scaled[1, at, :] * along_y
        for index, value in enumerate(
            (own, scaled[2, at, :] * before, scaled[2, at, :] * after, along_x, along_y, before, after)
        ):
            shapes[index, at, :] = value
        weighted = (step_length * third) * shape
        for component in range(5):
            value = weighted * start[component, at, :]
            totals[component] = value if totals[component] is None else totals[component] + value
    for component in range(5):
        sums[component] = totals[component]


def stage_kernel(sizes, weight, base, scaled, *refs):
    received, (section, *outs) = split(refs, sizes)
    add_halo(base, received, weight, sizes, section)
    put_messages(section, scaled, None, split(outs, sizes, True)[0])


def merge_rows(tiles):
    sublanes = lax.broadcasted_iota(jnp.int32, TILE, 0)
    zero = jnp.zeros(TILE, jnp.float32)
    tiles = list(tiles) + [None] * (CY - len(tiles))
    for width in (4, 2, 1):
        upper = (sublanes & width) != 0
        merged = []
        for index in range(width):
            low, high = tiles[index], tiles[index + width]
            low = zero if low is None else low + pltpu.roll(low, CY - width, 0)
            high = zero if high is None else high + pltpu.roll(high, width, 0)
            merged.append(jnp.where(upper, high, low))
        tiles = merged
    return tiles[0]


def target_kernel(sizes, patches, owners, out):
    here = positions()
    sublanes = lax.broadcasted_iota(jnp.int32, TILE, 0)
    result = jnp.zeros(TILE, jnp.int32)
    for index, offset in enumerate(OFFSETS):
        place = [
            jnp.clip(here[axis] + offset[axis], 0, sizes[axis] - 1) for axis in range(3)
        ]
        target = owners[patches[place[0], place[2], place[1]]]
        result = jnp.where(sublanes == index, target, result)
    out[...] = result


OFFSETS = (
    (0, 0, 0),
    (1, 0, 0),
    (-1, 0, 0),
    (0, 1, 0),
    (0, -1, 0),
    (0, 0, 1),
    (0, 0, -1),
)


def gradient_kernel(sizes, weight, base, scaled, shapes, sums, targets, *refs):
    received, rest = split(refs, sizes)
    sources, (section, table, *outs) = split(rest, sizes)
    here = positions()
    add_halo(base, received, weight, sizes, section)
    x_low, x_high, y_low, y_high, packed = put_messages(
        section, scaled, None, split(outs, sizes, True)[0]
    )
    main = [sums[component] for component in range(5)]
    before = [None] * 5
    after = [None] * 5

    def accumulate(totals, component, value):
        old = totals[component]
        totals[component] = value if old is None else old + value

    for x in range(CX):
        at = tile_at(x)
        state = [section[component, at, :] for component in range(5)]
        own, lane_before, lane_after, along_x, along_y, shape_before, shape_after = (
            shapes[index, at, :] for index in range(7)
        )
        push = scaled[3, at, :] * state[0] + scaled[4, at, :] * state[4]
        drawn = [scaled[5, at, :] * state[1 + direction] for direction in range(3)]
        for component in range(5):
            accumulate(main, component, own * state[component])
            accumulate(before, component, lane_before * state[component])
            accumulate(after, component, lane_after * state[component])
        accumulate(main, 1, along_x * push)
        accumulate(main, 2, along_y * push)
        accumulate(before, 3, shape_before * push)
        accumulate(after, 3, shape_after * push)
        accumulate(main, 4, along_x * drawn[0] + along_y * drawn[1])
        accumulate(before, 4, shape_before * drawn[2])
        accumulate(after, 4, shape_after * drawn[2])
    own_tiles = [
        main[f] + pltpu.roll(before[f], CZ - 1, 1) - pltpu.roll(after[f], 1, 1) for f in range(5)
    ]
    lanes = lax.broadcasted_iota(jnp.int32, TILE, 1)
    outer = step_length * two_thirds * step_length
    x_below, x_above = sorted_field(sources[0], 5, here[0], sizes[0])
    y_below, y_above = sorted_field(sources[1], 5, here[1], sizes[1])
    z_below, z_above = sorted_lanes(sources[2], here[2], sizes[2])
    aligned_above = jnp.zeros(TILE, jnp.float32)
    aligned_below = jnp.zeros(TILE, jnp.float32)
    for component in range(5):
        group = lanes // (2 * CX) == component
        shift = 2 * CX * (component - 5)
        aligned_above = jnp.where(
            group & (lanes % 2 == 0), pltpu.roll(z_above, (shift - 1) % CZ, 1), aligned_above
        )
        aligned_below = jnp.where(
            group & (lanes % 2 == 1), pltpu.roll(z_below, (shift + 1) % CZ, 1), aligned_below
        )
    above = -outer * aligned_above * packed
    below = outer * aligned_below * packed
    last = CZ - BZ
    contributions = [
        own_tiles,
        [(-outer * x_above) * x_high[f] for f in range(5)],
        [(outer * x_below) * x_low[f] for f in range(5)],
        [(-outer * y_above) * y_high[f] for f in range(5)],
        [(outer * y_below) * y_low[f] for f in range(5)],
        [jnp.where(lanes < BZ, pltpu.roll(above, (-BZ * f) % CZ, 1), 0.0) for f in range(5)],
        [jnp.where(lanes >= last, pltpu.roll(below, (last - BZ * f) % CZ, 1), 0.0) for f in range(5)],
    ]
    merged = [merge_rows(tiles) for tiles in contributions]
    aims = [jnp.broadcast_to(targets[j : j + 1, :], TILE) for j in range(len(OFFSETS))]

    def fill(device):
        total = None
        for tile, aim in zip(merged, aims):
            part = jnp.where(aim == device, tile, 0.0)
            total = part if total is None else total + part
        table[device] = total

    devices = table.shape[0]
    if devices <= 64:
        for device in range(devices):
            fill(device)
    else:
        lax.fori_loop(0, devices, lambda device, carry: (fill(device), carry)[1], 0)


def last_kernel(sizes, base, table, *refs):
    received, (out, gradient, done, sent) = split(refs, sizes)
    add_halo(base, received, two_thirds * step_length, sizes, done)
    copy = pltpu.make_async_copy(done, out, sent)
    copy.start()
    devices = table.shape[0]
    total = table[0]
    if devices <= 64:
        for device in range(1, devices):
            total = total + table[device]
    else:
        total = lax.fori_loop(1, devices, lambda device, old: old + table[device], total)
    for shift in (1, 2, 4, 8):
        total = total + pltpu.roll(total, CZ - shift, 1)
    sublanes = lax.broadcasted_iota(jnp.int32, TILE, 0)
    lanes = lax.broadcasted_iota(jnp.int32, TILE, 1)
    result = jnp.zeros(TILE, jnp.float32)
    total = pltpu.roll(total, 0, 1, stride=BOXES, stride_axis=0)
    for box in range(BOXES):
        moved = pltpu.roll(total, (box - BZ * box) % CZ, 1)
        result = jnp.where(lanes == BOXES * sublanes + box, moved, result)
    for shift in (4, 2, 1):
        result = result + pltpu.roll(result, shift, 0)
    gradient[...] = result[0:1, : 5 * BOXES]
    copy.wait()


VMEM = pl.BlockSpec(memory_space=pltpu.VMEM)
SMEM = pl.BlockSpec(memory_space=pltpu.SMEM)
HBM = pl.BlockSpec(memory_space=pltpu.HBM)


def call(
    kernel, in_specs, operands, out_shapes, out_specs=None, scratch=(), dtype=jnp.float32, vmem=16
):
    return pl.pallas_call(
        kernel,
        out_shape=[jax.ShapeDtypeStruct(shape, dtype) for shape in out_shapes],
        in_specs=in_specs,
        out_specs=out_specs or [VMEM] * len(out_shapes),
        scratch_shapes=list(scratch),
        compiler_params=pltpu.CompilerParams(vmem_limit_bytes=vmem * 1024 * 1024),
        cost_estimate=pl.CostEstimate(flops=2000000, bytes_accessed=1000000, transcendentals=0),
    )(*operands)


def body(
    terminal_adjoint,
    density,
    velocity,
    stiffness,
    sponge,
    source_shape,
    brick_level,
    brick_patch,
    patch_owner,
):
    sizes = tuple(lax.axis_size(axis) for axis in AXES)
    permutations = (
        pairings(sizes, 0, 1),
        pairings(sizes, 1, 1),
        pairings(sizes, 2, 1),
    )
    devices = patch_owner.shape[0]
    state_shape = terminal_adjoint.shape
    start = terminal_adjoint.reshape(STATE)
    density, stiffness, sponge, source = (
        array.reshape(FLAT) for array in (density, stiffness, sponge, source_shape)
    )
    velocity = velocity.reshape((3,) + FLAT)
    level = jnp.transpose(brick_level, (0, 2, 1))
    patches = jnp.transpose(brick_patch, (0, 2, 1))

    def message_shapes(fields):
        return [
            TILE if key[0] == 2 else (fields,) + TILE for key in message_keys(sizes, True)
        ]

    def exchange(messages):
        sends = dict(zip(message_keys(sizes, True), messages))
        sends[2, 1] = sends[2, 0]
        return [
            lax.ppermute(sends[key], AXES, permutations[key[0]][key[1]])
            for key in message_keys(sizes, False)
        ]

    scaled, *sent = call(
        functools.partial(first_kernel, sizes),
        [SMEM] + [HBM] * 5,
        (level, start, density, velocity, stiffness, source),
        [(6,) + FLAT] + message_shapes(6),
        scratch=[
            pltpu.VMEM(STATE, jnp.float32),
            pltpu.VMEM(FLAT, jnp.float32),
            pltpu.VMEM((3,) + FLAT, jnp.float32),
            pltpu.VMEM(FLAT, jnp.float32),
            pltpu.VMEM(FLAT, jnp.float32),
            pltpu.SemaphoreType.DMA((5,)),
        ],
        vmem=60,
    )
    received_one = exchange(sent)
    (targets,) = call(
        functools.partial(target_kernel, sizes),
        [SMEM] * 2,
        (patches, patch_owner),
        [TILE],
        dtype=jnp.int32,
    )
    (base,) = call(
        functools.partial(own_kernel, (0.0, 1.0)), [VMEM] * 3, (scaled, sponge, start), [STATE]
    )
    operands = (base, scaled, *received_one)
    section, *sent = call(
        functools.partial(stage_kernel, sizes, step_length),
        [VMEM] * len(operands),
        operands,
        [STATE] + message_shapes(5),
    )
    received = exchange(sent)
    (base,) = call(
        functools.partial(own_kernel, (0.75, 0.25)),
        [VMEM] * 4,
        (scaled, sponge, start, section),
        [STATE],
    )
    shapes, sums = call(
        shape_kernel, [VMEM] * 4, (source, scaled, sponge, start), [(7,) + FLAT, (5,) + TILE]
    )
    operands = (base, scaled, shapes, sums, targets, *received, *received_one)
    section, table, *sent = call(
        functools.partial(gradient_kernel, sizes, 0.25 * step_length),
        [VMEM] * len(operands),
        operands,
        [STATE, (devices,) + TILE] + message_shapes(5),
    )
    table = lax.all_to_all(table, AXES, 0, 0, tiled=True)
    received = exchange(sent)
    (base,) = call(
        functools.partial(own_kernel, (third, two_thirds)),
        [VMEM] * 4,
        (scaled, sponge, start, section),
        [STATE],
    )
    operands = (base, table, *received)
    adjoint, gradient = call(
        functools.partial(last_kernel, sizes),
        [VMEM] * len(operands),
        operands,
        [STATE, (1, 5 * BOXES)],
        [HBM, VMEM],
        [pltpu.VMEM(STATE, jnp.float32), pltpu.SemaphoreType.DMA],
    )
    return adjoint.reshape(state_shape), gradient


def solution(mesh):
    in_specs = (
        P(None, "gx", "gy", "gz"),
        P("gx", "gy", "gz"),
        P(None, "gx", "gy", "gz"),
        P("gx", "gy", "gz"),
        P("gx", "gy", "gz"),
        P("gx", "gy", "gz"),
        P(),
        P(),
        P(),
    )
    out_specs = (P(None, "gx", "gy", "gz"), P(("gx", "gy", "gz"), None))
    return jax.shard_map(body, mesh=mesh, in_specs=in_specs, out_specs=out_specs, check_vma=False)
```

```python
import functools

import jax
import jax.numpy as jnp
from jax import lax
from jax.experimental import pallas as pl
from jax.experimental.pallas import tpu as pltpu
from jax.sharding import PartitionSpec as P

CX = 8
CY = 8
CZ = 128
BZ = 16
BOXES = CZ // BZ
ROWS = CX * CY

AXES = ("gx", "gy", "gz")

step_length = 0.14
third = 1.0 / 3.0
two_thirds = 2.0 / 3.0

TILE = (CY, CZ)
FLAT = (ROWS, CZ)
STATE = (5,) + FLAT


def pairings(sizes, axis, near_axis):
    size = sizes[axis]
    first, second = [], []
    for x in range(sizes[0]):
        for y in range(sizes[1]):
            for z in range(sizes[2]):
                here = [x, y, z]
                index = (x * sizes[1] + y) * sizes[2] + z
                place = here[axis]
                other = list(here)
                other[axis] = place ^ 1
                first.append((index, (other[0] * sizes[1] + other[1]) * sizes[2] + other[2]))
                other = list(here)
                if 0 < place < size - 1 or near_axis == axis:
                    other[axis] = (place + (1 if place % 2 else -1)) % size
                else:
                    other[near_axis] = here[near_axis] ^ 1
                second.append((index, (other[0] * sizes[1] + other[1]) * sizes[2] + other[2]))
    return first, second if size > 2 else None


def positions():
    return [lax.axis_index(axis) for axis in AXES]


def tile_at(x):
    return slice(x * CY, (x + 1) * CY)


def row_at(y):
    return pl.ds(y, CX, stride=CY)


def partials_of(adjoint, speed, density, stiffness, inverse, direction):
    components = [speed * component for component in adjoint]
    row = 1 + direction
    components[row] = components[row] + (density * adjoint[0] + stiffness * adjoint[4])
    components[4] = components[4] + adjoint[row] * inverse
    return components


def faces_at(state, scaled, rows, direction):
    adjoint = [state[component, rows, :] for component in range(5)]
    return partials_of(
        adjoint,
        scaled[direction, rows, :],
        scaled[3, rows, :],
        scaled[4, rows, :],
        scaled[5, rows, :],
        direction,
    )


def pack_lanes(fields):
    lanes = lax.broadcasted_iota(jnp.int32, TILE, 1) // 2
    packed = jnp.zeros(TILE, jnp.float32)
    for index, field in enumerate(fields):
        for x in range(CX):
            k = index * CX + x
            packed = jnp.where(lanes == k, pltpu.roll(field[x], (2 * k + 1) % CZ, 1), packed)
    return packed


def put_pair(low, high, position, outs):
    even = position % 2 == 0
    for index, (below, above) in enumerate(zip(low, high)):
        outs[0][index] = jnp.where(even, above, below)
        if outs[1] is not None:
            outs[1][index] = jnp.where(even, below, above)


def put_messages(state, scaled, source, outs):
    here = positions()
    x_low = faces_at(state, scaled, tile_at(0), 0)
    x_high = faces_at(state, scaled, tile_at(CX - 1), 0)
    y_low = faces_at(state, scaled, row_at(0), 1)
    y_high = faces_at(state, scaled, row_at(CY - 1), 1)
    z_tiles = [faces_at(state, scaled, tile_at(x), 2) for x in range(CX)]
    z_fields = [[z_tiles[x][component] for x in range(CX)] for component in range(5)]
    if source is None:
        extra = [[]] * 4
    else:
        rows = (tile_at(0), tile_at(CX - 1), row_at(0), row_at(CY - 1))
        extra = [[source[row, :]] for row in rows]
        z_fields.append([source[tile_at(x), :] for x in range(CX)])
    put_pair(x_low + extra[0], x_high + extra[1], here[0], outs[0])
    put_pair(y_low + extra[2], y_high + extra[3], here[1], outs[1])
    packed = pack_lanes(z_fields)
    outs[2][0][...] = packed
    return x_low, x_high, y_low, y_high, packed


def sort_pair(first, second, position, size):
    even = position % 2 == 0
    zero = jnp.zeros_like(first)
    if second is None:
        return jnp.where(even, zero, first), jnp.where(even, first, zero)
    below = jnp.where(position == 0, zero, jnp.where(even, second, first))
    above = jnp.where(position == size - 1, zero, jnp.where(even, first, second))
    return below, above


def sorted_field(refs, index, position, size):
    first, second = refs
    return sort_pair(first[index], None if second is None else second[index], position, size)


def sorted_lanes(refs, position, size):
    first, second = refs
    return sort_pair(first[...], None if second is None else second[...], position, size)


def add_halo(base, received, weight, sizes, out, finish=None):
    here = positions()
    lanes = lax.broadcasted_iota(jnp.int32, TILE, 1)
    edges = (lanes == 0) | (lanes == CZ - 1)
    z_below, z_above = sorted_lanes(received[2], here[2], sizes[2])
    z_halo = weight * jnp.where(
        lanes % 2 == 0, pltpu.roll(z_above, CZ - 1, 1), -pltpu.roll(z_below, 1, 1)
    )
    for component in range(5):
        x_below, x_above = sorted_field(received[0], component, here[0], sizes[0])
        y_below, y_above = sorted_field(received[1], component, here[1], sizes[1])
        for x in range(CX):
            k = component * CX + x
            value = base[component, tile_at(x), :]
            value = value + jnp.where(edges, pltpu.roll(z_halo, (CZ - 1 - 2 * k) % CZ, 1), 0.0)
            if x == 0:
                value = value - weight * x_below
            if x == CX - 1:
                value = value + weight * x_above
            out[component, tile_at(x), :] = value
        out[component, row_at(0), :] = out[component, row_at(0), :] - weight * y_below
        out[component, row_at(CY - 1), :] = out[component, row_at(CY - 1), :] + weight * y_above
        if finish is not None:
            finish(component)


ORDER = ((1, 0), (2, 0), (0, 1), (0, 0), (1, 1), (2, 1))


def message_keys(sizes, sent):
    keys = [key for key in ORDER if key[1] == 0 or sizes[key[0]] > 2]
    return [key for key in keys if not (sent and key == (2, 1))]


def split(refs, sizes, sent=False):
    refs, out = list(refs), [[None, None] for axis in range(3)]
    for axis, which in message_keys(sizes, sent):
        out[axis][which] = refs.pop(0)
    return out, refs


def first_kernel(sizes, level, adjoint, density, velocity, stiffness, source, scaled, *refs):
    outs, scratch = split(refs, sizes, True)
    level_now, adjoint_now, density_now, velocity_now, stiffness_now, source_now, arrived = scratch
    pairs = (
        (level, level_now),
        (density, density_now),
        (velocity, velocity_now),
        (stiffness, stiffness_now),
        (adjoint, adjoint_now),
        (source, source_now),
    )
    copies = [
        pltpu.make_async_copy(there, here, arrived.at[index])
        for index, (there, here) in enumerate(pairs)
    ]
    for copy in copies:
        copy.start()
    for copy in copies:
        copy.wait()
    here = positions()
    own_level = level_now[here[0], here[2], here[1]]
    half_inverse = 0.5 * lax.shift_left(jnp.int32(1), own_level).astype(jnp.float32)
    for direction in range(3):
        scaled[direction] = half_inverse * velocity_now[direction]
    scaled[3] = half_inverse * density_now[...]
    scaled[4] = half_inverse * stiffness_now[...]
    scaled[5] = half_inverse / density_now[...]
    put_messages(adjoint_now, scaled, source_now, outs)


def own_kernel(weights, scaled, sponge, *refs):
    keep, blend = weights
    start, state, out = refs if keep else (None,) + refs
    rows = lax.broadcasted_iota(jnp.int32, TILE, 0)
    lanes = lax.broadcasted_iota(jnp.int32, TILE, 1)
    tiles = [
        [faces_at(state, scaled, tile_at(x), direction) for direction in range(3)]
        for x in range(CX)
    ]
    for x in range(CX):
        damp = sponge[tile_at(x), :]
        for component in range(5):
            total = None
            if x < CX - 1:
                total = tiles[x + 1][0][component]
            if x > 0:
                before = tiles[x - 1][0][component]
                total = -before if total is None else total - before
            part = tiles[x][1][component]
            total = total + jnp.where(rows == CY - 1, 0.0, pltpu.roll(part, CY - 1, 0))
            total = total - jnp.where(rows == 0, 0.0, pltpu.roll(part, 1, 0))
            part = tiles[x][2][component]
            total = total + jnp.where(lanes == CZ - 1, 0.0, pltpu.roll(part, CZ - 1, 1))
            total = total - jnp.where(lanes == 0, 0.0, pltpu.roll(part, 1, 1))
            value = state[component, tile_at(x), :]
            value = blend * (value + step_length * (total - damp * value))
            if keep:
                value = value + keep * start[component, tile_at(x), :]
            out[component, tile_at(x), :] = value


def shape_kernel(sizes, source, scaled, sponge, start, *refs):
    sources, (shapes, sums, faces) = split(refs, sizes)
    rows = lax.broadcasted_iota(jnp.int32, TILE, 0)
    lanes = lax.broadcasted_iota(jnp.int32, TILE, 1)
    outer = step_length * two_thirds
    inner = outer * step_length
    totals = [None] * 5
    for x in range(CX):
        at = tile_at(x)
        shape = source[at, :]
        along_x = jnp.zeros(TILE, jnp.float32)
        if x > 0:
            along_x = along_x + source[tile_at(x - 1), :]
        if x < CX - 1:
            along_x = along_x - source[tile_at(x + 1), :]
        along_y = jnp.where(rows == 0, 0.0, pltpu.roll(shape, 1, 0)) - jnp.where(
            rows == CY - 1, 0.0, pltpu.roll(shape, CY - 1, 0)
        )
        before = inner * jnp.where(lanes == 0, 0.0, pltpu.roll(shape, 1, 1))
        after = inner * jnp.where(lanes == CZ - 1, 0.0, pltpu.roll(shape, CZ - 1, 1))
        along_x, along_y = inner * along_x, inner * along_y
        own = outer * shape * (1.0 - step_length * sponge[at, :])
        own = own + scaled[0, at, :] * along_x + scaled[1, at, :] * along_y
        for index, value in enumerate(
            (own, scaled[2, at, :] * before, scaled[2, at, :] * after, along_x, along_y, before, after)
        ):
            shapes[index, at, :] = value
        weighted = (step_length * third) * shape
        for component in range(5):
            value = weighted * start[component, at, :]
            totals[component] = value if totals[component] is None else totals[component] + value
    for component in range(5):
        sums[component] = totals[component]
    here = positions()
    x_below, x_above = sorted_field(sources[0], 5, here[0], sizes[0])
    y_below, y_above = sorted_field(sources[1], 5, here[1], sizes[1])
    z_below, z_above = sorted_lanes(sources[2], here[2], sizes[2])
    aligned_above = jnp.zeros(TILE, jnp.float32)
    aligned_below = jnp.zeros(TILE, jnp.float32)
    for component in range(5):
        group = lanes // (2 * CX) == component
        shift = 2 * CX * (component - 5)
        aligned_above = jnp.where(
            group & (lanes % 2 == 0), pltpu.roll(z_above, (shift - 1) % CZ, 1), aligned_above
        )
        aligned_below = jnp.where(
            group & (lanes % 2 == 1), pltpu.roll(z_below, (shift + 1) % CZ, 1), aligned_below
        )
    for index, (sign, face) in enumerate(
        (
            (-inner, x_above),
            (inner, x_below),
            (-inner, y_above),
            (inner, y_below),
            (-inner, aligned_above),
            (inner, aligned_below),
        )
    ):
        faces[index] = sign * face


def stage_kernel(sizes, weight, base, scaled, *refs):
    received, (section, *outs) = split(refs, sizes)
    add_halo(base, received, weight, sizes, section)
    put_messages(section, scaled, None, split(outs, sizes, True)[0])


def sublane_total(tile):
    for shift in (4, 2, 1):
        tile = tile + pltpu.roll(tile, shift, 0)
    return tile


def group_totals(tile):
    for shift in (1, 2, 4, 8):
        tile = tile + pltpu.roll(tile, CZ - shift, 1)
    return tile


def target_kernel(sizes, patches, owners, out):
    here = positions()
    sublanes = lax.broadcasted_iota(jnp.int32, TILE, 0)
    result = jnp.zeros(TILE, jnp.int32)
    for index, offset in enumerate(OFFSETS):
        place = [
            jnp.clip(here[axis] + offset[axis], 0, sizes[axis] - 1) for axis in range(3)
        ]
        target = owners[patches[place[0], place[2], place[1]]]
        result = jnp.where(sublanes == index, target, result)
    out[...] = result


OFFSETS = (
    (0, 0, 0),
    (1, 0, 0),
    (-1, 0, 0),
    (0, 1, 0),
    (0, -1, 0),
    (0, 0, 1),
    (0, 0, -1),
)


def gradient_kernel(sizes, weight, base, scaled, shapes, sums, faces, targets, *refs):
    received, (section, table, *rest) = split(refs, sizes)
    outs, (tiles, blocks) = split(rest, sizes, True)
    add_halo(base, received, weight, sizes, section)
    x_low, x_high, y_low, y_high, packed = put_messages(section, scaled, None, outs)
    main = [sums[component] for component in range(5)]
    before = [None] * 5
    after = [None] * 5

    def accumulate(totals, component, value):
        old = totals[component]
        totals[component] = value if old is None else old + value

    for x in range(CX):
        at = tile_at(x)
        state = [section[component, at, :] for component in range(5)]
        own, lane_before, lane_after, along_x, along_y, shape_before, shape_after = (
            shapes[index, at, :] for index in range(7)
        )
        push = scaled[3, at, :] * state[0] + scaled[4, at, :] * state[4]
        drawn = [scaled[5, at, :] * state[1 + direction] for direction in range(3)]
        for component in range(5):
            accumulate(main, component, own * state[component])
            accumulate(before, component, lane_before * state[component])
            accumulate(after, component, lane_after * state[component])
        accumulate(main, 1, along_x * push)
        accumulate(main, 2, along_y * push)
        accumulate(before, 3, shape_before * push)
        accumulate(after, 3, shape_after * push)
        accumulate(main, 4, along_x * drawn[0] + along_y * drawn[1])
        accumulate(before, 4, shape_before * drawn[2])
        accumulate(after, 4, shape_after * drawn[2])
    lanes = lax.broadcasted_iota(jnp.int32, TILE, 1)
    for f in range(5):
        own = main[f] + pltpu.roll(before[f], CZ - 1, 1) - pltpu.roll(after[f], 1, 1)
        for index, tile in enumerate(
            (own, faces[0] * x_high[f], faces[1] * x_low[f], faces[2] * y_high[f], faces[3] * y_low[f])
        ):
            tiles[index, f * CY : (f + 1) * CY, :] = tile
    sublanes = lax.broadcasted_iota(jnp.int32, TILE, 0)
    for index in range(5):
        total = tiles[index, pl.ds(0, 5, stride=CY), :]
        for row in range(1, CY):
            total = total + tiles[index, pl.ds(row, 5, stride=CY), :]
        total = jnp.concatenate([total, jnp.zeros((CY - 5, CZ), jnp.float32)], axis=0)
        total = jnp.where(lanes % BZ == 0, group_totals(total), 0.0)
        total = pltpu.roll(total, 0, 1, stride=1, stride_axis=0)
        blocks[index] = total
    for index, (face, first) in enumerate(((faces[4], 0), (faces[5], CZ - BZ))):
        total = group_totals(sublane_total(face * packed))
        placed = jnp.zeros(TILE, jnp.float32)
        for f in range(5):
            moved = pltpu.roll(total, (first + f - 2 * CX * f) % CZ, 1)
            placed = jnp.where(lanes == first + f, moved, placed)
        blocks[5 + index] = jnp.where(sublanes == 0, placed, 0.0)
    sums_over = []
    for index in range(7):
        total = blocks[index, 0:1, :]
        for row in range(1, 5 if index < 5 else 1):
            total = total + blocks[index, row : row + 1, :]
        sums_over.append(jnp.broadcast_to(total, TILE))
    aims = [jnp.broadcast_to(targets[j : j + 1, :], TILE) for j in range(len(OFFSETS))]

    def fill(start):
        total = None
        for block, aim in zip(sums_over, aims):
            part = jnp.where(aim == sublanes + start, block, 0.0)
            total = part if total is None else total + part
        table[pl.ds(start, CY), :] = total

    devices = table.shape[0]
    if devices <= 64:
        for start in range(0, devices, CY):
            fill(start)
    else:
        lax.fori_loop(
            0, devices // CY, lambda step, carry: (fill(pl.multiple_of(step * CY, CY)), carry)[1], 0
        )


def last_kernel(sizes, base, table, *refs):
    received, (out, gradient, done, block, sent) = split(refs, sizes)
    devices = table.shape[0]
    total = table[0:CY, :]
    if devices <= 64:
        for start in range(CY, devices, CY):
            total = total + table[start : start + CY, :]
    else:
        total = lax.fori_loop(
            1,
            devices // CY,
            lambda step, old: old + table[pl.ds(pl.multiple_of(step * CY, CY), CY), :],
            total,
        )
    total = sublane_total(total)
    lanes = lax.broadcasted_iota(jnp.int32, TILE, 1)
    result = jnp.zeros(TILE, jnp.float32)
    for component in range(5):
        for box in range(BOXES):
            want, have = component * BOXES + box, box * BZ + component
            result = jnp.where(lanes == want, pltpu.roll(total, (want - have) % CZ, 1), result)
    block[...] = result[0:1, : 5 * BOXES]
    copies = [pltpu.make_async_copy(block, gradient, sent.at[5])]
    copies[0].start()

    def send(component):
        copy = pltpu.make_async_copy(done.at[component], out.at[component], sent.at[component])
        copy.start()
        copies.append(copy)

    add_halo(base, received, two_thirds * step_length, sizes, done, send)
    for copy in copies:
        copy.wait()


VMEM = pl.BlockSpec(memory_space=pltpu.VMEM)
SMEM = pl.BlockSpec(memory_space=pltpu.SMEM)
HBM = pl.BlockSpec(memory_space=pltpu.HBM)


def call(kernel, in_specs, operands, out_shapes, scratch=(), dtype=jnp.float32, space=pltpu.VMEM):
    operands = [
        pltpu.with_memory_space_constraint(operand, pltpu.HBM) if spec is HBM else operand
        for spec, operand in zip(in_specs, operands)
    ]
    return pl.pallas_call(
        kernel,
        out_shape=[space(shape, dtype) for shape in out_shapes],
        in_specs=in_specs,
        out_specs=[pl.BlockSpec(memory_space=space)] * len(out_shapes),
        scratch_shapes=list(scratch),
        compiler_params=pltpu.CompilerParams(vmem_limit_bytes=16 * 1024 * 1024),
        cost_estimate=pl.CostEstimate(flops=2000000, bytes_accessed=1000000, transcendentals=0),
    )(*operands)


def body(
    terminal_adjoint,
    density,
    velocity,
    stiffness,
    sponge,
    source_shape,
    brick_level,
    brick_patch,
    patch_owner,
):
    sizes = tuple(lax.axis_size(axis) for axis in AXES)
    permutations = (
        pairings(sizes, 0, 1),
        pairings(sizes, 1, 1),
        pairings(sizes, 2, 1),
    )
    devices = patch_owner.shape[0]
    state_shape = terminal_adjoint.shape
    start = terminal_adjoint.reshape(STATE)
    density, stiffness, sponge, source = (
        array.reshape(FLAT) for array in (density, stiffness, sponge, source_shape)
    )
    velocity = velocity.reshape((3,) + FLAT)
    level = jnp.transpose(brick_level, (0, 2, 1))
    patches = jnp.transpose(brick_patch, (0, 2, 1))

    def message_shapes(fields):
        return [
            TILE if key[0] == 2 else (fields,) + TILE for key in message_keys(sizes, True)
        ]

    def exchange(messages):
        sends = dict(zip(message_keys(sizes, True), messages))
        sends[2, 1] = sends[2, 0]
        return [
            lax.ppermute(sends[key], AXES, permutations[key[0]][key[1]])
            for key in message_keys(sizes, False)
        ]

    scaled, *sent = call(
        functools.partial(first_kernel, sizes),
        [HBM] * 6,
        (level, start, density, velocity, stiffness, source),
        [(6,) + FLAT] + message_shapes(6),
        scratch=[
            pltpu.SMEM(level.shape, jnp.int32),
            pltpu.VMEM(STATE, jnp.float32),
            pltpu.VMEM(FLAT, jnp.float32),
            pltpu.VMEM((3,) + FLAT, jnp.float32),
            pltpu.VMEM(FLAT, jnp.float32),
            pltpu.VMEM(FLAT, jnp.float32),
            pltpu.SemaphoreType.DMA((6,)),
        ],
    )
    received_one = exchange(sent)
    (targets,) = call(
        functools.partial(target_kernel, sizes),
        [SMEM] * 2,
        (patches, patch_owner),
        [TILE],
        dtype=jnp.int32,
    )
    (base,) = call(
        functools.partial(own_kernel, (0.0, 1.0)), [VMEM] * 3, (scaled, sponge, start), [STATE]
    )
    operands = (base, scaled, *received_one)
    section, *sent = call(
        functools.partial(stage_kernel, sizes, step_length),
        [VMEM] * len(operands),
        operands,
        [STATE] + message_shapes(5),
    )
    received = exchange(sent)
    (base,) = call(
        functools.partial(own_kernel, (0.75, 0.25)),
        [VMEM] * 4,
        (scaled, sponge, start, section),
        [STATE],
    )
    operands = (source, scaled, sponge, start, *received_one)
    shapes, sums, faces = call(
        functools.partial(shape_kernel, sizes),
        [VMEM] * len(operands),
        operands,
        [(7,) + FLAT, (5,) + TILE, (6,) + TILE],
    )
    operands = (base, scaled, shapes, sums, faces, targets, *received)
    section, table, *sent = call(
        functools.partial(gradient_kernel, sizes, 0.25 * step_length),
        [VMEM] * len(operands),
        operands,
        [STATE, (devices, CZ)] + message_shapes(5),
        scratch=[
            pltpu.VMEM((5, 5 * CY, CZ), jnp.float32),
            pltpu.VMEM((7,) + TILE, jnp.float32),
        ],
    )
    table = lax.all_to_all(table.reshape(devices, 1, CZ), AXES, 0, 0, tiled=True)
    received = exchange(sent)
    (base,) = call(
        functools.partial(own_kernel, (third, two_thirds)),
        [VMEM] * 4,
        (scaled, sponge, start, section),
        [STATE],
    )
    operands = (base, table.reshape(devices, CZ), *received)
    adjoint, gradient = call(
        functools.partial(last_kernel, sizes),
        [VMEM] * len(operands),
        operands,
        [STATE, (1, 5 * BOXES)],
        scratch=[
            pltpu.VMEM(STATE, jnp.float32),
            pltpu.VMEM((1, 5 * BOXES), jnp.float32),
            pltpu.SemaphoreType.DMA((6,)),
        ],
        space=pltpu.HBM,
    )
    return adjoint.reshape(state_shape), gradient


def solution(mesh):
    in_specs = (
        P(None, "gx", "gy", "gz"),
        P("gx", "gy", "gz"),
        P(None, "gx", "gy", "gz"),
        P("gx", "gy", "gz"),
        P("gx", "gy", "gz"),
        P("gx", "gy", "gz"),
        P(),
        P(),
        P(),
    )
    out_specs = (P(None, "gx", "gy", "gz"), P(("gx", "gy", "gz"), None))
    return jax.shard_map(body, mesh=mesh, in_specs=in_specs, out_specs=out_specs, check_vma=False)
```

```python
import functools

import jax
import jax.numpy as jnp
from jax import lax
from jax.experimental import pallas as pl
from jax.experimental.pallas import tpu as pltpu
from jax.sharding import PartitionSpec as P

CX = 8
CY = 8
CZ = 128
BZ = 16
BOXES = CZ // BZ
ROWS = CX * CY

AXES = ("gx", "gy", "gz")

step_length = 0.14
third = 1.0 / 3.0
two_thirds = 2.0 / 3.0

BASE = 5 * BOXES
SHARE = CY // 2

TILE = (CY, CZ)
FLAT = (ROWS, CZ)
STATE = (5,) + FLAT


def pairings(sizes, axis, near_axis):
    size = sizes[axis]
    first, second = [], []
    for x in range(sizes[0]):
        for y in range(sizes[1]):
            for z in range(sizes[2]):
                here = [x, y, z]
                index = (x * sizes[1] + y) * sizes[2] + z
                place = here[axis]
                other = list(here)
                other[axis] = place ^ 1
                first.append((index, (other[0] * sizes[1] + other[1]) * sizes[2] + other[2]))
                other = list(here)
                if 0 < place < size - 1 or near_axis == axis:
                    other[axis] = (place + (1 if place % 2 else -1)) % size
                else:
                    other[near_axis] = here[near_axis] ^ 1
                second.append((index, (other[0] * sizes[1] + other[1]) * sizes[2] + other[2]))
    return first, second if size > 2 else None


def positions():
    return [lax.axis_index(axis) for axis in AXES]


def tile_at(x):
    return slice(x * CY, (x + 1) * CY)


def row_at(y):
    return pl.ds(y, CX, stride=CY)


def partials_of(adjoint, speed, density, stiffness, inverse, direction):
    components = [speed * component for component in adjoint]
    row = 1 + direction
    components[row] = components[row] + (density * adjoint[0] + stiffness * adjoint[4])
    components[4] = components[4] + adjoint[row] * inverse
    return components


def faces_at(state, scaled, rows, direction):
    adjoint = [state[component, rows, :] for component in range(5)]
    return partials_of(
        adjoint,
        scaled[direction, rows, :],
        scaled[3, rows, :],
        scaled[4, rows, :],
        scaled[5, rows, :],
        direction,
    )


def pack_lanes(fields):
    lanes = (lax.broadcasted_iota(jnp.int32, TILE, 1) + (CZ - BASE)) % CZ // 2
    tiles = []
    for index, field in enumerate(fields):
        for x in range(CX):
            k = index * CX + x
            tiles.append(pltpu.roll(field[x], (BASE + 2 * k + 1) % CZ, 1))
    bit = 1
    while len(tiles) > 1:
        upper = (lanes & bit) != 0
        pairs = [
            jnp.where(upper, tiles[at + 1], tiles[at]) if at + 1 < len(tiles) else tiles[at]
            for at in range(0, len(tiles), 2)
        ]
        tiles, bit = pairs, 2 * bit
    return tiles[0]


def put_pair(low, high, position, outs):
    even = position % 2 == 0
    for index, (below, above) in enumerate(zip(low, high)):
        outs[0][index] = jnp.where(even, above, below)
        if outs[1] is not None:
            outs[1][index] = jnp.where(even, below, above)


def outer_faces(state, scaled):
    x_low = faces_at(state, scaled, tile_at(0), 0)
    x_high = faces_at(state, scaled, tile_at(CX - 1), 0)
    y_low = faces_at(state, scaled, row_at(0), 1)
    y_high = faces_at(state, scaled, row_at(CY - 1), 1)
    z_tiles = [faces_at(state, scaled, tile_at(x), 2) for x in range(CX)]
    z_fields = [[z_tiles[x][component] for x in range(CX)] for component in range(5)]
    return x_low, x_high, y_low, y_high, z_fields


def put_messages(state, scaled, source, outs):
    here = positions()
    x_low, x_high, y_low, y_high, z_fields = outer_faces(state, scaled)
    if source is not None:
        x_low.append(source[tile_at(0), :])
        x_high.append(source[tile_at(CX - 1), :])
        y_low.append(source[row_at(0), :])
        y_high.append(source[row_at(CY - 1), :])
        z_fields.append([source[tile_at(x), :] for x in range(CX)])
    outs[2][0][...] = pack_lanes(z_fields)
    put_pair(x_low, x_high, here[0], outs[0])
    put_pair(y_low, y_high, here[1], outs[1])


def sort_pair(first, second, position, size):
    even = position % 2 == 0
    zero = jnp.zeros_like(first)
    if second is None:
        return jnp.where(even, zero, first), jnp.where(even, first, zero)
    below = jnp.where(position == 0, zero, jnp.where(even, second, first))
    above = jnp.where(position == size - 1, zero, jnp.where(even, first, second))
    return below, above


def sorted_field(refs, index, position, size):
    first, second = refs
    return sort_pair(first[index], None if second is None else second[index], position, size)


def sorted_lanes(refs, position, size):
    first, second = refs
    return sort_pair(first[...], None if second is None else second[...], position, size)


def add_halo(base, received, weight, sizes, out, finish=None, z_halo=None):
    here = positions()
    lanes = lax.broadcasted_iota(jnp.int32, TILE, 1)
    edges = (lanes == 0) | (lanes == CZ - 1)
    if z_halo is None:
        z_below, z_above = sorted_lanes(received[2], here[2], sizes[2])
        z_halo = jnp.where(
            lanes % 2 == 0, pltpu.roll(z_above, CZ - 1, 1), -pltpu.roll(z_below, 1, 1)
        )
    z_halo = weight * z_halo
    for component in range(5):
        x_below, x_above = sorted_field(received[0], component, here[0], sizes[0])
        y_below, y_above = sorted_field(received[1], component, here[1], sizes[1])
        for x in range(CX):
            k = component * CX + x
            value = base[component, tile_at(x), :]
            value = value + jnp.where(edges, pltpu.roll(z_halo, (CZ - 1 - BASE - 2 * k) % CZ, 1), 0.0)
            if x == 0:
                value = value - weight * x_below
            if x == CX - 1:
                value = value + weight * x_above
            out[component, tile_at(x), :] = value
        out[component, row_at(0), :] = out[component, row_at(0), :] - weight * y_below
        out[component, row_at(CY - 1), :] = out[component, row_at(CY - 1), :] + weight * y_above
        if finish is not None:
            finish(component)


ORDER = ((1, 0), (2, 0), (0, 1), (0, 0), (1, 1), (2, 1))


def message_keys(sizes, sent, with_z=True):
    keys = [key for key in ORDER if key[1] == 0 or sizes[key[0]] > 2]
    keys = [key for key in keys if with_z or key[0] != 2]
    return [key for key in keys if not (sent and key == (2, 1))]


def split(refs, sizes, sent=False, with_z=True):
    refs, out = list(refs), [[None, None] for axis in range(3)]
    for axis, which in message_keys(sizes, sent, with_z):
        out[axis][which] = refs.pop(0)
    return out, refs


def first_kernel(sizes, level, adjoint, density, velocity, stiffness, source, scaled, *refs):
    outs, scratch = split(refs, sizes, True)
    level_now, adjoint_now, density_now, velocity_now, stiffness_now, source_now, arrived = scratch
    pairs = (
        (level, level_now),
        (density, density_now),
        (velocity, velocity_now),
        (stiffness, stiffness_now),
        (adjoint, adjoint_now),
        (source, source_now),
    )
    copies = [
        pltpu.make_async_copy(there, here, arrived.at[index])
        for index, (there, here) in enumerate(pairs)
    ]
    for copy in copies:
        copy.start()
    for copy in copies:
        copy.wait()
    here = positions()
    own_level = level_now[here[0], here[2], here[1]]
    half_inverse = 0.5 * lax.shift_left(jnp.int32(1), own_level).astype(jnp.float32)
    for direction in range(3):
        scaled[direction] = half_inverse * velocity_now[direction]
    scaled[3] = half_inverse * density_now[...]
    scaled[4] = half_inverse * stiffness_now[...]
    scaled[5] = half_inverse / density_now[...]
    put_messages(adjoint_now, scaled, source_now, outs)


def own_kernel(weights, scaled, sponge, *refs):
    keep, blend = weights
    start, state, out = refs if keep else (None,) + refs
    rows = lax.broadcasted_iota(jnp.int32, TILE, 0)
    lanes = lax.broadcasted_iota(jnp.int32, TILE, 1)
    tiles = [
        [faces_at(state, scaled, tile_at(x), direction) for direction in range(3)]
        for x in range(CX)
    ]
    for x in range(CX):
        damp = sponge[tile_at(x), :]
        for component in range(5):
            total = None
            if x < CX - 1:
                total = tiles[x + 1][0][component]
            if x > 0:
                before = tiles[x - 1][0][component]
                total = -before if total is None else total - before
            part = tiles[x][1][component]
            total = total + jnp.where(rows == CY - 1, 0.0, pltpu.roll(part, CY - 1, 0))
            total = total - jnp.where(rows == 0, 0.0, pltpu.roll(part, 1, 0))
            part = tiles[x][2][component]
            total = total + jnp.where(lanes == CZ - 1, 0.0, pltpu.roll(part, CZ - 1, 1))
            total = total - jnp.where(lanes == 0, 0.0, pltpu.roll(part, 1, 1))
            value = state[component, tile_at(x), :]
            value = blend * (value + step_length * (total - damp * value))
            if keep:
                value = value + keep * start[component, tile_at(x), :]
            out[component, tile_at(x), :] = value


def shape_kernel(sizes, source, scaled, sponge, start, *refs):
    sources, (shapes, sums, faces) = split(refs, sizes)
    rows = lax.broadcasted_iota(jnp.int32, TILE, 0)
    lanes = lax.broadcasted_iota(jnp.int32, TILE, 1)
    outer = step_length * two_thirds
    inner = outer * step_length
    totals = [None] * 5
    for x in range(CX):
        at = tile_at(x)
        shape = source[at, :]
        along_x = jnp.zeros(TILE, jnp.float32)
        if x > 0:
            along_x = along_x + source[tile_at(x - 1), :]
        if x < CX - 1:
            along_x = along_x - source[tile_at(x + 1), :]
        along_y = jnp.where(rows == 0, 0.0, pltpu.roll(shape, 1, 0)) - jnp.where(
            rows == CY - 1, 0.0, pltpu.roll(shape, CY - 1, 0)
        )
        before = inner * jnp.where(lanes == 0, 0.0, pltpu.roll(shape, 1, 1))
        after = inner * jnp.where(lanes == CZ - 1, 0.0, pltpu.roll(shape, CZ - 1, 1))
        along_x, along_y = inner * along_x, inner * along_y
        own = outer * shape * (1.0 - step_length * sponge[at, :])
        own = own + scaled[0, at, :] * along_x + scaled[1, at, :] * along_y
        for index, value in enumerate(
            (own, scaled[2, at, :] * before, scaled[2, at, :] * after, along_x, along_y, before, after)
        ):
            shapes[index, at, :] = value
        weighted = (step_length * third) * shape
        for component in range(5):
            value = weighted * start[component, at, :]
            totals[component] = value if totals[component] is None else totals[component] + value
    for component in range(5):
        sums[component] = totals[component]
    here = positions()
    x_below, x_above = sorted_field(sources[0], 5, here[0], sizes[0])
    y_below, y_above = sorted_field(sources[1], 5, here[1], sizes[1])
    z_below, z_above = sorted_lanes(sources[2], here[2], sizes[2])
    aligned_above = jnp.zeros(TILE, jnp.float32)
    aligned_below = jnp.zeros(TILE, jnp.float32)
    for component in range(5):
        group = (lanes >= BASE) & ((lanes - BASE) // (2 * CX) == component)
        shift = 2 * CX * (component - 5)
        aligned_above = jnp.where(
            group & (lanes % 2 == 0), pltpu.roll(z_above, (shift - 1) % CZ, 1), aligned_above
        )
        aligned_below = jnp.where(
            group & (lanes % 2 == 1), pltpu.roll(z_below, (shift + 1) % CZ, 1), aligned_below
        )
    for index, (sign, face) in enumerate(
        (
            (-inner, x_above),
            (inner, x_below),
            (-inner, y_above),
            (inner, y_below),
            (-inner, aligned_above),
            (inner, aligned_below),
        )
    ):
        faces[index] = sign * face


def stage_kernel(sizes, weight, base, scaled, *refs):
    received, (section, *outs) = split(refs, sizes)
    add_halo(base, received, weight, sizes, section)
    put_messages(section, scaled, None, split(outs, sizes, True)[0])


def sublane_total(tile):
    for shift in (4, 2, 1):
        tile = tile + pltpu.roll(tile, shift, 0)
    return tile


def three_parts(value):
    parts = []
    for _ in range(3):
        part = value.astype(jnp.bfloat16)
        parts.append(part)
        value = value - part.astype(jnp.float32)
    return parts


def product(value, matrix):
    count = value.shape[0]
    stacked = jnp.concatenate(three_parts(value), axis=0)
    result = jnp.dot(stacked, matrix, preferred_element_type=jnp.float32)
    return result[:count] + result[count : 2 * count] + result[2 * count :]


def target_kernel(sizes, patches, owners, routes, gather):
    here = positions()
    shape = routes.shape
    rows = lax.broadcasted_iota(jnp.int32, shape, 0)
    lanes = lax.broadcasted_iota(jnp.int32, shape, 1) % (CY * CY)
    chosen = jnp.zeros(shape, jnp.bool_)
    for index, offset in enumerate(OFFSETS):
        place = [
            jnp.clip(here[axis] + offset[axis], 0, sizes[axis] - 1) for axis in range(3)
        ]
        target = owners[patches[place[0], place[2], place[1]]]
        chosen = chosen | ((lanes // CY == index) & (rows == target))
    routes[...] = jnp.where(chosen, 1.0, 0.0).astype(jnp.bfloat16)
    rows = lax.broadcasted_iota(jnp.int32, (CZ, CZ), 0)
    lanes = lax.broadcasted_iota(jnp.int32, (CZ, CZ), 1)
    for component in range(5):
        ones = lanes == BOXES * component + rows // BZ
        gather[component * CZ : (component + 1) * CZ, :] = jnp.where(ones, 1.0, 0.0).astype(
            jnp.bfloat16
        )
    for index, box in enumerate((0, BOXES - 1)):
        ones = (lanes == BOXES * ((rows - BASE) // (2 * CX)) + box) & (rows >= BASE)
        ones = ones & (rows < BASE + 5 * 2 * CX)
        start = (5 + index) * CZ
        gather[start : start + CZ, :] = jnp.where(ones, 1.0, 0.0).astype(jnp.bfloat16)


OFFSETS = (
    (0, 0, 0),
    (1, 0, 0),
    (-1, 0, 0),
    (0, 1, 0),
    (0, -1, 0),
    (0, 0, 1),
    (0, 0, -1),
)


def gradient_kernel(sizes, weight, base, scaled, shapes, sums, faces, routes, gather, *refs):
    received, (section, table, *rest) = split(refs, sizes)
    outs, (rows_out, sent) = split(rest, sizes, True, False)
    add_halo(base, received, weight, sizes, section)
    x_low, x_high, y_low, y_high, z_fields = outer_faces(section, scaled)
    packed = pack_lanes(z_fields)
    main = [sums[component] for component in range(5)]
    before = [None] * 5
    after = [None] * 5

    def accumulate(totals, component, value):
        old = totals[component]
        totals[component] = value if old is None else old + value

    for x in range(CX):
        at = tile_at(x)
        state = [section[component, at, :] for component in range(5)]
        own, lane_before, lane_after, along_x, along_y, shape_before, shape_after = (
            shapes[index, at, :] for index in range(7)
        )
        push = scaled[3, at, :] * state[0] + scaled[4, at, :] * state[4]
        drawn = [scaled[5, at, :] * state[1 + direction] for direction in range(3)]
        for component in range(5):
            accumulate(main, component, own * state[component])
            accumulate(before, component, lane_before * state[component])
            accumulate(after, component, lane_after * state[component])
        accumulate(main, 1, along_x * push)
        accumulate(main, 2, along_y * push)
        accumulate(before, 3, shape_before * push)
        accumulate(after, 3, shape_after * push)
        accumulate(main, 4, along_x * drawn[0] + along_y * drawn[1])
        accumulate(before, 4, shape_before * drawn[2])
        accumulate(after, 4, shape_after * drawn[2])
    columns = []
    for f in range(5):
        own = main[f] + pltpu.roll(before[f], CZ - 1, 1) - pltpu.roll(after[f], 1, 1)
        columns.append(
            jnp.concatenate(
                [own, faces[0] * x_high[f], faces[1] * x_low[f], faces[2] * y_high[f], faces[3] * y_low[f]],
                axis=0,
            )
        )
    blocks = product(jnp.concatenate(columns, axis=1), gather[: 5 * CZ, :])
    above = product(faces[4] * packed, gather[5 * CZ : 6 * CZ, :])
    below = product(faces[5] * packed, gather[6 * CZ :, :])
    blocks = jnp.concatenate([blocks, above, below, jnp.zeros(TILE, jnp.float32)], axis=0)
    devices = routes.shape[0]
    rows_out[pl.ds(0, devices, stride=SHARE), :] = jnp.dot(
        routes[...],
        jnp.concatenate(three_parts(blocks), axis=0),
        preferred_element_type=jnp.float32,
    )
    lanes = lax.broadcasted_iota(jnp.int32, TILE, 1)
    here = positions()
    own_place = (here[0] * sizes[1] + here[1]) * sizes[2] + here[2]
    paired = pltpu.roll(packed, CY - SHARE, 0)
    up = jnp.where(lanes % 2 == 0, packed, pltpu.roll(paired, 1, 1))[:SHARE]
    down = jnp.where(lanes % 2 == 1, packed, pltpu.roll(paired, CZ - 1, 1))[:SHARE]
    lanes = lax.broadcasted_iota(jnp.int32, (SHARE, CZ), 1)
    for step, message in ((1, up), (-1, down)):
        position = here[2] + step

        @pl.when((position >= 0) & (position < sizes[2]))
        def _():
            at = pl.ds(pl.multiple_of((own_place + step) * SHARE, SHARE), SHARE)
            rows_out[at, :] = jnp.where(lanes < BASE, rows_out[at, :], message)

    copy = pltpu.make_async_copy(rows_out, table, sent)
    copy.start()
    put_pair(x_low, x_high, here[0], outs[0])
    put_pair(y_low, y_high, here[1], outs[1])
    copy.wait()


def last_kernel(sizes, base, table, *refs):
    received, (out, gradient, done, block, sent) = split(refs, sizes, False, False)
    devices = table.shape[0] // SHARE
    here = positions()
    own_place = (here[0] * sizes[1] + here[1]) * sizes[2] + here[2]
    sublanes = lax.broadcasted_iota(jnp.int32, TILE, 0)
    lanes = lax.broadcasted_iota(jnp.int32, TILE, 1)

    def z_rows(step):
        inside = (here[2] + step >= 0) & (here[2] + step < sizes[2])
        place = jnp.where(inside, own_place + step, own_place)
        rows = table[pl.ds(pl.multiple_of(place * SHARE, SHARE), SHARE), :]
        return jnp.where(inside, jnp.concatenate([rows, rows], axis=0), 0.0)

    z_above, z_below = z_rows(1), z_rows(-1)
    first_half = sublanes < SHARE
    z_halo = jnp.where(
        lanes % 2 == 0,
        jnp.where(first_half, pltpu.roll(z_above, CZ - 1, 1), z_above),
        -jnp.where(first_half, pltpu.roll(z_below, 1, 1), z_below),
    )
    totals = [None] * 4
    for device in range(devices):
        part = table[device * SHARE : device * SHARE + 1, :]
        old = totals[device % 4]
        totals[device % 4] = part if old is None else old + part
    total = (totals[0] + totals[1]) + (totals[2] + totals[3])
    block[...] = total[:, : 5 * BOXES]
    copies = [pltpu.make_async_copy(block, gradient, sent.at[5])]
    copies[0].start()

    def send(component):
        copy = pltpu.make_async_copy(done.at[component], out.at[component], sent.at[component])
        copy.start()
        copies.append(copy)

    add_halo(base, received, two_thirds * step_length, sizes, done, send, z_halo)
    for copy in copies:
        copy.wait()


VMEM = pl.BlockSpec(memory_space=pltpu.VMEM)
SMEM = pl.BlockSpec(memory_space=pltpu.SMEM)
HBM = pl.BlockSpec(memory_space=pltpu.HBM)


def call(kernel, in_specs, operands, out_shapes, scratch=(), spaces=None, dtype=jnp.float32):
    spaces = spaces or [pltpu.VMEM] * len(out_shapes)
    operands = [
        pltpu.with_memory_space_constraint(operand, pltpu.HBM) if spec is HBM else operand
        for spec, operand in zip(in_specs, operands)
    ]
    return pl.pallas_call(
        kernel,
        out_shape=[space(shape, dtype) for space, shape in zip(spaces, out_shapes)],
        in_specs=in_specs,
        out_specs=[pl.BlockSpec(memory_space=space) for space in spaces],
        scratch_shapes=list(scratch),
        compiler_params=pltpu.CompilerParams(vmem_limit_bytes=16 * 1024 * 1024),
        cost_estimate=pl.CostEstimate(flops=2000000, bytes_accessed=1000000, transcendentals=0),
    )(*operands)


def body(
    terminal_adjoint,
    density,
    velocity,
    stiffness,
    sponge,
    source_shape,
    brick_level,
    brick_patch,
    patch_owner,
):
    sizes = tuple(lax.axis_size(axis) for axis in AXES)
    permutations = (
        pairings(sizes, 0, 1),
        pairings(sizes, 1, 1),
        pairings(sizes, 2, 1),
    )
    devices = patch_owner.shape[0]
    state_shape = terminal_adjoint.shape
    start = terminal_adjoint.reshape(STATE)
    density, stiffness, sponge, source = (
        array.reshape(FLAT) for array in (density, stiffness, sponge, source_shape)
    )
    velocity = velocity.reshape((3,) + FLAT)
    level = jnp.transpose(brick_level, (0, 2, 1))
    patches = jnp.transpose(brick_patch, (0, 2, 1))

    def message_shapes(fields, with_z=True):
        return [
            TILE if key[0] == 2 else (fields,) + TILE
            for key in message_keys(sizes, True, with_z)
        ]

    def exchange(messages, with_z=True):
        sends = dict(zip(message_keys(sizes, True, with_z), messages))
        sends[2, 1] = sends.get((2, 0))
        return [
            lax.ppermute(sends[key], AXES, permutations[key[0]][key[1]])
            for key in message_keys(sizes, False, with_z)
        ]

    scaled, *sent = call(
        functools.partial(first_kernel, sizes),
        [HBM] * 6,
        (level, start, density, velocity, stiffness, source),
        [(6,) + FLAT] + message_shapes(6),
        scratch=[
            pltpu.SMEM(level.shape, jnp.int32),
            pltpu.VMEM(STATE, jnp.float32),
            pltpu.VMEM(FLAT, jnp.float32),
            pltpu.VMEM((3,) + FLAT, jnp.float32),
            pltpu.VMEM(FLAT, jnp.float32),
            pltpu.VMEM(FLAT, jnp.float32),
            pltpu.SemaphoreType.DMA((6,)),
        ],
    )
    received_one = exchange(sent)
    routes, gather = call(
        functools.partial(target_kernel, sizes),
        [SMEM] * 2,
        (patches, patch_owner),
        [(devices, 3 * CY * CY), (7 * CZ, CZ)],
        dtype=jnp.bfloat16,
    )
    (base,) = call(
        functools.partial(own_kernel, (0.0, 1.0)), [VMEM] * 3, (scaled, sponge, start), [STATE]
    )
    operands = (base, scaled, *received_one)
    section, *sent = call(
        functools.partial(stage_kernel, sizes, step_length),
        [VMEM] * len(operands),
        operands,
        [STATE] + message_shapes(5),
    )
    received = exchange(sent)
    (base,) = call(
        functools.partial(own_kernel, (0.75, 0.25)),
        [VMEM] * 4,
        (scaled, sponge, start, section),
        [STATE],
    )
    operands = (source, scaled, sponge, start, *received_one)
    shapes, sums, faces = call(
        functools.partial(shape_kernel, sizes),
        [VMEM] * len(operands),
        operands,
        [(7,) + FLAT, (5,) + TILE, (6,) + TILE],
    )
    operands = (base, scaled, shapes, sums, faces, routes, gather, *received)
    section, table, *sent = call(
        functools.partial(gradient_kernel, sizes, 0.25 * step_length),
        [VMEM] * len(operands),
        operands,
        [STATE, (devices * SHARE, CZ)] + message_shapes(5, False),
        scratch=[pltpu.VMEM((devices * SHARE, CZ), jnp.float32), pltpu.SemaphoreType.DMA],
        spaces=[pltpu.VMEM, pltpu.HBM] + [pltpu.VMEM] * len(message_shapes(5, False)),
    )
    table = lax.all_to_all(table.reshape(devices, SHARE, CZ), AXES, 0, 0, tiled=True)
    received = exchange(sent, False)
    (base,) = call(
        functools.partial(own_kernel, (third, two_thirds)),
        [VMEM] * 4,
        (scaled, sponge, start, section),
        [STATE],
    )
    operands = (base, table.reshape(devices * SHARE, CZ), *received)
    adjoint, gradient = call(
        functools.partial(last_kernel, sizes),
        [VMEM] * len(operands),
        operands,
        [STATE, (1, 5 * BOXES)],
        scratch=[
            pltpu.VMEM(STATE, jnp.float32),
            pltpu.VMEM((1, 5 * BOXES), jnp.float32),
            pltpu.SemaphoreType.DMA((6,)),
        ],
        spaces=[pltpu.HBM] * 2,
    )
    return adjoint.reshape(state_shape), gradient


def solution(mesh):
    in_specs = (
        P(None, "gx", "gy", "gz"),
        P("gx", "gy", "gz"),
        P(None, "gx", "gy", "gz"),
        P("gx", "gy", "gz"),
        P("gx", "gy", "gz"),
        P("gx", "gy", "gz"),
        P(),
        P(),
        P(),
    )
    out_specs = (P(None, "gx", "gy", "gz"), P(("gx", "gy", "gz"), None))
    return jax.shard_map(body, mesh=mesh, in_specs=in_specs, out_specs=out_specs, check_vma=False)
```

```python
import functools

import jax
import jax.numpy as jnp
from jax import lax
from jax.experimental import pallas as pl
from jax.experimental.pallas import tpu as pltpu
from jax.sharding import PartitionSpec as P

CX = 8
CY = 8
CZ = 128
BZ = 16
BOXES = CZ // BZ
ROWS = CX * CY

AXES = ("gx", "gy", "gz")

step_length = 0.14
third = 1.0 / 3.0
two_thirds = 2.0 / 3.0

BASE = 5 * BOXES
SHARE = CY // 2

TILE = (CY, CZ)
FLAT = (ROWS, CZ)
STATE = (5,) + FLAT


def pairings(sizes, axis, near_axis):
    size = sizes[axis]
    first, second = [], []
    for x in range(sizes[0]):
        for y in range(sizes[1]):
            for z in range(sizes[2]):
                here = [x, y, z]
                index = (x * sizes[1] + y) * sizes[2] + z
                place = here[axis]
                other = list(here)
                other[axis] = place ^ 1
                first.append((index, (other[0] * sizes[1] + other[1]) * sizes[2] + other[2]))
                other = list(here)
                if 0 < place < size - 1 or near_axis == axis:
                    other[axis] = (place + (1 if place % 2 else -1)) % size
                else:
                    other[near_axis] = here[near_axis] ^ 1
                second.append((index, (other[0] * sizes[1] + other[1]) * sizes[2] + other[2]))
    return first, second if size > 2 else None


def positions():
    return [lax.axis_index(axis) for axis in AXES]


def tile_at(x):
    return slice(x * CY, (x + 1) * CY)


def row_at(y):
    return pl.ds(y, CX, stride=CY)


def partials_of(adjoint, speed, density, stiffness, inverse, direction):
    components = [speed * component for component in adjoint]
    row = 1 + direction
    components[row] = components[row] + (density * adjoint[0] + stiffness * adjoint[4])
    components[4] = components[4] + adjoint[row] * inverse
    return components


def faces_at(state, scaled, rows, direction):
    adjoint = [state[component, rows, :] for component in range(5)]
    return partials_of(
        adjoint,
        scaled[direction, rows, :],
        scaled[3, rows, :],
        scaled[4, rows, :],
        scaled[5, rows, :],
        direction,
    )


def pack_lanes(fields):
    lanes = (lax.broadcasted_iota(jnp.int32, TILE, 1) + (CZ - BASE)) % CZ // 2
    tiles = []
    for index, field in enumerate(fields):
        for x in range(CX):
            k = index * CX + x
            tiles.append(pltpu.roll(field[x], (BASE + 2 * k + 1) % CZ, 1))
    bit = 1
    while len(tiles) > 1:
        upper = (lanes & bit) != 0
        pairs = [
            jnp.where(upper, tiles[at + 1], tiles[at]) if at + 1 < len(tiles) else tiles[at]
            for at in range(0, len(tiles), 2)
        ]
        tiles, bit = pairs, 2 * bit
    return tiles[0]


def put_pair(low, high, position, outs):
    even = position % 2 == 0
    for index, (below, above) in enumerate(zip(low, high)):
        outs[0][index] = jnp.where(even, above, below)
        if outs[1] is not None:
            outs[1][index] = jnp.where(even, below, above)


def outer_faces(state, scaled):
    x_low = faces_at(state, scaled, tile_at(0), 0)
    x_high = faces_at(state, scaled, tile_at(CX - 1), 0)
    y_low = faces_at(state, scaled, row_at(0), 1)
    y_high = faces_at(state, scaled, row_at(CY - 1), 1)
    z_tiles = [faces_at(state, scaled, tile_at(x), 2) for x in range(CX)]
    z_fields = [[z_tiles[x][component] for x in range(CX)] for component in range(5)]
    return x_low, x_high, y_low, y_high, z_fields


def put_messages(state, scaled, source, outs):
    here = positions()
    x_low, x_high, y_low, y_high, z_fields = outer_faces(state, scaled)
    if source is not None:
        x_low.append(source[tile_at(0), :])
        x_high.append(source[tile_at(CX - 1), :])
        y_low.append(source[row_at(0), :])
        y_high.append(source[row_at(CY - 1), :])
        z_fields.append([source[tile_at(x), :] for x in range(CX)])
    outs[2][0][0] = pack_lanes(z_fields)
    for index in range(1, outs[2][0].shape[0]):
        outs[2][0][index] = jnp.zeros(TILE, jnp.float32)
    put_pair(x_low, x_high, here[0], outs[0])
    put_pair(y_low, y_high, here[1], outs[1])


def sort_pair(first, second, position, size):
    even = position % 2 == 0
    zero = jnp.zeros_like(first)
    if second is None:
        return jnp.where(even, zero, first), jnp.where(even, first, zero)
    below = jnp.where(position == 0, zero, jnp.where(even, second, first))
    above = jnp.where(position == size - 1, zero, jnp.where(even, first, second))
    return below, above


def sorted_field(refs, index, position, size):
    first, second = refs
    return sort_pair(first[index], None if second is None else second[index], position, size)


def sorted_lanes(refs, position, size):
    return sorted_field(refs, 0, position, size)


def add_halo(base, received, weight, sizes, out, finish=None, z_halo=None):
    here = positions()
    lanes = lax.broadcasted_iota(jnp.int32, TILE, 1)
    edges = (lanes == 0) | (lanes == CZ - 1)
    if z_halo is None:
        z_below, z_above = sorted_lanes(received[2], here[2], sizes[2])
        z_halo = jnp.where(
            lanes % 2 == 0, pltpu.roll(z_above, CZ - 1, 1), -pltpu.roll(z_below, 1, 1)
        )
    z_halo = weight * z_halo
    for component in range(5):
        x_below, x_above = sorted_field(received[0], component, here[0], sizes[0])
        y_below, y_above = sorted_field(received[1], component, here[1], sizes[1])
        for x in range(CX):
            k = component * CX + x
            value = base[component, tile_at(x), :]
            value = value + jnp.where(edges, pltpu.roll(z_halo, (CZ - 1 - BASE - 2 * k) % CZ, 1), 0.0)
            if x == 0:
                value = value - weight * x_below
            if x == CX - 1:
                value = value + weight * x_above
            out[component, tile_at(x), :] = value
        out[component, row_at(0), :] = out[component, row_at(0), :] - weight * y_below
        out[component, row_at(CY - 1), :] = out[component, row_at(CY - 1), :] + weight * y_above
        if finish is not None:
            finish(component)


ORDERS = (
    ((1, 0), (0, 1), (0, 0), (1, 1), (2, 0), (2, 1)),
    ((1, 0), (0, 1), (0, 0), (1, 1)),
    ((1, 0), (0, 1), (0, 0), (1, 1)),
)


def message_keys(sizes, sent, stage):
    keys = [key for key in ORDERS[stage] if key[1] == 0 or sizes[key[0]] > 2]
    return [key for key in keys if not (sent and key == (2, 1))]


def split(refs, sizes, stage, sent=False):
    refs, out = list(refs), [[None, None] for axis in range(3)]
    for axis, which in message_keys(sizes, sent, stage):
        out[axis][which] = refs.pop(0)
    return out, refs


def first_kernel(
    sizes, level, adjoint, density, velocity, stiffness, sponge, source, scaled, base, *refs
):
    outs, scratch = split(refs, sizes, 0, True)
    *targets, arrived = scratch
    level_now, adjoint_now, density_now, velocity_now, stiffness_now, sponge_now, source_now = targets
    copies = [
        pltpu.make_async_copy(there, here, arrived.at[index])
        for index, (there, here) in enumerate(
            zip((level, adjoint, density, velocity, stiffness, sponge, source), targets)
        )
    ]
    for copy in copies:
        copy.start()
    for copy in copies:
        copy.wait()
    here = positions()
    own_level = level_now[here[0], here[2], here[1]]
    half_inverse = 0.5 * lax.shift_left(jnp.int32(1), own_level).astype(jnp.float32)
    for direction in range(3):
        scaled[direction] = half_inverse * velocity_now[direction]
    scaled[3] = half_inverse * density_now[...]
    scaled[4] = half_inverse * stiffness_now[...]
    scaled[5] = half_inverse / density_now[...]
    tiles = own_part((0.0, 1.0), scaled, sponge_now, None, adjoint_now, base)
    x_low = tiles[0][0] + [source_now[tile_at(0), :]]
    x_high = tiles[CX - 1][0] + [source_now[tile_at(CX - 1), :]]
    y_low = faces_at(adjoint_now, scaled, row_at(0), 1) + [source_now[row_at(0), :]]
    y_high = faces_at(adjoint_now, scaled, row_at(CY - 1), 1) + [source_now[row_at(CY - 1), :]]
    put_pair(x_low, x_high, here[0], outs[0])
    put_pair(y_low, y_high, here[1], outs[1])
    along = [
        [[tiles[x][direction][component] for x in range(CX)] for component in range(5)]
        for direction in range(3)
    ]
    along[2].append([source_now[tile_at(x), :] for x in range(CX)])
    for index, fields in enumerate(
        (
            along[2],
            [[base[component, tile_at(x), :] for x in range(CX)] for component in range(5)],
            along[0],
            along[1],
            [[scaled[row, tile_at(x), :] for x in range(CX)] for row in range(2, 6)],
        )
    ):
        outs[2][0][index] = pack_lanes(fields)
    outs[2][0][5] = jnp.zeros(TILE, jnp.float32)


def own_kernel(weights, scaled, sponge, start, state, out):
    own_part(weights, scaled, sponge, start, state, out)


def own_part(weights, scaled, sponge, start, state, out):
    keep, blend = weights
    rows = lax.broadcasted_iota(jnp.int32, TILE, 0)
    lanes = lax.broadcasted_iota(jnp.int32, TILE, 1)
    tiles = [
        [faces_at(state, scaled, tile_at(x), direction) for direction in range(3)]
        for x in range(CX)
    ]
    for x in range(CX):
        damp = sponge[tile_at(x), :]
        for component in range(5):
            total = None
            if x < CX - 1:
                total = tiles[x + 1][0][component]
            if x > 0:
                before = tiles[x - 1][0][component]
                total = -before if total is None else total - before
            part = tiles[x][1][component]
            total = total + jnp.where(rows == CY - 1, 0.0, pltpu.roll(part, CY - 1, 0))
            total = total - jnp.where(rows == 0, 0.0, pltpu.roll(part, 1, 0))
            part = tiles[x][2][component]
            total = total + jnp.where(lanes == CZ - 1, 0.0, pltpu.roll(part, CZ - 1, 1))
            total = total - jnp.where(lanes == 0, 0.0, pltpu.roll(part, 1, 1))
            value = state[component, tile_at(x), :]
            value = blend * (value + step_length * (total - damp * value))
            if keep:
                value = value + keep * start[component, tile_at(x), :]
            out[component, tile_at(x), :] = value
    return tiles


def shape_kernel(sizes, source, scaled, sponge, start, *refs):
    sources, (shapes, sums, faces) = split(refs, sizes, 0)
    rows = lax.broadcasted_iota(jnp.int32, TILE, 0)
    lanes = lax.broadcasted_iota(jnp.int32, TILE, 1)
    outer = step_length * two_thirds
    inner = outer * step_length
    totals = [None] * 5
    for x in range(CX):
        at = tile_at(x)
        shape = source[at, :]
        along_x = jnp.zeros(TILE, jnp.float32)
        if x > 0:
            along_x = along_x + source[tile_at(x - 1), :]
        if x < CX - 1:
            along_x = along_x - source[tile_at(x + 1), :]
        along_y = jnp.where(rows == 0, 0.0, pltpu.roll(shape, 1, 0)) - jnp.where(
            rows == CY - 1, 0.0, pltpu.roll(shape, CY - 1, 0)
        )
        before = inner * jnp.where(lanes == 0, 0.0, pltpu.roll(shape, 1, 1))
        after = inner * jnp.where(lanes == CZ - 1, 0.0, pltpu.roll(shape, CZ - 1, 1))
        along_x, along_y = inner * along_x, inner * along_y
        own = outer * shape * (1.0 - step_length * sponge[at, :])
        own = own + scaled[0, at, :] * along_x + scaled[1, at, :] * along_y
        for index, value in enumerate(
            (own, scaled[2, at, :] * before, scaled[2, at, :] * after, along_x, along_y, before, after)
        ):
            shapes[index, at, :] = value
        weighted = (step_length * third) * shape
        for component in range(5):
            value = weighted * start[component, at, :]
            totals[component] = value if totals[component] is None else totals[component] + value
    for component in range(5):
        sums[component] = totals[component]
    here = positions()
    x_below, x_above = sorted_field(sources[0], 5, here[0], sizes[0])
    y_below, y_above = sorted_field(sources[1], 5, here[1], sizes[1])
    z_below, z_above = sorted_lanes(sources[2], here[2], sizes[2])
    aligned_above = jnp.zeros(TILE, jnp.float32)
    aligned_below = jnp.zeros(TILE, jnp.float32)
    for component in range(5):
        group = (lanes >= BASE) & ((lanes - BASE) // (2 * CX) == component)
        shift = 2 * CX * (component - 5)
        aligned_above = jnp.where(
            group & (lanes % 2 == 0), pltpu.roll(z_above, (shift - 1) % CZ, 1), aligned_above
        )
        aligned_below = jnp.where(
            group & (lanes % 2 == 1), pltpu.roll(z_below, (shift + 1) % CZ, 1), aligned_below
        )
    for index, (sign, face) in enumerate(
        (
            (-inner, x_above),
            (inner, x_below),
            (-inner, y_above),
            (inner, y_below),
            (-inner, aligned_above),
            (inner, aligned_below),
        )
    ):
        faces[index] = sign * face


def stage_kernel(sizes, weight, base, scaled, *refs):
    received, (section, *outs) = split(refs, sizes, 0)
    add_halo(base, received, weight, sizes, section)
    outs = split(outs, sizes, 1, True)[0]
    here = positions()
    x_low, x_high, y_low, y_high, z_fields = outer_faces(section, scaled)
    lanes = lax.broadcasted_iota(jnp.int32, TILE, 1)
    rows = lax.broadcasted_iota(jnp.int32, TILE, 0)
    place = (lanes + (CZ - BASE)) % CZ // 2 % CX
    x_below, x_above = sorted_field(received[2], 2, here[2], sizes[2])
    y_below, y_above = sorted_field(received[2], 3, here[2], sizes[2])
    far = 2 * (CX - 1)
    x_high.append(jnp.where(place == 0, both_layers(x_below, x_above, -far), 0.0))
    x_low.append(jnp.where(place == CX - 1, both_layers(x_below, x_above, far), 0.0))
    y_layers = both_layers(y_below, y_above, 0)
    y_high.append(jnp.where(rows == 0, pltpu.roll(y_layers, 1, 0), 0.0))
    y_low.append(jnp.where(rows == CY - 1, pltpu.roll(y_layers, CY - 1, 0), 0.0))
    put_pair(x_low, x_high, here[0], outs[0])
    put_pair(y_low, y_high, here[1], outs[1])


def both_layers(below, above, shift):
    lanes = lax.broadcasted_iota(jnp.int32, TILE, 1)
    return jnp.where(
        lanes % 2 == 0,
        pltpu.roll(above, (shift - 1) % CZ, 1),
        pltpu.roll(below, (shift + 1) % CZ, 1),
    )


def layer_partials(state, layer):
    group = 2 * CX
    return (
        layer[0] * state
        + layer[1] * pltpu.roll(state, 3 * group, 1)
        + layer[2] * pltpu.roll(state, CZ - group, 1)
        + layer[3] * pltpu.roll(state, group, 1)
    )


def layer_kernel(sizes, own, *refs):
    received, (layer, known) = split(refs, sizes, 0)
    here = positions()
    lanes = lax.broadcasted_iota(jnp.int32, TILE, 1)
    even = lanes % 2 == 0
    inside = (lanes >= BASE) & (lanes < BASE + 5 * 2 * CX)
    group = (lanes - BASE) // (2 * CX)
    below, above = sorted_field(received[2], 4, here[2], sizes[2])
    packed = jnp.where(even, 1.0, -1.0) * both_layers(below, above, 0)
    speed = jnp.zeros(TILE, jnp.float32)
    for component in range(5):
        speed = jnp.where(group == component, pltpu.roll(packed, 2 * CX * component, 1), speed)
    layer[0] = jnp.where(inside, speed, 0.0)
    layer[1] = jnp.where(inside & (group == 3), pltpu.roll(packed, 2 * CX * 2, 1), 0.0)
    layer[2] = jnp.where(inside & (group == 3), pltpu.roll(packed, 2 * CX, 1), 0.0)
    layer[3] = jnp.where(inside & (group == 4), pltpu.roll(packed, 2 * CX, 1), 0.0)
    below, above = sorted_field(received[2], 1, here[2], sizes[2])
    state = both_layers(below, above, 0)
    state = state + step_length * jnp.where(even, -own[0], own[0])
    known[...] = layer_partials(jnp.where(inside, state, 0.0), layer)


def sublane_total(tile):
    for shift in (4, 2, 1):
        tile = tile + pltpu.roll(tile, shift, 0)
    return tile


def three_parts(value):
    parts = []
    for _ in range(3):
        part = value.astype(jnp.bfloat16)
        parts.append(part)
        value = value - part.astype(jnp.float32)
    return parts


def product(value, matrix):
    count = value.shape[0]
    stacked = jnp.concatenate(three_parts(value), axis=0)
    result = jnp.dot(stacked, matrix, preferred_element_type=jnp.float32)
    return result[:count] + result[count : 2 * count] + result[2 * count :]


def target_kernel(sizes, patches, owners, routes, gather):
    here = positions()
    shape = routes.shape
    rows = lax.broadcasted_iota(jnp.int32, shape, 0)
    lanes = lax.broadcasted_iota(jnp.int32, shape, 1) % (CY * CY)
    chosen = jnp.zeros(shape, jnp.bool_)
    for index, offset in enumerate(OFFSETS):
        place = [
            jnp.clip(here[axis] + offset[axis], 0, sizes[axis] - 1) for axis in range(3)
        ]
        target = owners[patches[place[0], place[2], place[1]]]
        chosen = chosen | ((lanes // CY == index) & (rows == target))
    routes[...] = jnp.where(chosen, 1.0, 0.0).astype(jnp.bfloat16)
    rows = lax.broadcasted_iota(jnp.int32, (CZ, CZ), 0)
    lanes = lax.broadcasted_iota(jnp.int32, (CZ, CZ), 1)
    for component in range(5):
        ones = lanes == BOXES * component + rows // BZ
        gather[component * CZ : (component + 1) * CZ, :] = jnp.where(ones, 1.0, 0.0).astype(
            jnp.bfloat16
        )
    for index, box in enumerate((0, BOXES - 1)):
        ones = (lanes == BOXES * ((rows - BASE) // (2 * CX)) + box) & (rows >= BASE)
        ones = ones & (rows < BASE + 5 * 2 * CX)
        start = (5 + index) * CZ
        gather[start : start + CZ, :] = jnp.where(ones, 1.0, 0.0).astype(jnp.bfloat16)


OFFSETS = (
    (0, 0, 0),
    (1, 0, 0),
    (-1, 0, 0),
    (0, 1, 0),
    (0, -1, 0),
    (0, 0, 1),
    (0, 0, -1),
)


def gradient_kernel(
    sizes, weight, base, scaled, shapes, sums, faces, routes, gather, layer, known, *refs
):
    received, (section, table, *rest) = split(refs, sizes, 1)
    outs, (rows_out, sent) = split(rest, sizes, 2, True)
    here = positions()
    x_below, x_above = sorted_field(received[0], 5, here[0], sizes[0])
    y_below, y_above = sorted_field(received[1], 5, here[1], sizes[1])
    late = step_length * ((x_above - x_below) + (y_above - y_below))
    z_halo = known[...] + layer_partials(late, layer)
    add_halo(base, received, weight, sizes, section, z_halo=z_halo)
    x_low, x_high, y_low, y_high, z_fields = outer_faces(section, scaled)
    packed = pack_lanes(z_fields)
    main = [sums[component] for component in range(5)]
    before = [None] * 5
    after = [None] * 5

    def accumulate(totals, component, value):
        old = totals[component]
        totals[component] = value if old is None else old + value

    for x in range(CX):
        at = tile_at(x)
        state = [section[component, at, :] for component in range(5)]
        own, lane_before, lane_after, along_x, along_y, shape_before, shape_after = (
            shapes[index, at, :] for index in range(7)
        )
        push = scaled[3, at, :] * state[0] + scaled[4, at, :] * state[4]
        drawn = [scaled[5, at, :] * state[1 + direction] for direction in range(3)]
        for component in range(5):
            accumulate(main, component, own * state[component])
            accumulate(before, component, lane_before * state[component])
            accumulate(after, component, lane_after * state[component])
        accumulate(main, 1, along_x * push)
        accumulate(main, 2, along_y * push)
        accumulate(before, 3, shape_before * push)
        accumulate(after, 3, shape_after * push)
        accumulate(main, 4, along_x * drawn[0] + along_y * drawn[1])
        accumulate(before, 4, shape_before * drawn[2])
        accumulate(after, 4, shape_after * drawn[2])
    columns = []
    for f in range(5):
        own = main[f] + pltpu.roll(before[f], CZ - 1, 1) - pltpu.roll(after[f], 1, 1)
        columns.append(
            jnp.concatenate(
                [own, faces[0] * x_high[f], faces[1] * x_low[f], faces[2] * y_high[f], faces[3] * y_low[f]],
                axis=0,
            )
        )
    blocks = product(jnp.concatenate(columns, axis=1), gather[: 5 * CZ, :])
    above = product(faces[4] * packed, gather[5 * CZ : 6 * CZ, :])
    below = product(faces[5] * packed, gather[6 * CZ :, :])
    blocks = jnp.concatenate([blocks, above, below, jnp.zeros(TILE, jnp.float32)], axis=0)
    devices = routes.shape[0]
    rows_out[pl.ds(0, devices, stride=SHARE), :] = jnp.dot(
        routes[...],
        jnp.concatenate(three_parts(blocks), axis=0),
        preferred_element_type=jnp.float32,
    )
    lanes = lax.broadcasted_iota(jnp.int32, TILE, 1)
    own_place = (here[0] * sizes[1] + here[1]) * sizes[2] + here[2]
    paired = pltpu.roll(packed, CY - SHARE, 0)
    up = jnp.where(lanes % 2 == 0, packed, pltpu.roll(paired, 1, 1))[:SHARE]
    down = jnp.where(lanes % 2 == 1, packed, pltpu.roll(paired, CZ - 1, 1))[:SHARE]
    lanes = lax.broadcasted_iota(jnp.int32, (SHARE, CZ), 1)
    for step, message in ((1, up), (-1, down)):
        position = here[2] + step

        @pl.when((position >= 0) & (position < sizes[2]))
        def _():
            at = pl.ds(pl.multiple_of((own_place + step) * SHARE, SHARE), SHARE)
            rows_out[at, :] = jnp.where(lanes < BASE, rows_out[at, :], message)

    copy = pltpu.make_async_copy(rows_out, table, sent)
    copy.start()
    put_pair(x_low, x_high, here[0], outs[0])
    put_pair(y_low, y_high, here[1], outs[1])
    copy.wait()


def last_kernel(sizes, base, table, *refs):
    received, (out, gradient, done, block, sent) = split(refs, sizes, 2)
    devices = table.shape[0] // SHARE
    here = positions()
    own_place = (here[0] * sizes[1] + here[1]) * sizes[2] + here[2]
    sublanes = lax.broadcasted_iota(jnp.int32, TILE, 0)
    lanes = lax.broadcasted_iota(jnp.int32, TILE, 1)

    def z_rows(step):
        inside = (here[2] + step >= 0) & (here[2] + step < sizes[2])
        place = jnp.where(inside, own_place + step, own_place)
        rows = table[pl.ds(pl.multiple_of(place * SHARE, SHARE), SHARE), :]
        return jnp.where(inside, jnp.concatenate([rows, rows], axis=0), 0.0)

    z_above, z_below = z_rows(1), z_rows(-1)
    first_half = sublanes < SHARE
    z_halo = jnp.where(
        lanes % 2 == 0,
        jnp.where(first_half, pltpu.roll(z_above, CZ - 1, 1), z_above),
        -jnp.where(first_half, pltpu.roll(z_below, 1, 1), z_below),
    )
    totals = [None] * 4
    for device in range(devices):
        part = table[device * SHARE : device * SHARE + 1, :]
        old = totals[device % 4]
        totals[device % 4] = part if old is None else old + part
    total = (totals[0] + totals[1]) + (totals[2] + totals[3])
    block[...] = total[:, : 5 * BOXES]
    copies = [pltpu.make_async_copy(block, gradient, sent.at[5])]
    copies[0].start()

    def send(component):
        copy = pltpu.make_async_copy(done.at[component], out.at[component], sent.at[component])
        copy.start()
        copies.append(copy)

    add_halo(base, received, two_thirds * step_length, sizes, done, send, z_halo)
    for copy in copies:
        copy.wait()


VMEM = pl.BlockSpec(memory_space=pltpu.VMEM)
SMEM = pl.BlockSpec(memory_space=pltpu.SMEM)
HBM = pl.BlockSpec(memory_space=pltpu.HBM)


def call(kernel, in_specs, operands, out_shapes, scratch=(), spaces=None, dtype=jnp.float32):
    spaces = spaces or [pltpu.VMEM] * len(out_shapes)
    operands = [
        pltpu.with_memory_space_constraint(operand, pltpu.HBM) if spec is HBM else operand
        for spec, operand in zip(in_specs, operands)
    ]
    return pl.pallas_call(
        kernel,
        out_shape=[space(shape, dtype) for space, shape in zip(spaces, out_shapes)],
        in_specs=in_specs,
        out_specs=[pl.BlockSpec(memory_space=space) for space in spaces],
        scratch_shapes=list(scratch),
        compiler_params=pltpu.CompilerParams(vmem_limit_bytes=16 * 1024 * 1024),
        cost_estimate=pl.CostEstimate(flops=2000000, bytes_accessed=1000000, transcendentals=0),
    )(*operands)


def body(
    terminal_adjoint,
    density,
    velocity,
    stiffness,
    sponge,
    source_shape,
    brick_level,
    brick_patch,
    patch_owner,
):
    sizes = tuple(lax.axis_size(axis) for axis in AXES)
    permutations = (
        pairings(sizes, 0, 1),
        pairings(sizes, 1, 1),
        pairings(sizes, 2, 1),
    )
    devices = patch_owner.shape[0]
    state_shape = terminal_adjoint.shape
    start = terminal_adjoint.reshape(STATE)
    density, stiffness, sponge, source = (
        array.reshape(FLAT) for array in (density, stiffness, sponge, source_shape)
    )
    velocity = velocity.reshape((3,) + FLAT)
    level = jnp.transpose(brick_level, (0, 2, 1))
    patches = jnp.transpose(brick_patch, (0, 2, 1))

    def message_shapes(fields, stage):
        return [
            (fields,) + TILE for key in message_keys(sizes, True, stage)
        ]

    def exchange(messages, stage):
        sends = dict(zip(message_keys(sizes, True, stage), messages))
        sends[2, 1] = sends.get((2, 0))
        return [
            lax.ppermute(sends[key], AXES, permutations[key[0]][key[1]])
            for key in message_keys(sizes, False, stage)
        ]

    flat = pltpu.VMEM(FLAT, jnp.float32)
    state = pltpu.VMEM(STATE, jnp.float32)
    scaled, base, *sent = call(
        functools.partial(first_kernel, sizes),
        [HBM] * 7,
        (level, start, density, velocity, stiffness, sponge, source),
        [(6,) + FLAT, STATE] + message_shapes(6, 0),
        scratch=[
            pltpu.SMEM(level.shape, jnp.int32),
            state,
            flat,
            pltpu.VMEM((3,) + FLAT, jnp.float32),
            flat,
            flat,
            flat,
            pltpu.SemaphoreType.DMA((7,)),
        ],
    )
    received_one = exchange(sent, 0)
    own_layers = dict(zip(message_keys(sizes, True, 0), sent))[2, 0]
    routes, gather = call(
        functools.partial(target_kernel, sizes),
        [SMEM] * 2,
        (patches, patch_owner),
        [(devices, 3 * CY * CY), (7 * CZ, CZ)],
        dtype=jnp.bfloat16,
    )
    operands = (base, scaled, *received_one)
    section, *sent = call(
        functools.partial(stage_kernel, sizes, step_length),
        [VMEM] * len(operands),
        operands,
        [STATE] + message_shapes(6, 1),
    )
    received = exchange(sent, 1)
    operands = (own_layers, *received_one)
    layer, known = call(
        functools.partial(layer_kernel, sizes),
        [VMEM] * len(operands),
        operands,
        [(4,) + TILE, TILE],
    )
    (base,) = call(
        functools.partial(own_kernel, (0.75, 0.25)),
        [VMEM] * 4,
        (scaled, sponge, start, section),
        [STATE],
    )
    operands = (source, scaled, sponge, start, *received_one)
    shapes, sums, faces = call(
        functools.partial(shape_kernel, sizes),
        [VMEM] * len(operands),
        operands,
        [(7,) + FLAT, (5,) + TILE, (6,) + TILE],
    )
    operands = (base, scaled, shapes, sums, faces, routes, gather, layer, known, *received)
    section, table, *sent = call(
        functools.partial(gradient_kernel, sizes, 0.25 * step_length),
        [VMEM] * len(operands),
        operands,
        [STATE, (devices * SHARE, CZ)] + message_shapes(5, 2),
        scratch=[pltpu.VMEM((devices * SHARE, CZ), jnp.float32), pltpu.SemaphoreType.DMA],
        spaces=[pltpu.VMEM, pltpu.HBM] + [pltpu.VMEM] * len(message_shapes(5, 2)),
    )
    table = lax.all_to_all(table.reshape(devices, SHARE, CZ), AXES, 0, 0, tiled=True)
    received = exchange(sent, 2)
    (base,) = call(
        functools.partial(own_kernel, (third, two_thirds)),
        [VMEM] * 4,
        (scaled, sponge, start, section),
        [STATE],
    )
    operands = (base, table.reshape(devices * SHARE, CZ), *received)
    adjoint, gradient = call(
        functools.partial(last_kernel, sizes),
        [VMEM] * len(operands),
        operands,
        [STATE, (1, 5 * BOXES)],
        scratch=[
            pltpu.VMEM(STATE, jnp.float32),
            pltpu.VMEM((1, 5 * BOXES), jnp.float32),
            pltpu.SemaphoreType.DMA((6,)),
        ],
        spaces=[pltpu.HBM] * 2,
    )
    return adjoint.reshape(state_shape), gradient


def solution(mesh):
    in_specs = (
        P(None, "gx", "gy", "gz"),
        P("gx", "gy", "gz"),
        P(None, "gx", "gy", "gz"),
        P("gx", "gy", "gz"),
        P("gx", "gy", "gz"),
        P("gx", "gy", "gz"),
        P(),
        P(),
        P(),
    )
    out_specs = (P(None, "gx", "gy", "gz"), P(("gx", "gy", "gz"), None))
    return jax.shard_map(body, mesh=mesh, in_specs=in_specs, out_specs=out_specs, check_vma=False)
```

```python
import functools

import jax
import jax.numpy as jnp
from jax import lax
from jax.experimental import pallas as pl
from jax.experimental.pallas import tpu as pltpu
from jax.sharding import PartitionSpec as P

CX = 8
CY = 8
CZ = 128
BZ = 16
BOXES = CZ // BZ
ROWS = CX * CY

AXES = ("gx", "gy", "gz")

step_length = 0.14
third = 1.0 / 3.0
two_thirds = 2.0 / 3.0

BASE = 5 * BOXES

TILE = (CY, CZ)
FLAT = (ROWS, CZ)
STATE = (5,) + FLAT


def pairings(sizes, axis, near_axis):
    size = sizes[axis]
    first, second = [], []
    for x in range(sizes[0]):
        for y in range(sizes[1]):
            for z in range(sizes[2]):
                here = [x, y, z]
                index = (x * sizes[1] + y) * sizes[2] + z
                place = here[axis]
                other = list(here)
                other[axis] = place ^ 1
                first.append((index, (other[0] * sizes[1] + other[1]) * sizes[2] + other[2]))
                other = list(here)
                if 0 < place < size - 1 or near_axis == axis:
                    other[axis] = (place + (1 if place % 2 else -1)) % size
                else:
                    other[near_axis] = here[near_axis] ^ 1
                second.append((index, (other[0] * sizes[1] + other[1]) * sizes[2] + other[2]))
    return first, second if size > 2 else None


def positions():
    return [lax.axis_index(axis) for axis in AXES]


def tile_at(x):
    return slice(x * CY, (x + 1) * CY)


def row_at(y):
    return pl.ds(y, CX, stride=CY)


def partials_of(adjoint, speed, density, stiffness, inverse, direction):
    components = [speed * component for component in adjoint]
    row = 1 + direction
    components[row] = components[row] + (density * adjoint[0] + stiffness * adjoint[4])
    components[4] = components[4] + adjoint[row] * inverse
    return components


def faces_at(state, scaled, rows, direction):
    adjoint = [state[component, rows, :] for component in range(5)]
    return partials_of(
        adjoint,
        scaled[direction, rows, :],
        scaled[3, rows, :],
        scaled[4, rows, :],
        scaled[5, rows, :],
        direction,
    )


def pack_lanes(fields):
    lanes = (lax.broadcasted_iota(jnp.int32, TILE, 1) + (CZ - BASE)) % CZ // 2
    tiles = []
    for index, field in enumerate(fields):
        for x in range(CX):
            k = index * CX + x
            tiles.append(pltpu.roll(field[x], (BASE + 2 * k + 1) % CZ, 1))
    bit = 1
    while len(tiles) > 1:
        upper = (lanes & bit) != 0
        pairs = [
            jnp.where(upper, tiles[at + 1], tiles[at]) if at + 1 < len(tiles) else tiles[at]
            for at in range(0, len(tiles), 2)
        ]
        tiles, bit = pairs, 2 * bit
    return tiles[0]


def put_pair(low, high, position, outs):
    even = position % 2 == 0
    for index, (below, above) in enumerate(zip(low, high)):
        outs[0][index] = jnp.where(even, above, below)
        if outs[1] is not None:
            outs[1][index] = jnp.where(even, below, above)


def outer_faces(state, scaled):
    x_low = faces_at(state, scaled, tile_at(0), 0)
    x_high = faces_at(state, scaled, tile_at(CX - 1), 0)
    y_low = faces_at(state, scaled, row_at(0), 1)
    y_high = faces_at(state, scaled, row_at(CY - 1), 1)
    z_tiles = [faces_at(state, scaled, tile_at(x), 2) for x in range(CX)]
    z_fields = [[z_tiles[x][component] for x in range(CX)] for component in range(5)]
    return x_low, x_high, y_low, y_high, z_fields


def put_messages(state, scaled, source, outs):
    here = positions()
    x_low, x_high, y_low, y_high, z_fields = outer_faces(state, scaled)
    if source is not None:
        x_low.append(source[tile_at(0), :])
        x_high.append(source[tile_at(CX - 1), :])
        y_low.append(source[row_at(0), :])
        y_high.append(source[row_at(CY - 1), :])
        z_fields.append([source[tile_at(x), :] for x in range(CX)])
    outs[2][0][0] = pack_lanes(z_fields)
    for index in range(1, outs[2][0].shape[0]):
        outs[2][0][index] = jnp.zeros(TILE, jnp.float32)
    put_pair(x_low, x_high, here[0], outs[0])
    put_pair(y_low, y_high, here[1], outs[1])


def sort_pair(first, second, position, size):
    even = position % 2 == 0
    zero = jnp.zeros_like(first)
    if second is None:
        return jnp.where(even, zero, first), jnp.where(even, first, zero)
    below = jnp.where(position == 0, zero, jnp.where(even, second, first))
    above = jnp.where(position == size - 1, zero, jnp.where(even, first, second))
    return below, above


def sorted_field(refs, index, position, size):
    first, second = refs
    return sort_pair(first[index], None if second is None else second[index], position, size)


def sorted_lanes(refs, position, size):
    return sorted_field(refs, 0, position, size)


def add_halo(base, received, weight, sizes, out, finish=None, z_halo=None):
    here = positions()
    lanes = lax.broadcasted_iota(jnp.int32, TILE, 1)
    edges = (lanes == 0) | (lanes == CZ - 1)
    if z_halo is None:
        z_below, z_above = sorted_lanes(received[2], here[2], sizes[2])
        z_halo = jnp.where(
            lanes % 2 == 0, pltpu.roll(z_above, CZ - 1, 1), -pltpu.roll(z_below, 1, 1)
        )
    z_halo = weight * z_halo
    for component in range(5):
        x_below, x_above = sorted_field(received[0], component, here[0], sizes[0])
        y_below, y_above = sorted_field(received[1], component, here[1], sizes[1])
        for x in range(CX):
            k = component * CX + x
            value = base[component, tile_at(x), :]
            value = value + jnp.where(edges, pltpu.roll(z_halo, (CZ - 1 - BASE - 2 * k) % CZ, 1), 0.0)
            if x == 0:
                value = value - weight * x_below
            if x == CX - 1:
                value = value + weight * x_above
            out[component, tile_at(x), :] = value
        out[component, row_at(0), :] = out[component, row_at(0), :] - weight * y_below
        out[component, row_at(CY - 1), :] = out[component, row_at(CY - 1), :] + weight * y_above
        if finish is not None:
            finish(component)


ORDERS = (
    ((1, 0), (0, 1), (0, 0), (1, 1), (2, 0), (2, 1)),
    ((1, 0), (0, 1), (0, 0), (1, 1)),
    ((0, 0), (1, 1), (2, 0), (2, 1), (1, 0), (0, 1)),
)


def message_keys(sizes, sent, stage):
    keys = [key for key in ORDERS[stage] if key[1] == 0 or sizes[key[0]] > 2]
    return [key for key in keys if not (sent and key == (2, 1))]


def split(refs, sizes, stage, sent=False):
    refs, out = list(refs), [[None, None] for axis in range(3)]
    for axis, which in message_keys(sizes, sent, stage):
        out[axis][which] = refs.pop(0)
    return out, refs


def first_kernel(
    sizes, level, adjoint, density, velocity, stiffness, sponge, source, scaled, base, *refs
):
    outs, scratch = split(refs, sizes, 0, True)
    *targets, arrived = scratch
    level_now, adjoint_now, density_now, velocity_now, stiffness_now, sponge_now, source_now = targets
    copies = [
        pltpu.make_async_copy(there, here, arrived.at[index])
        for index, (there, here) in enumerate(
            zip((level, adjoint, density, velocity, stiffness, sponge, source), targets)
        )
    ]
    for copy in copies:
        copy.start()
    for copy in copies:
        copy.wait()
    here = positions()
    own_level = level_now[here[0], here[2], here[1]]
    half_inverse = 0.5 * lax.shift_left(jnp.int32(1), own_level).astype(jnp.float32)
    for direction in range(3):
        scaled[direction] = half_inverse * velocity_now[direction]
    scaled[3] = half_inverse * density_now[...]
    scaled[4] = half_inverse * stiffness_now[...]
    scaled[5] = half_inverse / density_now[...]
    tiles = own_part((0.0, 1.0), scaled, sponge_now, None, adjoint_now, base)
    x_low = tiles[0][0] + [source_now[tile_at(0), :]]
    x_high = tiles[CX - 1][0] + [source_now[tile_at(CX - 1), :]]
    y_low = faces_at(adjoint_now, scaled, row_at(0), 1) + [source_now[row_at(0), :]]
    y_high = faces_at(adjoint_now, scaled, row_at(CY - 1), 1) + [source_now[row_at(CY - 1), :]]
    put_pair(x_low, x_high, here[0], outs[0])
    put_pair(y_low, y_high, here[1], outs[1])
    along = [
        [[tiles[x][direction][component] for x in range(CX)] for component in range(5)]
        for direction in range(3)
    ]
    along[2].append([source_now[tile_at(x), :] for x in range(CX)])
    for index, fields in enumerate(
        (
            along[2],
            [[base[component, tile_at(x), :] for x in range(CX)] for component in range(5)],
            along[0],
            along[1],
            [[scaled[row, tile_at(x), :] for x in range(CX)] for row in range(2, 6)],
        )
    ):
        outs[2][0][index] = pack_lanes(fields)
    outs[2][0][5] = jnp.zeros(TILE, jnp.float32)


def own_kernel(weights, scaled, sponge, start, state, out):
    own_part(weights, scaled, sponge, start, state, out)


def own_part(weights, scaled, sponge, start, state, out):
    keep, blend = weights
    rows = lax.broadcasted_iota(jnp.int32, TILE, 0)
    lanes = lax.broadcasted_iota(jnp.int32, TILE, 1)
    tiles = [
        [faces_at(state, scaled, tile_at(x), direction) for direction in range(3)]
        for x in range(CX)
    ]
    for x in range(CX):
        damp = sponge[tile_at(x), :]
        for component in range(5):
            total = None
            if x < CX - 1:
                total = tiles[x + 1][0][component]
            if x > 0:
                before = tiles[x - 1][0][component]
                total = -before if total is None else total - before
            part = tiles[x][1][component]
            total = total + jnp.where(rows == CY - 1, 0.0, pltpu.roll(part, CY - 1, 0))
            total = total - jnp.where(rows == 0, 0.0, pltpu.roll(part, 1, 0))
            part = tiles[x][2][component]
            total = total + jnp.where(lanes == CZ - 1, 0.0, pltpu.roll(part, CZ - 1, 1))
            total = total - jnp.where(lanes == 0, 0.0, pltpu.roll(part, 1, 1))
            value = state[component, tile_at(x), :]
            value = blend * (value + step_length * (total - damp * value))
            if keep:
                value = value + keep * start[component, tile_at(x), :]
            out[component, tile_at(x), :] = value
    return tiles


def shape_kernel(sizes, source, scaled, sponge, start, *refs):
    sources, (shapes, sums, faces) = split(refs, sizes, 0)
    rows = lax.broadcasted_iota(jnp.int32, TILE, 0)
    lanes = lax.broadcasted_iota(jnp.int32, TILE, 1)
    outer = step_length * two_thirds
    inner = outer * step_length
    totals = [None] * 5
    for x in range(CX):
        at = tile_at(x)
        shape = source[at, :]
        along_x = jnp.zeros(TILE, jnp.float32)
        if x > 0:
            along_x = along_x + source[tile_at(x - 1), :]
        if x < CX - 1:
            along_x = along_x - source[tile_at(x + 1), :]
        along_y = jnp.where(rows == 0, 0.0, pltpu.roll(shape, 1, 0)) - jnp.where(
            rows == CY - 1, 0.0, pltpu.roll(shape, CY - 1, 0)
        )
        before = inner * jnp.where(lanes == 0, 0.0, pltpu.roll(shape, 1, 1))
        after = inner * jnp.where(lanes == CZ - 1, 0.0, pltpu.roll(shape, CZ - 1, 1))
        along_x, along_y = inner * along_x, inner * along_y
        own = outer * shape * (1.0 - step_length * sponge[at, :])
        own = own + scaled[0, at, :] * along_x + scaled[1, at, :] * along_y
        for index, value in enumerate(
            (own, scaled[2, at, :] * before, scaled[2, at, :] * after, along_x, along_y, before, after)
        ):
            shapes[index, at, :] = value
        weighted = (step_length * third) * shape
        for component in range(5):
            value = weighted * start[component, at, :]
            totals[component] = value if totals[component] is None else totals[component] + value
    for component in range(5):
        sums[component] = totals[component]
    here = positions()
    x_below, x_above = sorted_field(sources[0], 5, here[0], sizes[0])
    y_below, y_above = sorted_field(sources[1], 5, here[1], sizes[1])
    z_below, z_above = sorted_lanes(sources[2], here[2], sizes[2])
    aligned_above = jnp.zeros(TILE, jnp.float32)
    aligned_below = jnp.zeros(TILE, jnp.float32)
    for component in range(5):
        group = (lanes >= BASE) & ((lanes - BASE) // (2 * CX) == component)
        shift = 2 * CX * (component - 5)
        aligned_above = jnp.where(
            group & (lanes % 2 == 0), pltpu.roll(z_above, (shift - 1) % CZ, 1), aligned_above
        )
        aligned_below = jnp.where(
            group & (lanes % 2 == 1), pltpu.roll(z_below, (shift + 1) % CZ, 1), aligned_below
        )
    for index, (sign, face) in enumerate(
        (
            (-inner, x_above),
            (inner, x_below),
            (-inner, y_above),
            (inner, y_below),
            (-inner, aligned_above),
            (inner, aligned_below),
        )
    ):
        faces[index] = sign * face


def stage_kernel(sizes, weight, base, scaled, *refs):
    received, (section, *outs) = split(refs, sizes, 0)
    add_halo(base, received, weight, sizes, section)
    outs = split(outs, sizes, 1, True)[0]
    here = positions()
    x_low, x_high, y_low, y_high, z_fields = outer_faces(section, scaled)
    lanes = lax.broadcasted_iota(jnp.int32, TILE, 1)
    rows = lax.broadcasted_iota(jnp.int32, TILE, 0)
    place = (lanes + (CZ - BASE)) % CZ // 2 % CX
    x_below, x_above = sorted_field(received[2], 2, here[2], sizes[2])
    y_below, y_above = sorted_field(received[2], 3, here[2], sizes[2])
    far = 2 * (CX - 1)
    x_high.append(jnp.where(place == 0, both_layers(x_below, x_above, -far), 0.0))
    x_low.append(jnp.where(place == CX - 1, both_layers(x_below, x_above, far), 0.0))
    y_layers = both_layers(y_below, y_above, 0)
    y_high.append(jnp.where(rows == 0, pltpu.roll(y_layers, 1, 0), 0.0))
    y_low.append(jnp.where(rows == CY - 1, pltpu.roll(y_layers, CY - 1, 0), 0.0))
    put_pair(x_low, x_high, here[0], outs[0])
    put_pair(y_low, y_high, here[1], outs[1])


def both_layers(below, above, shift):
    lanes = lax.broadcasted_iota(jnp.int32, TILE, 1)
    return jnp.where(
        lanes % 2 == 0,
        pltpu.roll(above, (shift - 1) % CZ, 1),
        pltpu.roll(below, (shift + 1) % CZ, 1),
    )


def layer_partials(state, layer):
    group = 2 * CX
    return (
        layer[0] * state
        + layer[1] * pltpu.roll(state, 3 * group, 1)
        + layer[2] * pltpu.roll(state, CZ - group, 1)
        + layer[3] * pltpu.roll(state, group, 1)
    )


def layer_kernel(sizes, own, *refs):
    received, (layer, known) = split(refs, sizes, 0)
    here = positions()
    lanes = lax.broadcasted_iota(jnp.int32, TILE, 1)
    even = lanes % 2 == 0
    inside = (lanes >= BASE) & (lanes < BASE + 5 * 2 * CX)
    group = (lanes - BASE) // (2 * CX)
    below, above = sorted_field(received[2], 4, here[2], sizes[2])
    packed = jnp.where(even, 1.0, -1.0) * both_layers(below, above, 0)
    speed = jnp.zeros(TILE, jnp.float32)
    for component in range(5):
        speed = jnp.where(group == component, pltpu.roll(packed, 2 * CX * component, 1), speed)
    layer[0] = jnp.where(inside, speed, 0.0)
    layer[1] = jnp.where(inside & (group == 3), pltpu.roll(packed, 2 * CX * 2, 1), 0.0)
    layer[2] = jnp.where(inside & (group == 3), pltpu.roll(packed, 2 * CX, 1), 0.0)
    layer[3] = jnp.where(inside & (group == 4), pltpu.roll(packed, 2 * CX, 1), 0.0)
    below, above = sorted_field(received[2], 1, here[2], sizes[2])
    state = both_layers(below, above, 0)
    state = state + step_length * jnp.where(even, -own[0], own[0])
    known[...] = layer_partials(jnp.where(inside, state, 0.0), layer)


def sublane_total(tile):
    for shift in (4, 2, 1):
        tile = tile + pltpu.roll(tile, shift, 0)
    return tile


def three_parts(value):
    parts = []
    for _ in range(3):
        part = value.astype(jnp.bfloat16)
        parts.append(part)
        value = value - part.astype(jnp.float32)
    return parts


def product(value, matrix):
    count = value.shape[0]
    stacked = jnp.concatenate(three_parts(value), axis=0)
    result = jnp.dot(stacked, matrix, preferred_element_type=jnp.float32)
    return result[:count] + result[count : 2 * count] + result[2 * count :]


def target_kernel(sizes, patches, owners, routes, gather):
    here = positions()
    shape = routes.shape
    rows = lax.broadcasted_iota(jnp.int32, shape, 0)
    lanes = lax.broadcasted_iota(jnp.int32, shape, 1) % (CY * CY)
    chosen = jnp.zeros(shape, jnp.bool_)
    for index, offset in enumerate(OFFSETS):
        place = [
            jnp.clip(here[axis] + offset[axis], 0, sizes[axis] - 1) for axis in range(3)
        ]
        target = owners[patches[place[0], place[2], place[1]]]
        chosen = chosen | ((lanes // CY == index) & (rows == target))
    routes[...] = jnp.where(chosen, 1.0, 0.0).astype(jnp.bfloat16)
    rows = lax.broadcasted_iota(jnp.int32, (CZ, CZ), 0)
    lanes = lax.broadcasted_iota(jnp.int32, (CZ, CZ), 1)
    for component in range(5):
        ones = lanes == BOXES * component + rows // BZ
        gather[component * CZ : (component + 1) * CZ, :] = jnp.where(ones, 1.0, 0.0).astype(
            jnp.bfloat16
        )
    for index, box in enumerate((0, BOXES - 1)):
        ones = (lanes == BOXES * ((rows - BASE) // (2 * CX)) + box) & (rows >= BASE)
        ones = ones & (rows < BASE + 5 * 2 * CX)
        start = (5 + index) * CZ
        gather[start : start + CZ, :] = jnp.where(ones, 1.0, 0.0).astype(jnp.bfloat16)


OFFSETS = (
    (0, 0, 0),
    (1, 0, 0),
    (-1, 0, 0),
    (0, 1, 0),
    (0, -1, 0),
    (0, 0, 1),
    (0, 0, -1),
)


def gradient_kernel(
    sizes, weight, base, scaled, shapes, sums, faces, routes, gather, layer, known, *refs
):
    received, (section, table, *rest) = split(refs, sizes, 1)
    outs, (rows_out, sent) = split(rest, sizes, 2, True)
    here = positions()
    x_below, x_above = sorted_field(received[0], 5, here[0], sizes[0])
    y_below, y_above = sorted_field(received[1], 5, here[1], sizes[1])
    late = step_length * ((x_above - x_below) + (y_above - y_below))
    z_halo = known[...] + layer_partials(late, layer)
    add_halo(base, received, weight, sizes, section, z_halo=z_halo)
    x_low, x_high, y_low, y_high, z_fields = outer_faces(section, scaled)
    packed = pack_lanes(z_fields)
    main = [sums[component] for component in range(5)]
    before = [None] * 5
    after = [None] * 5

    def accumulate(totals, component, value):
        old = totals[component]
        totals[component] = value if old is None else old + value

    for x in range(CX):
        at = tile_at(x)
        state = [section[component, at, :] for component in range(5)]
        own, lane_before, lane_after, along_x, along_y, shape_before, shape_after = (
            shapes[index, at, :] for index in range(7)
        )
        push = scaled[3, at, :] * state[0] + scaled[4, at, :] * state[4]
        drawn = [scaled[5, at, :] * state[1 + direction] for direction in range(3)]
        for component in range(5):
            accumulate(main, component, own * state[component])
            accumulate(before, component, lane_before * state[component])
            accumulate(after, component, lane_after * state[component])
        accumulate(main, 1, along_x * push)
        accumulate(main, 2, along_y * push)
        accumulate(before, 3, shape_before * push)
        accumulate(after, 3, shape_after * push)
        accumulate(main, 4, along_x * drawn[0] + along_y * drawn[1])
        accumulate(before, 4, shape_before * drawn[2])
        accumulate(after, 4, shape_after * drawn[2])
    columns = []
    for f in range(5):
        own = main[f] + pltpu.roll(before[f], CZ - 1, 1) - pltpu.roll(after[f], 1, 1)
        columns.append(
            jnp.concatenate(
                [own, faces[0] * x_high[f], faces[1] * x_low[f], faces[2] * y_high[f], faces[3] * y_low[f]],
                axis=0,
            )
        )
    blocks = product(jnp.concatenate(columns, axis=1), gather[: 5 * CZ, :])
    above = product(faces[4] * packed, gather[5 * CZ : 6 * CZ, :])
    below = product(faces[5] * packed, gather[6 * CZ :, :])
    blocks = jnp.concatenate([blocks, above, below, jnp.zeros(TILE, jnp.float32)], axis=0)
    rows_out[...] = jnp.dot(
        routes[...],
        jnp.concatenate(three_parts(blocks), axis=0),
        preferred_element_type=jnp.float32,
    )
    copy = pltpu.make_async_copy(rows_out, table, sent)
    copy.start()
    put_pair(x_low, x_high, here[0], outs[0])
    put_pair(y_low, y_high, here[1], outs[1])
    outs[2][0][0] = packed
    for index in range(1, 5):
        outs[2][0][index] = jnp.zeros(TILE, jnp.float32)
    copy.wait()


def last_kernel(sizes, base, table, *refs):
    received, (out, gradient, done, block, sent) = split(refs, sizes, 2)
    totals = [None] * 4
    for device in range(table.shape[0]):
        part = table[device : device + 1, :]
        old = totals[device % 4]
        totals[device % 4] = part if old is None else old + part
    total = (totals[0] + totals[1]) + (totals[2] + totals[3])
    block[...] = total[:, : 5 * BOXES]
    copies = [pltpu.make_async_copy(block, gradient, sent.at[5])]
    copies[0].start()

    def send(component):
        copy = pltpu.make_async_copy(done.at[component], out.at[component], sent.at[component])
        copy.start()
        copies.append(copy)

    add_halo(base, received, two_thirds * step_length, sizes, done, send)
    for copy in copies:
        copy.wait()


VMEM = pl.BlockSpec(memory_space=pltpu.VMEM)
SMEM = pl.BlockSpec(memory_space=pltpu.SMEM)
HBM = pl.BlockSpec(memory_space=pltpu.HBM)


def call(kernel, in_specs, operands, out_shapes, scratch=(), spaces=None, dtype=jnp.float32):
    spaces = spaces or [pltpu.VMEM] * len(out_shapes)
    operands = [
        pltpu.with_memory_space_constraint(operand, pltpu.HBM) if spec is HBM else operand
        for spec, operand in zip(in_specs, operands)
    ]
    return pl.pallas_call(
        kernel,
        out_shape=[space(shape, dtype) for space, shape in zip(spaces, out_shapes)],
        in_specs=in_specs,
        out_specs=[pl.BlockSpec(memory_space=space) for space in spaces],
        scratch_shapes=list(scratch),
        compiler_params=pltpu.CompilerParams(vmem_limit_bytes=16 * 1024 * 1024),
        cost_estimate=pl.CostEstimate(flops=2000000, bytes_accessed=1000000, transcendentals=0),
    )(*operands)


def body(
    terminal_adjoint,
    density,
    velocity,
    stiffness,
    sponge,
    source_shape,
    brick_level,
    brick_patch,
    patch_owner,
):
    sizes = tuple(lax.axis_size(axis) for axis in AXES)
    permutations = (
        pairings(sizes, 0, 1),
        pairings(sizes, 1, 1),
        pairings(sizes, 2, 1),
    )
    devices = patch_owner.shape[0]
    state_shape = terminal_adjoint.shape
    start = terminal_adjoint.reshape(STATE)
    density, stiffness, sponge, source = (
        array.reshape(FLAT) for array in (density, stiffness, sponge, source_shape)
    )
    velocity = velocity.reshape((3,) + FLAT)
    level = jnp.transpose(brick_level, (0, 2, 1))
    patches = jnp.transpose(brick_patch, (0, 2, 1))

    def message_shapes(fields, stage):
        return [
            (fields,) + TILE for key in message_keys(sizes, True, stage)
        ]

    def exchange(messages, stage):
        sends = dict(zip(message_keys(sizes, True, stage), messages))
        sends[2, 1] = sends.get((2, 0))
        return [
            lax.ppermute(sends[key], AXES, permutations[key[0]][key[1]])
            for key in message_keys(sizes, False, stage)
        ]

    flat = pltpu.VMEM(FLAT, jnp.float32)
    state = pltpu.VMEM(STATE, jnp.float32)
    scaled, base, *sent = call(
        functools.partial(first_kernel, sizes),
        [HBM] * 7,
        (level, start, density, velocity, stiffness, sponge, source),
        [(6,) + FLAT, STATE] + message_shapes(6, 0),
        scratch=[
            pltpu.SMEM(level.shape, jnp.int32),
            state,
            flat,
            pltpu.VMEM((3,) + FLAT, jnp.float32),
            flat,
            flat,
            flat,
            pltpu.SemaphoreType.DMA((7,)),
        ],
    )
    received_one = exchange(sent, 0)
    own_layers = dict(zip(message_keys(sizes, True, 0), sent))[2, 0]
    routes, gather = call(
        functools.partial(target_kernel, sizes),
        [SMEM] * 2,
        (patches, patch_owner),
        [(devices, 3 * CY * CY), (7 * CZ, CZ)],
        dtype=jnp.bfloat16,
    )
    operands = (base, scaled, *received_one)
    section, *sent = call(
        functools.partial(stage_kernel, sizes, step_length),
        [VMEM] * len(operands),
        operands,
        [STATE] + message_shapes(6, 1),
    )
    received = exchange(sent, 1)
    operands = (own_layers, *received_one)
    layer, known = call(
        functools.partial(layer_kernel, sizes),
        [VMEM] * len(operands),
        operands,
        [(4,) + TILE, TILE],
    )
    (base,) = call(
        functools.partial(own_kernel, (0.75, 0.25)),
        [VMEM] * 4,
        (scaled, sponge, start, section),
        [STATE],
    )
    operands = (source, scaled, sponge, start, *received_one)
    shapes, sums, faces = call(
        functools.partial(shape_kernel, sizes),
        [VMEM] * len(operands),
        operands,
        [(7,) + FLAT, (5,) + TILE, (6,) + TILE],
    )
    operands = (base, scaled, shapes, sums, faces, routes, gather, layer, known, *received)
    section, table, *sent = call(
        functools.partial(gradient_kernel, sizes, 0.25 * step_length),
        [VMEM] * len(operands),
        operands,
        [STATE, (devices, CZ)] + message_shapes(5, 2),
        scratch=[pltpu.VMEM((devices, CZ), jnp.float32), pltpu.SemaphoreType.DMA],
        spaces=[pltpu.VMEM, pltpu.HBM] + [pltpu.VMEM] * len(message_shapes(5, 2)),
    )
    table = lax.all_to_all(table.reshape(devices, 1, CZ), AXES, 0, 0, tiled=True)
    received = exchange(sent, 2)
    (base,) = call(
        functools.partial(own_kernel, (third, two_thirds)),
        [VMEM] * 4,
        (scaled, sponge, start, section),
        [STATE],
    )
    operands = (base, table.reshape(devices, CZ), *received)
    adjoint, gradient = call(
        functools.partial(last_kernel, sizes),
        [VMEM] * len(operands),
        operands,
        [STATE, (1, 5 * BOXES)],
        scratch=[state, pltpu.VMEM((1, 5 * BOXES), jnp.float32), pltpu.SemaphoreType.DMA((6,))],
        spaces=[pltpu.HBM] * 2,
    )
    return adjoint.reshape(state_shape), gradient


def solution(mesh):
    in_specs = (
        P(None, "gx", "gy", "gz"),
        P("gx", "gy", "gz"),
        P(None, "gx", "gy", "gz"),
        P("gx", "gy", "gz"),
        P("gx", "gy", "gz"),
        P("gx", "gy", "gz"),
        P(),
        P(),
        P(),
    )
    out_specs = (P(None, "gx", "gy", "gz"), P(("gx", "gy", "gz"), None))
    return jax.shard_map(body, mesh=mesh, in_specs=in_specs, out_specs=out_specs, check_vma=False)
```

```python
import functools

import jax
import jax.numpy as jnp
from jax import lax
from jax.experimental import pallas as pl
from jax.experimental.pallas import tpu as pltpu
from jax.sharding import PartitionSpec as P

CX = 8
CY = 8
CZ = 128
BZ = 16
BOXES = CZ // BZ
ROWS = CX * CY

AXES = ("gx", "gy", "gz")

step_length = 0.14
third = 1.0 / 3.0
two_thirds = 2.0 / 3.0

BASE = 5 * BOXES

TILE = (CY, CZ)
FLAT = (ROWS, CZ)
STATE = (5,) + FLAT


def pairings(sizes, axis, near_axis):
    size = sizes[axis]
    first, second = [], []
    for x in range(sizes[0]):
        for y in range(sizes[1]):
            for z in range(sizes[2]):
                here = [x, y, z]
                index = (x * sizes[1] + y) * sizes[2] + z
                place = here[axis]
                other = list(here)
                other[axis] = place ^ 1
                first.append((index, (other[0] * sizes[1] + other[1]) * sizes[2] + other[2]))
                other = list(here)
                if 0 < place < size - 1 or near_axis == axis:
                    other[axis] = (place + (1 if place % 2 else -1)) % size
                else:
                    other[near_axis] = here[near_axis] ^ 1
                second.append((index, (other[0] * sizes[1] + other[1]) * sizes[2] + other[2]))
    return first, second if size > 2 else None


def first_round(sizes):
    x, y, z = pairings(sizes, 0, 1), pairings(sizes, 1, 1), pairings(sizes, 2, 1)
    if sizes[0] > 2:
        plane = sizes[1] * sizes[2]
        first, second = dict(z[0]), dict(x[1])
        for index in range(plane):
            first[index], second[index] = second[index], first[index]
        x, z = (x[0], sorted(second.items())), (sorted(first.items()), z[1])
    return x, y, z


def at_start():
    return lax.axis_index(AXES[0]) == 0


class ZFields:
    def __init__(self, x_second, z_first):
        self.x_second, self.z_first = x_second, z_first

    def __getitem__(self, index):
        return jnp.where(at_start(), self.x_second[index], self.z_first[index])


def positions():
    return [lax.axis_index(axis) for axis in AXES]


def tile_at(x):
    return slice(x * CY, (x + 1) * CY)


def row_at(y):
    return pl.ds(y, CX, stride=CY)


def partials_of(adjoint, speed, density, stiffness, inverse, direction):
    components = [speed * component for component in adjoint]
    row = 1 + direction
    components[row] = components[row] + (density * adjoint[0] + stiffness * adjoint[4])
    components[4] = components[4] + adjoint[row] * inverse
    return components


def faces_at(state, scaled, rows, direction):
    adjoint = [state[component, rows, :] for component in range(5)]
    return partials_of(
        adjoint,
        scaled[direction, rows, :],
        scaled[3, rows, :],
        scaled[4, rows, :],
        scaled[5, rows, :],
        direction,
    )


def pack_lanes(fields):
    lanes = (lax.broadcasted_iota(jnp.int32, TILE, 1) + (CZ - BASE)) % CZ // 2
    tiles = []
    for index, field in enumerate(fields):
        for x in range(CX):
            k = index * CX + x
            tiles.append(pltpu.roll(field[x], (BASE + 2 * k + 1) % CZ, 1))
    bit = 1
    while len(tiles) > 1:
        upper = (lanes & bit) != 0
        pairs = [
            jnp.where(upper, tiles[at + 1], tiles[at]) if at + 1 < len(tiles) else tiles[at]
            for at in range(0, len(tiles), 2)
        ]
        tiles, bit = pairs, 2 * bit
    return tiles[0]


def put_pair(low, high, position, outs):
    even = position % 2 == 0
    for index, (below, above) in enumerate(zip(low, high)):
        outs[0][index] = jnp.where(even, above, below)
        if outs[1] is not None:
            outs[1][index] = jnp.where(even, below, above)


def outer_faces(state, scaled):
    x_low = faces_at(state, scaled, tile_at(0), 0)
    x_high = faces_at(state, scaled, tile_at(CX - 1), 0)
    y_low = faces_at(state, scaled, row_at(0), 1)
    y_high = faces_at(state, scaled, row_at(CY - 1), 1)
    z_tiles = [faces_at(state, scaled, tile_at(x), 2) for x in range(CX)]
    z_fields = [[z_tiles[x][component] for x in range(CX)] for component in range(5)]
    return x_low, x_high, y_low, y_high, z_fields


def put_messages(state, scaled, source, outs):
    here = positions()
    x_low, x_high, y_low, y_high, z_fields = outer_faces(state, scaled)
    if source is not None:
        x_low.append(source[tile_at(0), :])
        x_high.append(source[tile_at(CX - 1), :])
        y_low.append(source[row_at(0), :])
        y_high.append(source[row_at(CY - 1), :])
        z_fields.append([source[tile_at(x), :] for x in range(CX)])
    outs[2][0][0] = pack_lanes(z_fields)
    for index in range(1, outs[2][0].shape[0]):
        outs[2][0][index] = jnp.zeros(TILE, jnp.float32)
    put_pair(x_low, x_high, here[0], outs[0])
    put_pair(y_low, y_high, here[1], outs[1])


def sort_pair(first, second, position, size):
    even = position % 2 == 0
    zero = jnp.zeros_like(first)
    if second is None:
        return jnp.where(even, zero, first), jnp.where(even, first, zero)
    below = jnp.where(position == 0, zero, jnp.where(even, second, first))
    above = jnp.where(position == size - 1, zero, jnp.where(even, first, second))
    return below, above


def sorted_field(refs, index, position, size):
    first, second = refs
    return sort_pair(first[index], None if second is None else second[index], position, size)


def sorted_lanes(refs, position, size):
    return sorted_field(refs, 0, position, size)


def add_halo(base, received, weight, sizes, out, finish=None, z_halo=None):
    here = positions()
    lanes = lax.broadcasted_iota(jnp.int32, TILE, 1)
    edges = (lanes == 0) | (lanes == CZ - 1)
    if z_halo is None:
        z_below, z_above = sorted_lanes(received[2], here[2], sizes[2])
        z_halo = jnp.where(
            lanes % 2 == 0, pltpu.roll(z_above, CZ - 1, 1), -pltpu.roll(z_below, 1, 1)
        )
    z_halo = weight * z_halo
    for component in range(5):
        x_below, x_above = sorted_field(received[0], component, here[0], sizes[0])
        y_below, y_above = sorted_field(received[1], component, here[1], sizes[1])
        for x in range(CX):
            k = component * CX + x
            value = base[component, tile_at(x), :]
            value = value + jnp.where(edges, pltpu.roll(z_halo, (CZ - 1 - BASE - 2 * k) % CZ, 1), 0.0)
            if x == 0:
                value = value - weight * x_below
            if x == CX - 1:
                value = value + weight * x_above
            out[component, tile_at(x), :] = value
        out[component, row_at(0), :] = out[component, row_at(0), :] - weight * y_below
        out[component, row_at(CY - 1), :] = out[component, row_at(CY - 1), :] + weight * y_above
        if finish is not None:
            finish(component)


ORDERS = (
    ((1, 0), (0, 1), (0, 0), (1, 1), (2, 0), (2, 1)),
    ((1, 0), (0, 0), (0, 1), (1, 1)),
    ((0, 0), (1, 1), (2, 0), (2, 1), (1, 0), (0, 1)),
)


def message_keys(sizes, sent, stage):
    keys = [key for key in ORDERS[stage] if key[1] == 0 or sizes[key[0]] > 2]
    return [key for key in keys if not (sent and key == (2, 1))]


def split(refs, sizes, stage, sent=False):
    refs, out = list(refs), [[None, None] for axis in range(3)]
    for axis, which in message_keys(sizes, sent, stage):
        out[axis][which] = refs.pop(0)
    if stage == 0 and not sent and sizes[0] > 2:
        out[2][0] = ZFields(out[0][1], out[2][0])
    return out, refs


def first_kernel(sizes, level, adjoint, density, velocity, stiffness, sponge, source, *refs):
    adjoint_now, sponge_now, source_now, scaled, base, *refs = refs
    outs, scratch = split(refs, sizes, 0, True)
    level_now, density_now, velocity_now, stiffness_now, arrived = scratch
    targets = (
        level_now, density_now, velocity_now, stiffness_now, adjoint_now, sponge_now, source_now
    )
    copies = [
        pltpu.make_async_copy(there, here, arrived.at[index])
        for index, (there, here) in enumerate(
            zip((level, density, velocity, stiffness, adjoint, sponge, source), targets)
        )
    ]
    for copy in copies:
        copy.start()
    level_copy, density_copy, velocity_copy, stiffness_copy, *other_copies = copies
    level_copy.wait()
    here = positions()
    own_level = level_now[here[0], here[2], here[1]]
    half_inverse = 0.5 * lax.shift_left(jnp.int32(1), own_level).astype(jnp.float32)
    density_copy.wait()
    scaled[3] = half_inverse * density_now[...]
    scaled[5] = half_inverse / density_now[...]
    velocity_copy.wait()
    for direction in range(3):
        scaled[direction] = half_inverse * velocity_now[direction]
    stiffness_copy.wait()
    scaled[4] = half_inverse * stiffness_now[...]
    for copy in other_copies:
        copy.wait()
    tiles = own_part((0.0, 1.0), scaled, sponge_now, None, adjoint_now, base)
    x_low = tiles[0][0] + [source_now[tile_at(0), :]]
    x_high = tiles[CX - 1][0] + [source_now[tile_at(CX - 1), :]]
    y_low = faces_at(adjoint_now, scaled, row_at(0), 1) + [source_now[row_at(0), :]]
    y_high = faces_at(adjoint_now, scaled, row_at(CY - 1), 1) + [source_now[row_at(CY - 1), :]]
    put_pair(x_low, x_high, here[0], outs[0])
    put_pair(y_low, y_high, here[1], outs[1])
    along = [
        [[tiles[x][direction][component] for x in range(CX)] for component in range(5)]
        for direction in range(3)
    ]
    along[2].append([source_now[tile_at(x), :] for x in range(CX)])
    for index, fields in enumerate(
        (
            along[2],
            [[base[component, tile_at(x), :] for x in range(CX)] for component in range(5)],
            along[0],
            along[1],
            [[scaled[row, tile_at(x), :] for x in range(CX)] for row in range(2, 6)],
        )
    ):
        outs[2][0][index] = pack_lanes(fields)
    outs[2][0][5] = jnp.zeros(TILE, jnp.float32)
    if sizes[0] > 2:

        @pl.when(at_start())
        def _():
            for index in range(5):
                outs[0][1][index] = outs[2][0][index]


def own_kernel(weights, scaled, sponge, start, state, out):
    own_part(weights, scaled, sponge, start, state, out)


def own_part(weights, scaled, sponge, start, state, out):
    keep, blend = weights
    rows = lax.broadcasted_iota(jnp.int32, TILE, 0)
    lanes = lax.broadcasted_iota(jnp.int32, TILE, 1)
    tiles = [
        [faces_at(state, scaled, tile_at(x), direction) for direction in range(3)]
        for x in range(CX)
    ]
    for x in range(CX):
        damp = sponge[tile_at(x), :]
        for component in range(5):
            total = None
            if x < CX - 1:
                total = tiles[x + 1][0][component]
            if x > 0:
                before = tiles[x - 1][0][component]
                total = -before if total is None else total - before
            part = tiles[x][1][component]
            total = total + jnp.where(rows == CY - 1, 0.0, pltpu.roll(part, CY - 1, 0))
            total = total - jnp.where(rows == 0, 0.0, pltpu.roll(part, 1, 0))
            part = tiles[x][2][component]
            total = total + jnp.where(lanes == CZ - 1, 0.0, pltpu.roll(part, CZ - 1, 1))
            total = total - jnp.where(lanes == 0, 0.0, pltpu.roll(part, 1, 1))
            value = state[component, tile_at(x), :]
            value = blend * (value + step_length * (total - damp * value))
            if keep:
                value = value + keep * start[component, tile_at(x), :]
            out[component, tile_at(x), :] = value
    return tiles


def shape_kernel(sizes, source, scaled, sponge, start, *refs):
    sources, (shapes, sums, faces) = split(refs, sizes, 0)
    rows = lax.broadcasted_iota(jnp.int32, TILE, 0)
    lanes = lax.broadcasted_iota(jnp.int32, TILE, 1)
    outer = step_length * two_thirds
    inner = outer * step_length
    totals = [None] * 5
    for x in range(CX):
        at = tile_at(x)
        shape = source[at, :]
        along_x = jnp.zeros(TILE, jnp.float32)
        if x > 0:
            along_x = along_x + source[tile_at(x - 1), :]
        if x < CX - 1:
            along_x = along_x - source[tile_at(x + 1), :]
        along_y = jnp.where(rows == 0, 0.0, pltpu.roll(shape, 1, 0)) - jnp.where(
            rows == CY - 1, 0.0, pltpu.roll(shape, CY - 1, 0)
        )
        before = inner * jnp.where(lanes == 0, 0.0, pltpu.roll(shape, 1, 1))
        after = inner * jnp.where(lanes == CZ - 1, 0.0, pltpu.roll(shape, CZ - 1, 1))
        along_x, along_y = inner * along_x, inner * along_y
        own = outer * shape * (1.0 - step_length * sponge[at, :])
        own = own + scaled[0, at, :] * along_x + scaled[1, at, :] * along_y
        for index, value in enumerate(
            (own, scaled[2, at, :] * before, scaled[2, at, :] * after, along_x, along_y, before, after)
        ):
            shapes[index, at, :] = value
        weighted = (step_length * third) * shape
        for component in range(5):
            value = weighted * start[component, at, :]
            totals[component] = value if totals[component] is None else totals[component] + value
    for component in range(5):
        sums[component] = totals[component]
    here = positions()
    x_below, x_above = sorted_field(sources[0], 5, here[0], sizes[0])
    y_below, y_above = sorted_field(sources[1], 5, here[1], sizes[1])
    z_below, z_above = sorted_lanes(sources[2], here[2], sizes[2])
    aligned_above = jnp.zeros(TILE, jnp.float32)
    aligned_below = jnp.zeros(TILE, jnp.float32)
    for component in range(5):
        group = (lanes >= BASE) & ((lanes - BASE) // (2 * CX) == component)
        shift = 2 * CX * (component - 5)
        aligned_above = jnp.where(
            group & (lanes % 2 == 0), pltpu.roll(z_above, (shift - 1) % CZ, 1), aligned_above
        )
        aligned_below = jnp.where(
            group & (lanes % 2 == 1), pltpu.roll(z_below, (shift + 1) % CZ, 1), aligned_below
        )
    for index, (sign, face) in enumerate(
        (
            (-inner, x_above),
            (inner, x_below),
            (-inner, y_above),
            (inner, y_below),
            (-inner, aligned_above),
            (inner, aligned_below),
        )
    ):
        faces[index] = sign * face


def stage_kernel(sizes, weight, base, scaled, routes, *refs):
    received, (section, *outs) = split(refs, sizes, 0)
    add_halo(base, received, weight, sizes, section)
    outs = split(outs, sizes, 1, True)[0]
    here = positions()
    x_low, x_high, y_low, y_high, z_fields = outer_faces(section, scaled)
    lanes = lax.broadcasted_iota(jnp.int32, TILE, 1)
    rows = lax.broadcasted_iota(jnp.int32, TILE, 0)
    place = (lanes + (CZ - BASE)) % CZ // 2 % CX
    x_below, x_above = sorted_field(received[2], 2, here[2], sizes[2])
    y_below, y_above = sorted_field(received[2], 3, here[2], sizes[2])
    far = 2 * (CX - 1)
    x_high.append(jnp.where(place == 0, both_layers(x_below, x_above, -far), 0.0))
    x_low.append(jnp.where(place == CX - 1, both_layers(x_below, x_above, far), 0.0))
    y_layers = both_layers(y_below, y_above, 0)
    y_high.append(jnp.where(rows == 0, pltpu.roll(y_layers, 1, 0), 0.0))
    y_low.append(jnp.where(rows == CY - 1, pltpu.roll(y_layers, CY - 1, 0), 0.0))
    put_pair(x_low, x_high, here[0], outs[0])
    put_pair(y_low, y_high, here[1], outs[1])


def both_layers(below, above, shift):
    lanes = lax.broadcasted_iota(jnp.int32, TILE, 1)
    return jnp.where(
        lanes % 2 == 0,
        pltpu.roll(above, (shift - 1) % CZ, 1),
        pltpu.roll(below, (shift + 1) % CZ, 1),
    )


def layer_partials(state, layer):
    group = 2 * CX
    return (
        layer[0] * state
        + layer[1] * pltpu.roll(state, 3 * group, 1)
        + layer[2] * pltpu.roll(state, CZ - group, 1)
        + layer[3] * pltpu.roll(state, group, 1)
    )


def layer_kernel(sizes, own, *refs):
    received, (layer, known) = split(refs, sizes, 0)
    here = positions()
    lanes = lax.broadcasted_iota(jnp.int32, TILE, 1)
    even = lanes % 2 == 0
    inside = (lanes >= BASE) & (lanes < BASE + 5 * 2 * CX)
    group = (lanes - BASE) // (2 * CX)
    below, above = sorted_field(received[2], 4, here[2], sizes[2])
    packed = jnp.where(even, 1.0, -1.0) * both_layers(below, above, 0)
    speed = jnp.zeros(TILE, jnp.float32)
    for component in range(5):
        speed = jnp.where(group == component, pltpu.roll(packed, 2 * CX * component, 1), speed)
    layer[0] = jnp.where(inside, speed, 0.0)
    layer[1] = jnp.where(inside & (group == 3), pltpu.roll(packed, 2 * CX * 2, 1), 0.0)
    layer[2] = jnp.where(inside & (group == 3), pltpu.roll(packed, 2 * CX, 1), 0.0)
    layer[3] = jnp.where(inside & (group == 4), pltpu.roll(packed, 2 * CX, 1), 0.0)
    below, above = sorted_field(received[2], 1, here[2], sizes[2])
    state = both_layers(below, above, 0)
    state = state + step_length * jnp.where(even, -own[0], own[0])
    known[...] = layer_partials(jnp.where(inside, state, 0.0), layer)


def sublane_total(tile):
    for shift in (4, 2, 1):
        tile = tile + pltpu.roll(tile, shift, 0)
    return tile


def three_parts(value):
    parts = []
    for _ in range(3):
        part = value.astype(jnp.bfloat16)
        parts.append(part)
        value = value - part.astype(jnp.float32)
    return parts


def product(value, matrix):
    count = value.shape[0]
    stacked = jnp.concatenate(three_parts(value), axis=0)
    result = jnp.dot(stacked, matrix, preferred_element_type=jnp.float32)
    return result[:count] + result[count : 2 * count] + result[2 * count :]


def target_kernel(sizes, patches, owners, routes, gather):
    here = positions()
    shape = routes.shape
    rows = lax.broadcasted_iota(jnp.int32, shape, 0)
    lanes = lax.broadcasted_iota(jnp.int32, shape, 1) % (CY * CY)
    chosen = jnp.zeros(shape, jnp.bool_)
    for index, offset in enumerate(OFFSETS):
        place = [
            jnp.clip(here[axis] + offset[axis], 0, sizes[axis] - 1) for axis in range(3)
        ]
        target = owners[patches[place[0], place[2], place[1]]]
        chosen = chosen | ((lanes // CY == index) & (rows == target))
    routes[...] = jnp.where(chosen, 1.0, 0.0).astype(jnp.bfloat16)
    rows = lax.broadcasted_iota(jnp.int32, (CZ, CZ), 0)
    lanes = lax.broadcasted_iota(jnp.int32, (CZ, CZ), 1)
    for component in range(5):
        ones = lanes == BOXES * component + rows // BZ
        gather[component * CZ : (component + 1) * CZ, :] = jnp.where(ones, 1.0, 0.0).astype(
            jnp.bfloat16
        )
    for index, box in enumerate((0, BOXES - 1)):
        ones = (lanes == BOXES * ((rows - BASE) // (2 * CX)) + box) & (rows >= BASE)
        ones = ones & (rows < BASE + 5 * 2 * CX)
        start = (5 + index) * CZ
        gather[start : start + CZ, :] = jnp.where(ones, 1.0, 0.0).astype(jnp.bfloat16)


OFFSETS = (
    (0, 0, 0),
    (1, 0, 0),
    (-1, 0, 0),
    (0, 1, 0),
    (0, -1, 0),
    (0, 0, 1),
    (0, 0, -1),
)


def gradient_kernel(
    sizes, weight, base, scaled, shapes, sums, faces, routes, gather, layer, known, *refs
):
    received, (section, table, *rest) = split(refs, sizes, 1)
    outs, (rows_out, sent) = split(rest, sizes, 2, True)
    here = positions()
    x_below, x_above = sorted_field(received[0], 5, here[0], sizes[0])
    y_below, y_above = sorted_field(received[1], 5, here[1], sizes[1])
    late = step_length * ((x_above - x_below) + (y_above - y_below))
    z_halo = known[...] + layer_partials(late, layer)
    add_halo(base, received, weight, sizes, section, z_halo=z_halo)
    x_low, x_high, y_low, y_high, z_fields = outer_faces(section, scaled)
    packed = pack_lanes(z_fields)
    main = [sums[component] for component in range(5)]
    before = [None] * 5
    after = [None] * 5

    def accumulate(totals, component, value):
        old = totals[component]
        totals[component] = value if old is None else old + value

    for x in range(CX):
        at = tile_at(x)
        state = [section[component, at, :] for component in range(5)]
        own, lane_before, lane_after, along_x, along_y, shape_before, shape_after = (
            shapes[index, at, :] for index in range(7)
        )
        push = scaled[3, at, :] * state[0] + scaled[4, at, :] * state[4]
        drawn = [scaled[5, at, :] * state[1 + direction] for direction in range(3)]
        for component in range(5):
            accumulate(main, component, own * state[component])
            accumulate(before, component, lane_before * state[component])
            accumulate(after, component, lane_after * state[component])
        accumulate(main, 1, along_x * push)
        accumulate(main, 2, along_y * push)
        accumulate(before, 3, shape_before * push)
        accumulate(after, 3, shape_after * push)
        accumulate(main, 4, along_x * drawn[0] + along_y * drawn[1])
        accumulate(before, 4, shape_before * drawn[2])
        accumulate(after, 4, shape_after * drawn[2])
    columns = []
    for f in range(5):
        own = main[f] + pltpu.roll(before[f], CZ - 1, 1) - pltpu.roll(after[f], 1, 1)
        columns.append(
            jnp.concatenate(
                [own, faces[0] * x_high[f], faces[1] * x_low[f], faces[2] * y_high[f], faces[3] * y_low[f]],
                axis=0,
            )
        )
    blocks = product(jnp.concatenate(columns, axis=1), gather[: 5 * CZ, :])
    above = product(faces[4] * packed, gather[5 * CZ : 6 * CZ, :])
    below = product(faces[5] * packed, gather[6 * CZ :, :])
    blocks = jnp.concatenate([blocks, above, below, jnp.zeros(TILE, jnp.float32)], axis=0)
    rows_out[...] = jnp.dot(
        routes[...],
        jnp.concatenate(three_parts(blocks), axis=0),
        preferred_element_type=jnp.float32,
    )
    copy = pltpu.make_async_copy(rows_out, table, sent)
    copy.start()
    put_pair(x_low, x_high, here[0], outs[0])
    put_pair(y_low, y_high, here[1], outs[1])
    outs[2][0][0] = packed
    copy.wait()


def last_kernel(sizes, base, table, *refs):
    received, (out, gradient, done, block, sent) = split(refs, sizes, 2)
    totals = [None] * 4
    for device in range(table.shape[0]):
        part = table[device : device + 1, :]
        old = totals[device % 4]
        totals[device % 4] = part if old is None else old + part
    total = (totals[0] + totals[1]) + (totals[2] + totals[3])
    block[...] = total[:, : 5 * BOXES]
    copies = [pltpu.make_async_copy(block, gradient, sent.at[5])]
    copies[0].start()

    def send(component):
        copy = pltpu.make_async_copy(done.at[component], out.at[component], sent.at[component])
        copy.start()
        copies.append(copy)

    add_halo(base, received, two_thirds * step_length, sizes, done, send)
    for copy in copies:
        copy.wait()


VMEM = pl.BlockSpec(memory_space=pltpu.VMEM)
SMEM = pl.BlockSpec(memory_space=pltpu.SMEM)
HBM = pl.BlockSpec(memory_space=pltpu.HBM)


def call(kernel, in_specs, operands, out_shapes, scratch=(), spaces=None, dtype=jnp.float32):
    spaces = spaces or [pltpu.VMEM] * len(out_shapes)
    operands = [
        pltpu.with_memory_space_constraint(operand, pltpu.HBM) if spec is HBM else operand
        for spec, operand in zip(in_specs, operands)
    ]
    return pl.pallas_call(
        kernel,
        out_shape=[space(shape, dtype) for space, shape in zip(spaces, out_shapes)],
        in_specs=in_specs,
        out_specs=[pl.BlockSpec(memory_space=space) for space in spaces],
        scratch_shapes=list(scratch),
        compiler_params=pltpu.CompilerParams(vmem_limit_bytes=16 * 1024 * 1024),
        cost_estimate=pl.CostEstimate(flops=2000000, bytes_accessed=1000000, transcendentals=0),
    )(*operands)


def body(
    terminal_adjoint,
    density,
    velocity,
    stiffness,
    sponge,
    source_shape,
    brick_level,
    brick_patch,
    patch_owner,
):
    sizes = tuple(lax.axis_size(axis) for axis in AXES)
    later = (pairings(sizes, 0, 1), pairings(sizes, 1, 1), pairings(sizes, 2, 1))
    permutations = (first_round(sizes), later, later)
    devices = patch_owner.shape[0]
    state_shape = terminal_adjoint.shape
    start = terminal_adjoint.reshape(STATE)
    density, stiffness, sponge, source = (
        array.reshape(FLAT) for array in (density, stiffness, sponge, source_shape)
    )
    velocity = velocity.reshape((3,) + FLAT)
    level = jnp.transpose(brick_level, (0, 2, 1))
    patches = jnp.transpose(brick_patch, (0, 2, 1))

    def message_shapes(fields, stage):
        return [
            (1 if stage == 2 and key[0] == 2 else fields,) + TILE
            for key in message_keys(sizes, True, stage)
        ]

    def exchange(messages, stage):
        sends = dict(zip(message_keys(sizes, True, stage), messages))
        sends[2, 1] = sends.get((2, 0))
        return [
            lax.ppermute(sends[key], AXES, permutations[stage][key[0]][key[1]])
            for key in message_keys(sizes, False, stage)
        ]

    flat = pltpu.VMEM(FLAT, jnp.float32)
    state = pltpu.VMEM(STATE, jnp.float32)
    start, sponge, source, scaled, base, *sent = call(
        functools.partial(first_kernel, sizes),
        [HBM] * 7,
        (level, start, density, velocity, stiffness, sponge, source),
        [STATE, FLAT, FLAT, (6,) + FLAT, STATE] + message_shapes(6, 0),
        scratch=[
            pltpu.SMEM(level.shape, jnp.int32),
            flat,
            pltpu.VMEM((3,) + FLAT, jnp.float32),
            flat,
            pltpu.SemaphoreType.DMA((7,)),
        ],
    )
    received_one = exchange(sent, 0)
    own_layers = dict(zip(message_keys(sizes, True, 0), sent))[2, 0]
    routes, gather = call(
        functools.partial(target_kernel, sizes),
        [SMEM] * 2,
        (patches, patch_owner),
        [(devices, 3 * CY * CY), (7 * CZ, CZ)],
        dtype=jnp.bfloat16,
    )
    operands = (base, scaled, routes, *received_one)
    section, *sent = call(
        functools.partial(stage_kernel, sizes, step_length),
        [VMEM] * len(operands),
        operands,
        [STATE] + message_shapes(6, 1),
    )
    received = exchange(sent, 1)
    operands = (own_layers, *received_one)
    layer, known = call(
        functools.partial(layer_kernel, sizes),
        [VMEM] * len(operands),
        operands,
        [(4,) + TILE, TILE],
    )
    (base,) = call(
        functools.partial(own_kernel, (0.75, 0.25)),
        [VMEM] * 4,
        (scaled, sponge, start, section),
        [STATE],
    )
    operands = (source, scaled, sponge, start, *received_one)
    shapes, sums, faces = call(
        functools.partial(shape_kernel, sizes),
        [VMEM] * len(operands),
        operands,
        [(7,) + FLAT, (5,) + TILE, (6,) + TILE],
    )
    operands = (base, scaled, shapes, sums, faces, routes, gather, layer, known, *received)
    section, table, *sent = call(
        functools.partial(gradient_kernel, sizes, 0.25 * step_length),
        [VMEM] * len(operands),
        operands,
        [STATE, (devices, CZ)] + message_shapes(5, 2),
        scratch=[pltpu.VMEM((devices, CZ), jnp.float32), pltpu.SemaphoreType.DMA],
        spaces=[pltpu.VMEM, pltpu.HBM] + [pltpu.VMEM] * len(message_shapes(5, 2)),
    )
    table = lax.all_to_all(table.reshape(devices, 1, CZ), AXES, 0, 0, tiled=True)
    received = exchange(sent, 2)
    (base,) = call(
        functools.partial(own_kernel, (third, two_thirds)),
        [VMEM] * 4,
        (scaled, sponge, start, section),
        [STATE],
    )
    operands = (base, table.reshape(devices, CZ), *received)
    adjoint, gradient = call(
        functools.partial(last_kernel, sizes),
        [VMEM] * len(operands),
        operands,
        [STATE, (1, 5 * BOXES)],
        scratch=[state, pltpu.VMEM((1, 5 * BOXES), jnp.float32), pltpu.SemaphoreType.DMA((6,))],
        spaces=[pltpu.HBM] * 2,
    )
    return adjoint.reshape(state_shape), gradient


def solution(mesh):
    in_specs = (
        P(None, "gx", "gy", "gz"),
        P("gx", "gy", "gz"),
        P(None, "gx", "gy", "gz"),
        P("gx", "gy", "gz"),
        P("gx", "gy", "gz"),
        P("gx", "gy", "gz"),
        P(),
        P(),
        P(),
    )
    out_specs = (P(None, "gx", "gy", "gz"), P(("gx", "gy", "gz"), None))
    return jax.shard_map(body, mesh=mesh, in_specs=in_specs, out_specs=out_specs, check_vma=False)
```

```python
import functools

import jax
import jax.numpy as jnp
from jax import lax
from jax.experimental import pallas as pl
from jax.experimental.pallas import tpu as pltpu
from jax.sharding import PartitionSpec as P

CX = 8
CY = 8
CZ = 128
BZ = 16
BOXES = CZ // BZ
ROWS = CX * CY

AXES = ("gx", "gy", "gz")

step_length = 0.14
third = 1.0 / 3.0
two_thirds = 2.0 / 3.0

BASE = 5 * BOXES

TILE = (CY, CZ)
FLAT = (ROWS, CZ)
STATE = (5,) + FLAT


def pairings(sizes, axis, near_axis):
    size = sizes[axis]
    first, second = [], []
    for x in range(sizes[0]):
        for y in range(sizes[1]):
            for z in range(sizes[2]):
                here = [x, y, z]
                index = (x * sizes[1] + y) * sizes[2] + z
                place = here[axis]
                other = list(here)
                other[axis] = place ^ 1
                first.append((index, (other[0] * sizes[1] + other[1]) * sizes[2] + other[2]))
                other = list(here)
                if 0 < place < size - 1 or near_axis == axis:
                    other[axis] = (place + (1 if place % 2 else -1)) % size
                else:
                    other[near_axis] = here[near_axis] ^ 1
                second.append((index, (other[0] * sizes[1] + other[1]) * sizes[2] + other[2]))
    return first, second if size > 2 else None


def first_round(sizes):
    x, y, z = pairings(sizes, 0, 1), pairings(sizes, 1, 1), pairings(sizes, 2, 1)
    if sizes[0] > 2:
        plane = sizes[1] * sizes[2]
        first, second = dict(z[0]), dict(x[1])
        for index in range(plane):
            first[index], second[index] = second[index], first[index]
        x, z = (x[0], sorted(second.items())), (sorted(first.items()), z[1])
    return x, y, z


def at_start():
    return lax.axis_index(AXES[0]) == 0


class ZFields:
    def __init__(self, x_second, z_first):
        self.x_second, self.z_first = x_second, z_first

    def __getitem__(self, index):
        return jnp.where(at_start(), self.x_second[index], self.z_first[index])


def positions():
    return [lax.axis_index(axis) for axis in AXES]


def tile_at(x):
    return slice(x * CY, (x + 1) * CY)


def row_at(y):
    return pl.ds(y, CX, stride=CY)


def partials_of(adjoint, speed, density, stiffness, inverse, direction):
    components = [speed * component for component in adjoint]
    row = 1 + direction
    components[row] = components[row] + (density * adjoint[0] + stiffness * adjoint[4])
    components[4] = components[4] + adjoint[row] * inverse
    return components


def faces_at(state, scaled, rows, direction):
    adjoint = [state[component, rows, :] for component in range(5)]
    return partials_of(
        adjoint,
        scaled[direction, rows, :],
        scaled[3, rows, :],
        scaled[4, rows, :],
        scaled[5, rows, :],
        direction,
    )


def pack_lanes(fields):
    lanes = (lax.broadcasted_iota(jnp.int32, TILE, 1) + (CZ - BASE)) % CZ // 2
    tiles = []
    for index, field in enumerate(fields):
        for x in range(CX):
            k = index * CX + x
            tile = field[x]
            tiles.append(None if tile is None else pltpu.roll(tile, (BASE + 2 * k + 1) % CZ, 1))
    bit = 1
    while len(tiles) > 1:
        upper = (lanes & bit) != 0
        pairs = []
        for at in range(0, len(tiles), 2):
            low, high = tiles[at], tiles[at + 1] if at + 1 < len(tiles) else None
            if low is None or high is None:
                pairs.append(high if low is None else low)
            else:
                pairs.append(jnp.where(upper, high, low))
        tiles, bit = pairs, 2 * bit
    return tiles[0]


def put_pair(low, high, position, outs):
    even = position % 2 == 0
    for index, (below, above) in enumerate(zip(low, high)):
        outs[0][index] = jnp.where(even, above, below)
        if outs[1] is not None:
            outs[1][index] = jnp.where(even, below, above)


def outer_faces(state, scaled):
    x_low = faces_at(state, scaled, tile_at(0), 0)
    x_high = faces_at(state, scaled, tile_at(CX - 1), 0)
    y_low = faces_at(state, scaled, row_at(0), 1)
    y_high = faces_at(state, scaled, row_at(CY - 1), 1)
    z_tiles = [faces_at(state, scaled, tile_at(x), 2) for x in range(CX)]
    z_fields = [[z_tiles[x][component] for x in range(CX)] for component in range(5)]
    return x_low, x_high, y_low, y_high, z_fields


def put_messages(state, scaled, source, outs):
    here = positions()
    x_low, x_high, y_low, y_high, z_fields = outer_faces(state, scaled)
    if source is not None:
        x_low.append(source[tile_at(0), :])
        x_high.append(source[tile_at(CX - 1), :])
        y_low.append(source[row_at(0), :])
        y_high.append(source[row_at(CY - 1), :])
        z_fields.append([source[tile_at(x), :] for x in range(CX)])
    outs[2][0][0] = pack_lanes(z_fields)
    for index in range(1, outs[2][0].shape[0]):
        outs[2][0][index] = jnp.zeros(TILE, jnp.float32)
    put_pair(x_low, x_high, here[0], outs[0])
    put_pair(y_low, y_high, here[1], outs[1])


def sort_pair(first, second, position, size):
    even = position % 2 == 0
    zero = jnp.zeros_like(first)
    if second is None:
        return jnp.where(even, zero, first), jnp.where(even, first, zero)
    below = jnp.where(position == 0, zero, jnp.where(even, second, first))
    above = jnp.where(position == size - 1, zero, jnp.where(even, first, second))
    return below, above


def sorted_field(refs, index, position, size):
    first, second = refs
    return sort_pair(first[index], None if second is None else second[index], position, size)


def sorted_lanes(refs, position, size):
    return sorted_field(refs, 0, position, size)


def add_halo(base, received, weight, sizes, out, finish=None, z_halo=None):
    here = positions()
    lanes = lax.broadcasted_iota(jnp.int32, TILE, 1)
    edges = (lanes == 0) | (lanes == CZ - 1)
    if z_halo is None:
        z_below, z_above = sorted_lanes(received[2], here[2], sizes[2])
        z_halo = jnp.where(
            lanes % 2 == 0, pltpu.roll(z_above, CZ - 1, 1), -pltpu.roll(z_below, 1, 1)
        )
    z_halo = weight * z_halo
    for component in range(5):
        x_below, x_above = sorted_field(received[0], component, here[0], sizes[0])
        y_below, y_above = sorted_field(received[1], component, here[1], sizes[1])
        for x in range(CX):
            k = component * CX + x
            value = base[component, tile_at(x), :]
            value = value + jnp.where(edges, pltpu.roll(z_halo, (CZ - 1 - BASE - 2 * k) % CZ, 1), 0.0)
            if x == 0:
                value = value - weight * x_below
            if x == CX - 1:
                value = value + weight * x_above
            out[component, tile_at(x), :] = value
        out[component, row_at(0), :] = out[component, row_at(0), :] - weight * y_below
        out[component, row_at(CY - 1), :] = out[component, row_at(CY - 1), :] + weight * y_above
        if finish is not None:
            finish(component)


ORDERS = (
    ((1, 0), (0, 1), (0, 0), (1, 1), (2, 0), (2, 1)),
    ((1, 0), (0, 0), (0, 1), (1, 1)),
    ((0, 0), (1, 1), (2, 0), (2, 1), (1, 0), (0, 1)),
)


def message_keys(sizes, sent, stage):
    keys = [key for key in ORDERS[stage] if key[1] == 0 or sizes[key[0]] > 2]
    return [key for key in keys if not (sent and key == (2, 1))]


def split(refs, sizes, stage, sent=False):
    refs, out = list(refs), [[None, None] for axis in range(3)]
    for axis, which in message_keys(sizes, sent, stage):
        out[axis][which] = refs.pop(0)
    if stage == 0 and not sent and sizes[0] > 2:
        out[2][0] = ZFields(out[0][1], out[2][0])
    return out, refs


def first_kernel(sizes, level, adjoint, density, velocity, stiffness, sponge, source, *refs):
    adjoint_now, sponge_now, source_now, scaled, base, *refs = refs
    outs, scratch = split(refs, sizes, 0, True)
    level_now, density_now, velocity_now, stiffness_now, arrived = scratch
    targets = (
        level_now, density_now, velocity_now, stiffness_now, adjoint_now, sponge_now, source_now
    )
    copies = [
        pltpu.make_async_copy(there, here, arrived.at[index])
        for index, (there, here) in enumerate(
            zip((level, density, velocity, stiffness, adjoint, sponge, source), targets)
        )
    ]
    for copy in copies:
        copy.start()
    level_copy, density_copy, velocity_copy, stiffness_copy, *other_copies = copies
    level_copy.wait()
    here = positions()
    own_level = level_now[here[0], here[2], here[1]]
    half_inverse = 0.5 * lax.shift_left(jnp.int32(1), own_level).astype(jnp.float32)
    density_copy.wait()
    scaled[3] = half_inverse * density_now[...]
    scaled[5] = half_inverse / density_now[...]
    velocity_copy.wait()
    for direction in range(3):
        scaled[direction] = half_inverse * velocity_now[direction]
    stiffness_copy.wait()
    scaled[4] = half_inverse * stiffness_now[...]
    for copy in other_copies:
        copy.wait()
    tiles = own_part((0.0, 1.0), scaled, sponge_now, None, adjoint_now, base)
    x_low = tiles[0][0] + [source_now[tile_at(0), :]]
    x_high = tiles[CX - 1][0] + [source_now[tile_at(CX - 1), :]]
    y_low = faces_at(adjoint_now, scaled, row_at(0), 1) + [source_now[row_at(0), :]]
    y_high = faces_at(adjoint_now, scaled, row_at(CY - 1), 1) + [source_now[row_at(CY - 1), :]]
    put_pair(x_low, x_high, here[0], outs[0])
    put_pair(y_low, y_high, here[1], outs[1])
    along = [
        [[tiles[x][direction][component] for x in range(CX)] for component in range(5)]
        for direction in range(3)
    ]
    along[2].append([source_now[tile_at(x), :] for x in range(CX)])
    for index, fields in enumerate(
        (
            along[2],
            [[base[component, tile_at(x), :] for x in range(CX)] for component in range(5)],
            [[tile if x in (0, CX - 1) else None for x, tile in enumerate(f)] for f in along[0]],
            along[1],
            [[scaled[row, tile_at(x), :] for x in range(CX)] for row in range(2, 6)],
        )
    ):
        outs[2][0][index] = pack_lanes(fields)
    if sizes[0] > 2:

        @pl.when(at_start())
        def _():
            for index in range(5):
                outs[0][1][index] = outs[2][0][index]


def own_kernel(weights, scaled, sponge, start, state, out):
    own_part(weights, scaled, sponge, start, state, out)


def own_part(weights, scaled, sponge, start, state, out):
    keep, blend = weights
    rows = lax.broadcasted_iota(jnp.int32, TILE, 0)
    lanes = lax.broadcasted_iota(jnp.int32, TILE, 1)
    tiles = [
        [faces_at(state, scaled, tile_at(x), direction) for direction in range(3)]
        for x in range(CX)
    ]
    for x in range(CX):
        damp = sponge[tile_at(x), :]
        for component in range(5):
            total = None
            if x < CX - 1:
                total = tiles[x + 1][0][component]
            if x > 0:
                before = tiles[x - 1][0][component]
                total = -before if total is None else total - before
            part = tiles[x][1][component]
            total = total + jnp.where(rows == CY - 1, 0.0, pltpu.roll(part, CY - 1, 0))
            total = total - jnp.where(rows == 0, 0.0, pltpu.roll(part, 1, 0))
            part = tiles[x][2][component]
            total = total + jnp.where(lanes == CZ - 1, 0.0, pltpu.roll(part, CZ - 1, 1))
            total = total - jnp.where(lanes == 0, 0.0, pltpu.roll(part, 1, 1))
            value = state[component, tile_at(x), :]
            value = blend * (value + step_length * (total - damp * value))
            if keep:
                value = value + keep * start[component, tile_at(x), :]
            out[component, tile_at(x), :] = value
    return tiles


def shape_kernel(sizes, source, scaled, sponge, start, *refs):
    sources, (shapes, sums, faces) = split(refs, sizes, 0)
    rows = lax.broadcasted_iota(jnp.int32, TILE, 0)
    lanes = lax.broadcasted_iota(jnp.int32, TILE, 1)
    outer = step_length * two_thirds
    inner = outer * step_length
    totals = [None] * 5
    for x in range(CX):
        at = tile_at(x)
        shape = source[at, :]
        along_x = jnp.zeros(TILE, jnp.float32)
        if x > 0:
            along_x = along_x + source[tile_at(x - 1), :]
        if x < CX - 1:
            along_x = along_x - source[tile_at(x + 1), :]
        along_y = jnp.where(rows == 0, 0.0, pltpu.roll(shape, 1, 0)) - jnp.where(
            rows == CY - 1, 0.0, pltpu.roll(shape, CY - 1, 0)
        )
        before = inner * jnp.where(lanes == 0, 0.0, pltpu.roll(shape, 1, 1))
        after = inner * jnp.where(lanes == CZ - 1, 0.0, pltpu.roll(shape, CZ - 1, 1))
        along_x, along_y = inner * along_x, inner * along_y
        own = outer * shape * (1.0 - step_length * sponge[at, :])
        own = own + scaled[0, at, :] * along_x + scaled[1, at, :] * along_y
        for index, value in enumerate(
            (own, scaled[2, at, :] * before, scaled[2, at, :] * after, along_x, along_y, before, after)
        ):
            shapes[index, at, :] = value
        weighted = (step_length * third) * shape
        for component in range(5):
            value = weighted * start[component, at, :]
            totals[component] = value if totals[component] is None else totals[component] + value
    for component in range(5):
        sums[component] = totals[component]
    here = positions()
    x_below, x_above = sorted_field(sources[0], 5, here[0], sizes[0])
    y_below, y_above = sorted_field(sources[1], 5, here[1], sizes[1])
    z_below, z_above = sorted_lanes(sources[2], here[2], sizes[2])
    aligned_above = jnp.zeros(TILE, jnp.float32)
    aligned_below = jnp.zeros(TILE, jnp.float32)
    for component in range(5):
        group = (lanes >= BASE) & ((lanes - BASE) // (2 * CX) == component)
        shift = 2 * CX * (component - 5)
        aligned_above = jnp.where(
            group & (lanes % 2 == 0), pltpu.roll(z_above, (shift - 1) % CZ, 1), aligned_above
        )
        aligned_below = jnp.where(
            group & (lanes % 2 == 1), pltpu.roll(z_below, (shift + 1) % CZ, 1), aligned_below
        )
    for index, (sign, face) in enumerate(
        (
            (-inner, x_above),
            (inner, x_below),
            (-inner, y_above),
            (inner, y_below),
            (-inner, aligned_above),
            (inner, aligned_below),
        )
    ):
        faces[index] = sign * face


def stage_kernel(sizes, weight, base, scaled, routes, *refs):
    received, (section, *outs) = split(refs, sizes, 0)
    add_halo(base, received, weight, sizes, section)
    outs = split(outs, sizes, 1, True)[0]
    here = positions()
    x_low, x_high, y_low, y_high, z_fields = outer_faces(section, scaled)
    lanes = lax.broadcasted_iota(jnp.int32, TILE, 1)
    rows = lax.broadcasted_iota(jnp.int32, TILE, 0)
    place = (lanes + (CZ - BASE)) % CZ // 2 % CX
    x_below, x_above = sorted_field(received[2], 2, here[2], sizes[2])
    y_below, y_above = sorted_field(received[2], 3, here[2], sizes[2])
    far = 2 * (CX - 1)
    x_high.append(jnp.where(place == 0, both_layers(x_below, x_above, -far), 0.0))
    x_low.append(jnp.where(place == CX - 1, both_layers(x_below, x_above, far), 0.0))
    y_layers = both_layers(y_below, y_above, 0)
    y_high.append(jnp.where(rows == 0, pltpu.roll(y_layers, 1, 0), 0.0))
    y_low.append(jnp.where(rows == CY - 1, pltpu.roll(y_layers, CY - 1, 0), 0.0))
    put_pair(x_low, x_high, here[0], outs[0])
    put_pair(y_low, y_high, here[1], outs[1])


def both_layers(below, above, shift):
    lanes = lax.broadcasted_iota(jnp.int32, TILE, 1)
    return jnp.where(
        lanes % 2 == 0,
        pltpu.roll(above, (shift - 1) % CZ, 1),
        pltpu.roll(below, (shift + 1) % CZ, 1),
    )


def layer_partials(state, layer):
    group = 2 * CX
    return (
        layer[0] * state
        + layer[1] * pltpu.roll(state, 3 * group, 1)
        + layer[2] * pltpu.roll(state, CZ - group, 1)
        + layer[3] * pltpu.roll(state, group, 1)
    )


def layer_kernel(sizes, own, *refs):
    received, (layer, known) = split(refs, sizes, 0)
    here = positions()
    lanes = lax.broadcasted_iota(jnp.int32, TILE, 1)
    even = lanes % 2 == 0
    inside = (lanes >= BASE) & (lanes < BASE + 5 * 2 * CX)
    group = (lanes - BASE) // (2 * CX)
    below, above = sorted_field(received[2], 4, here[2], sizes[2])
    packed = jnp.where(even, 1.0, -1.0) * both_layers(below, above, 0)
    speed = jnp.zeros(TILE, jnp.float32)
    for component in range(5):
        speed = jnp.where(group == component, pltpu.roll(packed, 2 * CX * component, 1), speed)
    layer[0] = jnp.where(inside, speed, 0.0)
    layer[1] = jnp.where(inside & (group == 3), pltpu.roll(packed, 2 * CX * 2, 1), 0.0)
    layer[2] = jnp.where(inside & (group == 3), pltpu.roll(packed, 2 * CX, 1), 0.0)
    layer[3] = jnp.where(inside & (group == 4), pltpu.roll(packed, 2 * CX, 1), 0.0)
    below, above = sorted_field(received[2], 1, here[2], sizes[2])
    state = both_layers(below, above, 0)
    state = state + step_length * jnp.where(even, -own[0], own[0])
    known[...] = layer_partials(jnp.where(inside, state, 0.0), layer)


def sublane_total(tile):
    for shift in (4, 2, 1):
        tile = tile + pltpu.roll(tile, shift, 0)
    return tile


def three_parts(value):
    parts = []
    for _ in range(3):
        part = value.astype(jnp.bfloat16)
        parts.append(part)
        value = value - part.astype(jnp.float32)
    return parts


def product(value, matrix):
    count = value.shape[0]
    assert count % 16 == 0
    stacked = jnp.concatenate(three_parts(value), axis=0)
    result = jnp.dot(stacked, matrix, preferred_element_type=jnp.float32)
    return result[:count] + result[count : 2 * count] + result[2 * count :]


def target_kernel(sizes, patches, owners, routes, gather):
    here = positions()
    shape = routes.shape
    rows = lax.broadcasted_iota(jnp.int32, shape, 0)
    lanes = lax.broadcasted_iota(jnp.int32, shape, 1) % (CY * CY)
    chosen = jnp.zeros(shape, jnp.bool_)
    for index, offset in enumerate(OFFSETS):
        if offset is None:
            continue
        place = [
            jnp.clip(here[axis] + offset[axis], 0, sizes[axis] - 1) for axis in range(3)
        ]
        target = owners[patches[place[0], place[2], place[1]]]
        chosen = chosen | ((lanes // CY == index) & (rows == target))
    routes[...] = jnp.where(chosen, 1.0, 0.0).astype(jnp.bfloat16)
    rows = lax.broadcasted_iota(jnp.int32, (CZ, CZ), 0)
    lanes = lax.broadcasted_iota(jnp.int32, (CZ, CZ), 1)
    for component in range(5):
        ones = lanes == BOXES * component + rows // BZ
        gather[component * CZ : (component + 1) * CZ, :] = jnp.where(ones, 1.0, 0.0).astype(
            jnp.bfloat16
        )
    for index, box in enumerate((0, BOXES - 1)):
        ones = (lanes == BOXES * ((rows - BASE) // (2 * CX)) + box) & (rows >= BASE)
        ones = ones & (rows < BASE + 5 * 2 * CX)
        start = (5 + index) * CZ
        gather[start : start + CZ, :] = jnp.where(ones, 1.0, 0.0).astype(jnp.bfloat16)


OFFSETS = (
    (0, 0, 0),
    (1, 0, 0),
    (-1, 0, 0),
    (0, 1, 0),
    (0, -1, 0),
    None,
    (0, 0, 1),
    (0, 0, -1),
)


def gradient_kernel(
    sizes, weight, base, scaled, shapes, sums, faces, routes, gather, layer, known, *refs
):
    received, (section, table, *rest) = split(refs, sizes, 1)
    outs, (rows_out, sent) = split(rest, sizes, 2, True)
    here = positions()
    x_below, x_above = sorted_field(received[0], 5, here[0], sizes[0])
    y_below, y_above = sorted_field(received[1], 5, here[1], sizes[1])
    late = step_length * ((x_above - x_below) + (y_above - y_below))
    z_halo = known[...] + layer_partials(late, layer)
    add_halo(base, received, weight, sizes, section, z_halo=z_halo)
    x_low, x_high, y_low, y_high, z_fields = outer_faces(section, scaled)
    packed = pack_lanes(z_fields)
    main = [sums[component] for component in range(5)]
    before = [None] * 5
    after = [None] * 5

    def accumulate(totals, component, value):
        old = totals[component]
        totals[component] = value if old is None else old + value

    for x in range(CX):
        at = tile_at(x)
        state = [section[component, at, :] for component in range(5)]
        own, lane_before, lane_after, along_x, along_y, shape_before, shape_after = (
            shapes[index, at, :] for index in range(7)
        )
        push = scaled[3, at, :] * state[0] + scaled[4, at, :] * state[4]
        drawn = [scaled[5, at, :] * state[1 + direction] for direction in range(3)]
        for component in range(5):
            accumulate(main, component, own * state[component])
            accumulate(before, component, lane_before * state[component])
            accumulate(after, component, lane_after * state[component])
        accumulate(main, 1, along_x * push)
        accumulate(main, 2, along_y * push)
        accumulate(before, 3, shape_before * push)
        accumulate(after, 3, shape_after * push)
        accumulate(main, 4, along_x * drawn[0] + along_y * drawn[1])
        accumulate(before, 4, shape_before * drawn[2])
        accumulate(after, 4, shape_after * drawn[2])
    columns = []
    zero = jnp.zeros(TILE, jnp.float32)
    for f in range(5):
        own = main[f] + pltpu.roll(before[f], CZ - 1, 1) - pltpu.roll(after[f], 1, 1)
        columns.append(
            jnp.concatenate(
                [own, faces[0] * x_high[f], faces[1] * x_low[f], faces[2] * y_high[f], faces[3] * y_low[f], zero],
                axis=0,
            )
        )
    blocks = product(jnp.concatenate(columns, axis=1), gather[: 5 * CZ, :])
    above = jnp.concatenate([faces[4] * packed, zero], axis=1)
    below = jnp.concatenate([zero, faces[5] * packed], axis=1)
    z_blocks = product(jnp.concatenate([above, below], axis=0), gather[5 * CZ :, :])
    blocks = jnp.concatenate([blocks, z_blocks], axis=0)
    rows_out[...] = jnp.dot(
        routes[...],
        jnp.concatenate(three_parts(blocks), axis=0),
        preferred_element_type=jnp.float32,
    )
    copy = pltpu.make_async_copy(rows_out, table, sent)
    copy.start()
    put_pair(x_low, x_high, here[0], outs[0])
    put_pair(y_low, y_high, here[1], outs[1])
    outs[2][0][0] = packed
    copy.wait()


def last_kernel(sizes, base, table, *refs):
    received, (out, gradient, done, block, sent) = split(refs, sizes, 2)
    totals = [None] * 4
    for device in range(table.shape[0]):
        part = table[device : device + 1, :]
        old = totals[device % 4]
        totals[device % 4] = part if old is None else old + part
    total = (totals[0] + totals[1]) + (totals[2] + totals[3])
    block[...] = total[:, : 5 * BOXES]
    copies = [pltpu.make_async_copy(block, gradient, sent.at[5])]
    copies[0].start()

    def send(component):
        copy = pltpu.make_async_copy(done.at[component], out.at[component], sent.at[component])
        copy.start()
        copies.append(copy)

    add_halo(base, received, two_thirds * step_length, sizes, done, send)
    for copy in copies:
        copy.wait()


VMEM = pl.BlockSpec(memory_space=pltpu.VMEM)
SMEM = pl.BlockSpec(memory_space=pltpu.SMEM)
HBM = pl.BlockSpec(memory_space=pltpu.HBM)


def call(kernel, in_specs, operands, out_shapes, scratch=(), spaces=None, dtype=jnp.float32):
    spaces = spaces or [pltpu.VMEM] * len(out_shapes)
    operands = [
        pltpu.with_memory_space_constraint(operand, pltpu.HBM) if spec is HBM else operand
        for spec, operand in zip(in_specs, operands)
    ]
    return pl.pallas_call(
        kernel,
        out_shape=[space(shape, dtype) for space, shape in zip(spaces, out_shapes)],
        in_specs=in_specs,
        out_specs=[pl.BlockSpec(memory_space=space) for space in spaces],
        scratch_shapes=list(scratch),
        compiler_params=pltpu.CompilerParams(vmem_limit_bytes=16 * 1024 * 1024),
        cost_estimate=pl.CostEstimate(flops=2000000, bytes_accessed=1000000, transcendentals=0),
    )(*operands)


def body(
    terminal_adjoint,
    density,
    velocity,
    stiffness,
    sponge,
    source_shape,
    brick_level,
    brick_patch,
    patch_owner,
):
    sizes = tuple(lax.axis_size(axis) for axis in AXES)
    later = (pairings(sizes, 0, 1), pairings(sizes, 1, 1), pairings(sizes, 2, 1))
    permutations = (first_round(sizes), later, later)
    devices = patch_owner.shape[0]
    state_shape = terminal_adjoint.shape
    start = terminal_adjoint.reshape(STATE)
    density, stiffness, sponge, source = (
        array.reshape(FLAT) for array in (density, stiffness, sponge, source_shape)
    )
    velocity = velocity.reshape((3,) + FLAT)
    level = jnp.transpose(brick_level, (0, 2, 1))
    patches = jnp.transpose(brick_patch, (0, 2, 1))

    def message_shapes(fields, stage):
        return [
            ({0: 5, 2: 1}.get(stage) if key[0] == 2 else fields,) + TILE
            for key in message_keys(sizes, True, stage)
        ]

    def exchange(messages, stage):
        sends = dict(zip(message_keys(sizes, True, stage), messages))
        sends[2, 1] = sends.get((2, 0))
        return [
            lax.ppermute(sends[key], AXES, permutations[stage][key[0]][key[1]])
            for key in message_keys(sizes, False, stage)
        ]

    flat = pltpu.VMEM(FLAT, jnp.float32)
    state = pltpu.VMEM(STATE, jnp.float32)
    start, sponge, source, scaled, base, *sent = call(
        functools.partial(first_kernel, sizes),
        [HBM] * 7,
        (level, start, density, velocity, stiffness, sponge, source),
        [STATE, FLAT, FLAT, (6,) + FLAT, STATE] + message_shapes(6, 0),
        scratch=[
            pltpu.SMEM(level.shape, jnp.int32),
            flat,
            pltpu.VMEM((3,) + FLAT, jnp.float32),
            flat,
            pltpu.SemaphoreType.DMA((7,)),
        ],
    )
    received_one = exchange(sent, 0)
    own_layers = dict(zip(message_keys(sizes, True, 0), sent))[2, 0]
    routes, gather = call(
        functools.partial(target_kernel, sizes),
        [SMEM] * 2,
        (patches, patch_owner),
        [(devices, 3 * CY * CY), (7 * CZ, CZ)],
        dtype=jnp.bfloat16,
    )
    operands = (base, scaled, routes, *received_one)
    section, *sent = call(
        functools.partial(stage_kernel, sizes, step_length),
        [VMEM] * len(operands),
        operands,
        [STATE] + message_shapes(6, 1),
    )
    received = exchange(sent, 1)
    operands = (own_layers, *received_one)
    layer, known = call(
        functools.partial(layer_kernel, sizes),
        [VMEM] * len(operands),
        operands,
        [(4,) + TILE, TILE],
    )
    (base,) = call(
        functools.partial(own_kernel, (0.75, 0.25)),
        [VMEM] * 4,
        (scaled, sponge, start, section),
        [STATE],
    )
    operands = (source, scaled, sponge, start, *received_one)
    shapes, sums, faces = call(
        functools.partial(shape_kernel, sizes),
        [VMEM] * len(operands),
        operands,
        [(7,) + FLAT, (5,) + TILE, (6,) + TILE],
    )
    operands = (base, scaled, shapes, sums, faces, routes, gather, layer, known, *received)
    section, table, *sent = call(
        functools.partial(gradient_kernel, sizes, 0.25 * step_length),
        [VMEM] * len(operands),
        operands,
        [STATE, (devices, CZ)] + message_shapes(5, 2),
        scratch=[pltpu.VMEM((devices, CZ), jnp.float32), pltpu.SemaphoreType.DMA],
        spaces=[pltpu.VMEM, pltpu.HBM] + [pltpu.VMEM] * len(message_shapes(5, 2)),
    )
    table = lax.all_to_all(table.reshape(devices, 1, CZ), AXES, 0, 0, tiled=True)
    received = exchange(sent, 2)
    (base,) = call(
        functools.partial(own_kernel, (third, two_thirds)),
        [VMEM] * 4,
        (scaled, sponge, start, section),
        [STATE],
    )
    operands = (base, table.reshape(devices, CZ), *received)
    adjoint, gradient = call(
        functools.partial(last_kernel, sizes),
        [VMEM] * len(operands),
        operands,
        [STATE, (1, 5 * BOXES)],
        scratch=[state, pltpu.VMEM((1, 5 * BOXES), jnp.float32), pltpu.SemaphoreType.DMA((6,))],
        spaces=[pltpu.HBM] * 2,
    )
    return adjoint.reshape(state_shape), gradient


def solution(mesh):
    in_specs = (
        P(None, "gx", "gy", "gz"),
        P("gx", "gy", "gz"),
        P(None, "gx", "gy", "gz"),
        P("gx", "gy", "gz"),
        P("gx", "gy", "gz"),
        P("gx", "gy", "gz"),
        P(),
        P(),
        P(),
    )
    out_specs = (P(None, "gx", "gy", "gz"), P(("gx", "gy", "gz"), None))
    return jax.shard_map(body, mesh=mesh, in_specs=in_specs, out_specs=out_specs, check_vma=False)
```

```python
import functools

import jax
import jax.numpy as jnp
from jax import lax
from jax.experimental import pallas as pl
from jax.experimental.pallas import tpu as pltpu
from jax.sharding import PartitionSpec as P

CX = 8
CY = 8
CZ = 128
BZ = 16
BOXES = CZ // BZ
ROWS = CX * CY

AXES = ("gx", "gy", "gz")

step_length = 0.14
third = 1.0 / 3.0
two_thirds = 2.0 / 3.0

BASE = 5 * BOXES

TILE = (CY, CZ)
FLAT = (ROWS, CZ)
STATE = (5,) + FLAT


def pairings(sizes, axis, near_axis):
    size = sizes[axis]
    first, second = [], []
    for x in range(sizes[0]):
        for y in range(sizes[1]):
            for z in range(sizes[2]):
                here = [x, y, z]
                index = (x * sizes[1] + y) * sizes[2] + z
                place = here[axis]
                other = list(here)
                other[axis] = place ^ 1
                first.append((index, (other[0] * sizes[1] + other[1]) * sizes[2] + other[2]))
                other = list(here)
                if 0 < place < size - 1 or near_axis == axis:
                    other[axis] = (place + (1 if place % 2 else -1)) % size
                else:
                    other[near_axis] = here[near_axis] ^ 1
                second.append((index, (other[0] * sizes[1] + other[1]) * sizes[2] + other[2]))
    return first, second if size > 2 else None


def first_round(sizes):
    x, y, z = pairings(sizes, 0, 1), pairings(sizes, 1, 1), pairings(sizes, 2, 1)
    if sizes[0] > 2:
        plane = sizes[1] * sizes[2]
        first, second = dict(z[0]), dict(x[1])
        for index in range(plane):
            first[index], second[index] = second[index], first[index]
        x, z = (x[0], sorted(second.items())), (sorted(first.items()), z[1])
    return x, y, z


def at_start():
    return lax.axis_index(AXES[0]) == 0


class ZFields:
    def __init__(self, x_second, z_first):
        self.x_second, self.z_first = x_second, z_first

    def __getitem__(self, index):
        return jnp.where(at_start(), self.x_second[index], self.z_first[index])


def positions():
    return [lax.axis_index(axis) for axis in AXES]


def tile_at(x):
    return slice(x * CY, (x + 1) * CY)


def row_at(y):
    return pl.ds(y, CX, stride=CY)


def partials_of(adjoint, speed, density, stiffness, inverse, direction):
    components = [speed * component for component in adjoint]
    row = 1 + direction
    components[row] = components[row] + (density * adjoint[0] + stiffness * adjoint[4])
    components[4] = components[4] + adjoint[row] * inverse
    return components


def faces_at(state, scaled, rows, direction):
    adjoint = [state[component, rows, :] for component in range(5)]
    return partials_of(
        adjoint,
        scaled[direction, rows, :],
        scaled[3, rows, :],
        scaled[4, rows, :],
        scaled[5, rows, :],
        direction,
    )


def pack_lanes(fields):
    lanes = (lax.broadcasted_iota(jnp.int32, TILE, 1) + (CZ - BASE)) % CZ // 2
    tiles = []
    for index, field in enumerate(fields):
        for x in range(CX):
            k = index * CX + x
            tile = field[x]
            tiles.append(None if tile is None else pltpu.roll(tile, (BASE + 2 * k + 1) % CZ, 1))
    bit = 1
    while len(tiles) > 1:
        upper = (lanes & bit) != 0
        pairs = []
        for at in range(0, len(tiles), 2):
            low, high = tiles[at], tiles[at + 1] if at + 1 < len(tiles) else None
            if low is None or high is None:
                pairs.append(high if low is None else low)
            else:
                pairs.append(jnp.where(upper, high, low))
        tiles, bit = pairs, 2 * bit
    return tiles[0]


def put_pair(low, high, position, outs):
    even = position % 2 == 0
    for index, (below, above) in enumerate(zip(low, high)):
        outs[0][index] = jnp.where(even, above, below)
        if outs[1] is not None:
            outs[1][index] = jnp.where(even, below, above)


def outer_faces(state, scaled):
    x_low = faces_at(state, scaled, tile_at(0), 0)
    x_high = faces_at(state, scaled, tile_at(CX - 1), 0)
    y_low = faces_at(state, scaled, row_at(0), 1)
    y_high = faces_at(state, scaled, row_at(CY - 1), 1)
    z_tiles = [faces_at(state, scaled, tile_at(x), 2) for x in range(CX)]
    z_fields = [[z_tiles[x][component] for x in range(CX)] for component in range(5)]
    return x_low, x_high, y_low, y_high, z_fields


def put_messages(state, scaled, source, outs):
    here = positions()
    x_low, x_high, y_low, y_high, z_fields = outer_faces(state, scaled)
    if source is not None:
        x_low.append(source[tile_at(0), :])
        x_high.append(source[tile_at(CX - 1), :])
        y_low.append(source[row_at(0), :])
        y_high.append(source[row_at(CY - 1), :])
        z_fields.append([source[tile_at(x), :] for x in range(CX)])
    outs[2][0][0] = pack_lanes(z_fields)
    for index in range(1, outs[2][0].shape[0]):
        outs[2][0][index] = jnp.zeros(TILE, jnp.float32)
    put_pair(x_low, x_high, here[0], outs[0])
    put_pair(y_low, y_high, here[1], outs[1])


def sort_pair(first, second, position, size):
    even = position % 2 == 0
    zero = jnp.zeros_like(first)
    if second is None:
        return jnp.where(even, zero, first), jnp.where(even, first, zero)
    below = jnp.where(position == 0, zero, jnp.where(even, second, first))
    above = jnp.where(position == size - 1, zero, jnp.where(even, first, second))
    return below, above


def sorted_field(refs, index, position, size):
    first, second = refs
    return sort_pair(first[index], None if second is None else second[index], position, size)


def sorted_lanes(refs, position, size):
    return sorted_field(refs, 0, position, size)


def add_halo(base, received, weight, sizes, out, finish=None, z_halo=None):
    here = positions()
    lanes = lax.broadcasted_iota(jnp.int32, TILE, 1)
    edges = (lanes == 0) | (lanes == CZ - 1)
    if z_halo is None:
        z_below, z_above = sorted_lanes(received[2], here[2], sizes[2])
        z_halo = jnp.where(
            lanes % 2 == 0, pltpu.roll(z_above, CZ - 1, 1), -pltpu.roll(z_below, 1, 1)
        )
    z_halo = weight * z_halo
    for component in range(5):
        x_below, x_above = sorted_field(received[0], component, here[0], sizes[0])
        y_below, y_above = sorted_field(received[1], component, here[1], sizes[1])
        for x in range(CX):
            k = component * CX + x
            value = base[component, tile_at(x), :]
            value = value + jnp.where(edges, pltpu.roll(z_halo, (CZ - 1 - BASE - 2 * k) % CZ, 1), 0.0)
            if x == 0:
                value = value - weight * x_below
            if x == CX - 1:
                value = value + weight * x_above
            out[component, tile_at(x), :] = value
        out[component, row_at(0), :] = out[component, row_at(0), :] - weight * y_below
        out[component, row_at(CY - 1), :] = out[component, row_at(CY - 1), :] + weight * y_above
        if finish is not None:
            finish(component)


ORDERS = (
    ((1, 0), (0, 1), (0, 0), (1, 1), (2, 0), (2, 1)),
    ((1, 0), (0, 0), (0, 1), (1, 1)),
    ((0, 0), (1, 1), (0, 1), (2, 0), (2, 1), (1, 0)),
)


def message_keys(sizes, sent, stage):
    keys = [key for key in ORDERS[stage] if key[1] == 0 or sizes[key[0]] > 2]
    return [key for key in keys if not (sent and key == (2, 1))]


def split(refs, sizes, stage, sent=False):
    refs, out = list(refs), [[None, None] for axis in range(3)]
    for axis, which in message_keys(sizes, sent, stage):
        out[axis][which] = refs.pop(0)
    if stage == 0 and not sent and sizes[0] > 2:
        out[2][0] = ZFields(out[0][1], out[2][0])
    return out, refs


def first_kernel(sizes, level, adjoint, density, velocity, stiffness, sponge, source, *refs):
    adjoint_now, sponge_now, source_now, scaled, base, *refs = refs
    outs, scratch = split(refs, sizes, 0, True)
    level_now, density_now, velocity_now, stiffness_now, arrived = scratch
    targets = (
        level_now, density_now, velocity_now, stiffness_now, adjoint_now, sponge_now, source_now
    )
    copies = [
        pltpu.make_async_copy(there, here, arrived.at[index])
        for index, (there, here) in enumerate(
            zip((level, density, velocity, stiffness, adjoint, sponge, source), targets)
        )
    ]
    for copy in copies:
        copy.start()
    level_copy, density_copy, velocity_copy, stiffness_copy, *other_copies = copies
    level_copy.wait()
    here = positions()
    own_level = level_now[here[0], here[2], here[1]]
    half_inverse = 0.5 * lax.shift_left(jnp.int32(1), own_level).astype(jnp.float32)
    density_copy.wait()
    scaled[3] = half_inverse * density_now[...]
    scaled[5] = half_inverse / density_now[...]
    velocity_copy.wait()
    for direction in range(3):
        scaled[direction] = half_inverse * velocity_now[direction]
    stiffness_copy.wait()
    scaled[4] = half_inverse * stiffness_now[...]
    for copy in other_copies:
        copy.wait()
    tiles = own_part((0.0, 1.0), scaled, sponge_now, None, adjoint_now, base)
    x_low = tiles[0][0] + [source_now[tile_at(0), :]]
    x_high = tiles[CX - 1][0] + [source_now[tile_at(CX - 1), :]]
    y_low = faces_at(adjoint_now, scaled, row_at(0), 1) + [source_now[row_at(0), :]]
    y_high = faces_at(adjoint_now, scaled, row_at(CY - 1), 1) + [source_now[row_at(CY - 1), :]]
    put_pair(x_low, x_high, here[0], outs[0])
    put_pair(y_low, y_high, here[1], outs[1])
    along = [
        [[tiles[x][direction][component] for x in range(CX)] for component in range(5)]
        for direction in range(3)
    ]
    along[2].append([source_now[tile_at(x), :] for x in range(CX)])
    for index, fields in enumerate(
        (
            along[2],
            [[base[component, tile_at(x), :] for x in range(CX)] for component in range(5)],
            [[tile if x in (0, CX - 1) else None for x, tile in enumerate(f)] for f in along[0]],
            along[1],
            [[scaled[row, tile_at(x), :] for x in range(CX)] for row in range(2, 6)],
        )
    ):
        outs[2][0][index] = pack_lanes(fields)
    if sizes[0] > 2:

        @pl.when(at_start())
        def _():
            for index in range(5):
                outs[0][1][index] = outs[2][0][index]


def own_kernel(weights, scaled, sponge, start, state, out):
    own_part(weights, scaled, sponge, start, state, out)


def own_part(weights, scaled, sponge, start, state, out):
    keep, blend = weights
    rows = lax.broadcasted_iota(jnp.int32, TILE, 0)
    lanes = lax.broadcasted_iota(jnp.int32, TILE, 1)
    tiles = [
        [faces_at(state, scaled, tile_at(x), direction) for direction in range(3)]
        for x in range(CX)
    ]
    for x in range(CX):
        damp = sponge[tile_at(x), :]
        for component in range(5):
            total = None
            if x < CX - 1:
                total = tiles[x + 1][0][component]
            if x > 0:
                before = tiles[x - 1][0][component]
                total = -before if total is None else total - before
            part = tiles[x][1][component]
            total = total + jnp.where(rows == CY - 1, 0.0, pltpu.roll(part, CY - 1, 0))
            total = total - jnp.where(rows == 0, 0.0, pltpu.roll(part, 1, 0))
            part = tiles[x][2][component]
            total = total + jnp.where(lanes == CZ - 1, 0.0, pltpu.roll(part, CZ - 1, 1))
            total = total - jnp.where(lanes == 0, 0.0, pltpu.roll(part, 1, 1))
            value = state[component, tile_at(x), :]
            value = blend * (value + step_length * (total - damp * value))
            if keep:
                value = value + keep * start[component, tile_at(x), :]
            out[component, tile_at(x), :] = value
    return tiles


def shape_kernel(sizes, source, scaled, sponge, start, *refs):
    sources, (shapes, sums, faces) = split(refs, sizes, 0)
    rows = lax.broadcasted_iota(jnp.int32, TILE, 0)
    lanes = lax.broadcasted_iota(jnp.int32, TILE, 1)
    outer = step_length * two_thirds
    inner = outer * step_length
    totals = [None] * 5
    for x in range(CX):
        at = tile_at(x)
        shape = source[at, :]
        along_x = jnp.zeros(TILE, jnp.float32)
        if x > 0:
            along_x = along_x + source[tile_at(x - 1), :]
        if x < CX - 1:
            along_x = along_x - source[tile_at(x + 1), :]
        along_y = jnp.where(rows == 0, 0.0, pltpu.roll(shape, 1, 0)) - jnp.where(
            rows == CY - 1, 0.0, pltpu.roll(shape, CY - 1, 0)
        )
        before = inner * jnp.where(lanes == 0, 0.0, pltpu.roll(shape, 1, 1))
        after = inner * jnp.where(lanes == CZ - 1, 0.0, pltpu.roll(shape, CZ - 1, 1))
        along_x, along_y = inner * along_x, inner * along_y
        own = outer * shape * (1.0 - step_length * sponge[at, :])
        own = own + scaled[0, at, :] * along_x + scaled[1, at, :] * along_y
        for index, value in enumerate(
            (own, scaled[2, at, :] * before, scaled[2, at, :] * after, along_x, along_y, before, after)
        ):
            shapes[index, at, :] = value
        weighted = (step_length * third) * shape
        for component in range(5):
            value = weighted * start[component, at, :]
            totals[component] = value if totals[component] is None else totals[component] + value
    for component in range(5):
        sums[component] = totals[component]
    here = positions()
    x_below, x_above = sorted_field(sources[0], 5, here[0], sizes[0])
    y_below, y_above = sorted_field(sources[1], 5, here[1], sizes[1])
    z_below, z_above = sorted_lanes(sources[2], here[2], sizes[2])
    aligned_above = jnp.zeros(TILE, jnp.float32)
    aligned_below = jnp.zeros(TILE, jnp.float32)
    for component in range(5):
        group = (lanes >= BASE) & ((lanes - BASE) // (2 * CX) == component)
        shift = 2 * CX * (component - 5)
        aligned_above = jnp.where(
            group & (lanes % 2 == 0), pltpu.roll(z_above, (shift - 1) % CZ, 1), aligned_above
        )
        aligned_below = jnp.where(
            group & (lanes % 2 == 1), pltpu.roll(z_below, (shift + 1) % CZ, 1), aligned_below
        )
    for index, (sign, face) in enumerate(
        (
            (-inner, x_above),
            (inner, x_below),
            (-inner, y_above),
            (inner, y_below),
            (-inner, aligned_above),
            (inner, aligned_below),
        )
    ):
        faces[index] = sign * face


def stage_kernel(sizes, weight, base, scaled, routes, *refs):
    received, (section, *outs) = split(refs, sizes, 0)
    add_halo(base, received, weight, sizes, section)
    outs = split(outs, sizes, 1, True)[0]
    here = positions()
    x_low, x_high, y_low, y_high, z_fields = outer_faces(section, scaled)
    lanes = lax.broadcasted_iota(jnp.int32, TILE, 1)
    rows = lax.broadcasted_iota(jnp.int32, TILE, 0)
    place = (lanes + (CZ - BASE)) % CZ // 2 % CX
    x_below, x_above = sorted_field(received[2], 2, here[2], sizes[2])
    y_below, y_above = sorted_field(received[2], 3, here[2], sizes[2])
    far = 2 * (CX - 1)
    x_high.append(jnp.where(place == 0, both_layers(x_below, x_above, -far), 0.0))
    x_low.append(jnp.where(place == CX - 1, both_layers(x_below, x_above, far), 0.0))
    y_layers = both_layers(y_below, y_above, 0)
    y_high.append(jnp.where(rows == 0, pltpu.roll(y_layers, 1, 0), 0.0))
    y_low.append(jnp.where(rows == CY - 1, pltpu.roll(y_layers, CY - 1, 0), 0.0))
    put_pair(x_low, x_high, here[0], outs[0])
    put_pair(y_low, y_high, here[1], outs[1])


def both_layers(below, above, shift):
    lanes = lax.broadcasted_iota(jnp.int32, TILE, 1)
    return jnp.where(
        lanes % 2 == 0,
        pltpu.roll(above, (shift - 1) % CZ, 1),
        pltpu.roll(below, (shift + 1) % CZ, 1),
    )


def layer_partials(state, layer):
    group = 2 * CX
    return (
        layer[0] * state
        + layer[1] * pltpu.roll(state, 3 * group, 1)
        + layer[2] * pltpu.roll(state, CZ - group, 1)
        + layer[3] * pltpu.roll(state, group, 1)
    )


def layer_kernel(sizes, own, *refs):
    received, (layer, known) = split(refs, sizes, 0)
    here = positions()
    lanes = lax.broadcasted_iota(jnp.int32, TILE, 1)
    even = lanes % 2 == 0
    inside = (lanes >= BASE) & (lanes < BASE + 5 * 2 * CX)
    group = (lanes - BASE) // (2 * CX)
    below, above = sorted_field(received[2], 4, here[2], sizes[2])
    packed = jnp.where(even, 1.0, -1.0) * both_layers(below, above, 0)
    speed = jnp.zeros(TILE, jnp.float32)
    for component in range(5):
        speed = jnp.where(group == component, pltpu.roll(packed, 2 * CX * component, 1), speed)
    layer[0] = jnp.where(inside, speed, 0.0)
    layer[1] = jnp.where(inside & (group == 3), pltpu.roll(packed, 2 * CX * 2, 1), 0.0)
    layer[2] = jnp.where(inside & (group == 3), pltpu.roll(packed, 2 * CX, 1), 0.0)
    layer[3] = jnp.where(inside & (group == 4), pltpu.roll(packed, 2 * CX, 1), 0.0)
    below, above = sorted_field(received[2], 1, here[2], sizes[2])
    state = both_layers(below, above, 0)
    state = state + step_length * jnp.where(even, -own[0], own[0])
    known[...] = layer_partials(jnp.where(inside, state, 0.0), layer)


def sublane_total(tile):
    for shift in (4, 2, 1):
        tile = tile + pltpu.roll(tile, shift, 0)
    return tile


def three_parts(value):
    parts = []
    for _ in range(3):
        part = value.astype(jnp.bfloat16)
        parts.append(part)
        value = value - part.astype(jnp.float32)
    return parts


def product(value, matrix):
    count = value.shape[0]
    assert count % 16 == 0
    stacked = jnp.concatenate(three_parts(value), axis=0)
    result = jnp.dot(stacked, matrix, preferred_element_type=jnp.float32)
    return result[:count] + result[count : 2 * count] + result[2 * count :]


def target_kernel(sizes, patches, owners, routes, gather):
    here = positions()
    shape = routes.shape
    rows = lax.broadcasted_iota(jnp.int32, shape, 0)
    lanes = lax.broadcasted_iota(jnp.int32, shape, 1) % (CY * CY)
    chosen = jnp.zeros(shape, jnp.bool_)
    for index, offset in enumerate(OFFSETS):
        if offset is None:
            continue
        place = [
            jnp.clip(here[axis] + offset[axis], 0, sizes[axis] - 1) for axis in range(3)
        ]
        target = owners[patches[place[0], place[2], place[1]]]
        chosen = chosen | ((lanes // CY == index) & (rows == target))
    routes[...] = jnp.where(chosen, 1.0, 0.0).astype(jnp.bfloat16)
    rows = lax.broadcasted_iota(jnp.int32, (CZ, CZ), 0)
    lanes = lax.broadcasted_iota(jnp.int32, (CZ, CZ), 1)
    for component in range(5):
        ones = lanes == BOXES * component + rows // BZ
        gather[component * CZ : (component + 1) * CZ, :] = jnp.where(ones, 1.0, 0.0).astype(
            jnp.bfloat16
        )
    for index, box in enumerate((0, BOXES - 1)):
        ones = (lanes == BOXES * ((rows - BASE) // (2 * CX)) + box) & (rows >= BASE)
        ones = ones & (rows < BASE + 5 * 2 * CX)
        start = (5 + index) * CZ
        gather[start : start + CZ, :] = jnp.where(ones, 1.0, 0.0).astype(jnp.bfloat16)


OFFSETS = (
    (0, 0, 0),
    (1, 0, 0),
    (-1, 0, 0),
    (0, 1, 0),
    (0, -1, 0),
    None,
    (0, 0, 1),
    (0, 0, -1),
)


def gradient_kernel(
    sizes, weight, base, scaled, shapes, sums, faces, routes, gather, layer, known, *refs
):
    received, (section, table, *rest) = split(refs, sizes, 1)
    outs, (rows_out, sent) = split(rest, sizes, 2, True)
    here = positions()
    x_below, x_above = sorted_field(received[0], 5, here[0], sizes[0])
    y_below, y_above = sorted_field(received[1], 5, here[1], sizes[1])
    late = step_length * ((x_above - x_below) + (y_above - y_below))
    z_halo = known[...] + layer_partials(late, layer)
    add_halo(base, received, weight, sizes, section, z_halo=z_halo)
    x_low, x_high, y_low, y_high, z_fields = outer_faces(section, scaled)
    packed = pack_lanes(z_fields)
    main = [sums[component] for component in range(5)]
    before = [None] * 5
    after = [None] * 5

    def accumulate(totals, component, value):
        old = totals[component]
        totals[component] = value if old is None else old + value

    for x in range(CX):
        at = tile_at(x)
        state = [section[component, at, :] for component in range(5)]
        own, lane_before, lane_after, along_x, along_y, shape_before, shape_after = (
            shapes[index, at, :] for index in range(7)
        )
        push = scaled[3, at, :] * state[0] + scaled[4, at, :] * state[4]
        drawn = [scaled[5, at, :] * state[1 + direction] for direction in range(3)]
        for component in range(5):
            accumulate(main, component, own * state[component])
            accumulate(before, component, lane_before * state[component])
            accumulate(after, component, lane_after * state[component])
        accumulate(main, 1, along_x * push)
        accumulate(main, 2, along_y * push)
        accumulate(before, 3, shape_before * push)
        accumulate(after, 3, shape_after * push)
        accumulate(main, 4, along_x * drawn[0] + along_y * drawn[1])
        accumulate(before, 4, shape_before * drawn[2])
        accumulate(after, 4, shape_after * drawn[2])
    columns = []
    zero = jnp.zeros(TILE, jnp.float32)
    for f in range(5):
        own = main[f] + pltpu.roll(before[f], CZ - 1, 1) - pltpu.roll(after[f], 1, 1)
        columns.append(
            jnp.concatenate(
                [own, faces[0] * x_high[f], faces[1] * x_low[f], faces[2] * y_high[f], faces[3] * y_low[f], zero],
                axis=0,
            )
        )
    blocks = product(jnp.concatenate(columns, axis=1), gather[: 5 * CZ, :])
    above = jnp.concatenate([faces[4] * packed, zero], axis=1)
    below = jnp.concatenate([zero, faces[5] * packed], axis=1)
    z_blocks = product(jnp.concatenate([above, below], axis=0), gather[5 * CZ :, :])
    blocks = jnp.concatenate([blocks, z_blocks], axis=0)
    rows_out[...] = jnp.dot(
        routes[...],
        jnp.concatenate(three_parts(blocks), axis=0),
        preferred_element_type=jnp.float32,
    )
    copy = pltpu.make_async_copy(rows_out, table, sent)
    copy.start()
    put_pair(x_low, x_high, here[0], outs[0])
    put_pair(y_low, y_high, here[1], outs[1])
    outs[2][0][0] = packed
    copy.wait()


def last_kernel(sizes, base, table, *refs):
    received, (out, gradient, done, block, sent) = split(refs, sizes, 2)
    totals = [None] * 4
    for device in range(table.shape[0]):
        part = table[device : device + 1, :]
        old = totals[device % 4]
        totals[device % 4] = part if old is None else old + part
    total = (totals[0] + totals[1]) + (totals[2] + totals[3])
    block[...] = total[:, : 5 * BOXES]
    copies = [pltpu.make_async_copy(block, gradient, sent.at[5])]
    copies[0].start()

    def send(component):
        copy = pltpu.make_async_copy(done.at[component], out.at[component], sent.at[component])
        copy.start()
        copies.append(copy)

    add_halo(base, received, two_thirds * step_length, sizes, done, send)
    for copy in copies:
        copy.wait()


VMEM = pl.BlockSpec(memory_space=pltpu.VMEM)
SMEM = pl.BlockSpec(memory_space=pltpu.SMEM)
HBM = pl.BlockSpec(memory_space=pltpu.HBM)


def call(kernel, in_specs, operands, out_shapes, scratch=(), spaces=None, dtype=jnp.float32):
    spaces = spaces or [pltpu.VMEM] * len(out_shapes)
    operands = [
        pltpu.with_memory_space_constraint(operand, pltpu.HBM) if spec is HBM else operand
        for spec, operand in zip(in_specs, operands)
    ]
    return pl.pallas_call(
        kernel,
        out_shape=[space(shape, dtype) for space, shape in zip(spaces, out_shapes)],
        in_specs=in_specs,
        out_specs=[pl.BlockSpec(memory_space=space) for space in spaces],
        scratch_shapes=list(scratch),
        compiler_params=pltpu.CompilerParams(vmem_limit_bytes=16 * 1024 * 1024),
        cost_estimate=pl.CostEstimate(flops=2000000, bytes_accessed=1000000, transcendentals=0),
    )(*operands)


def body(
    terminal_adjoint,
    density,
    velocity,
    stiffness,
    sponge,
    source_shape,
    brick_level,
    brick_patch,
    patch_owner,
):
    sizes = tuple(lax.axis_size(axis) for axis in AXES)
    later = (pairings(sizes, 0, 1), pairings(sizes, 1, 1), pairings(sizes, 2, 1))
    permutations = (first_round(sizes), later, later)
    devices = patch_owner.shape[0]
    state_shape = terminal_adjoint.shape
    start = terminal_adjoint.reshape(STATE)
    density, stiffness, sponge, source = (
        array.reshape(FLAT) for array in (density, stiffness, sponge, source_shape)
    )
    velocity = velocity.reshape((3,) + FLAT)
    level = jnp.transpose(brick_level, (0, 2, 1))
    patches = jnp.transpose(brick_patch, (0, 2, 1))

    def message_shapes(fields, stage):
        return [
            ({0: 5, 2: 1}.get(stage) if key[0] == 2 else fields,) + TILE
            for key in message_keys(sizes, True, stage)
        ]

    def exchange(messages, stage):
        sends = dict(zip(message_keys(sizes, True, stage), messages))
        sends[2, 1] = sends.get((2, 0))
        return [
            lax.ppermute(sends[key], AXES, permutations[stage][key[0]][key[1]])
            for key in message_keys(sizes, False, stage)
        ]

    flat = pltpu.VMEM(FLAT, jnp.float32)
    state = pltpu.VMEM(STATE, jnp.float32)
    start, sponge, source, scaled, base, *sent = call(
        functools.partial(first_kernel, sizes),
        [HBM] * 7,
        (level, start, density, velocity, stiffness, sponge, source),
        [STATE, FLAT, FLAT, (6,) + FLAT, STATE] + message_shapes(6, 0),
        scratch=[
            pltpu.SMEM(level.shape, jnp.int32),
            flat,
            pltpu.VMEM((3,) + FLAT, jnp.float32),
            flat,
            pltpu.SemaphoreType.DMA((7,)),
        ],
    )
    received_one = exchange(sent, 0)
    own_layers = dict(zip(message_keys(sizes, True, 0), sent))[2, 0]
    routes, gather = call(
        functools.partial(target_kernel, sizes),
        [SMEM] * 2,
        (patches, patch_owner),
        [(devices, 3 * CY * CY), (7 * CZ, CZ)],
        dtype=jnp.bfloat16,
    )
    operands = (base, scaled, routes, *received_one)
    section, *sent = call(
        functools.partial(stage_kernel, sizes, step_length),
        [VMEM] * len(operands),
        operands,
        [STATE] + message_shapes(6, 1),
    )
    received = exchange(sent, 1)
    operands = (own_layers, *received_one)
    layer, known = call(
        functools.partial(layer_kernel, sizes),
        [VMEM] * len(operands),
        operands,
        [(4,) + TILE, TILE],
    )
    (base,) = call(
        functools.partial(own_kernel, (0.75, 0.25)),
        [VMEM] * 4,
        (scaled, sponge, start, section),
        [STATE],
    )
    operands = (source, scaled, sponge, start, *received_one)
    shapes, sums, faces = call(
        functools.partial(shape_kernel, sizes),
        [VMEM] * len(operands),
        operands,
        [(7,) + FLAT, (5,) + TILE, (6,) + TILE],
    )
    operands = (base, scaled, shapes, sums, faces, routes, gather, layer, known, *received)
    section, table, *sent = call(
        functools.partial(gradient_kernel, sizes, 0.25 * step_length),
        [VMEM] * len(operands),
        operands,
        [STATE, (devices, CZ)] + message_shapes(5, 2),
        scratch=[pltpu.VMEM((devices, CZ), jnp.float32), pltpu.SemaphoreType.DMA],
        spaces=[pltpu.VMEM, pltpu.HBM] + [pltpu.VMEM] * len(message_shapes(5, 2)),
    )
    table = lax.all_to_all(table.reshape(devices, 1, CZ), AXES, 0, 0, tiled=True)
    received = exchange(sent, 2)
    (base,) = call(
        functools.partial(own_kernel, (third, two_thirds)),
        [VMEM] * 4,
        (scaled, sponge, start, section),
        [STATE],
    )
    operands = (base, table.reshape(devices, CZ), *received)
    adjoint, gradient = call(
        functools.partial(last_kernel, sizes),
        [VMEM] * len(operands),
        operands,
        [STATE, (1, 5 * BOXES)],
        scratch=[state, pltpu.VMEM((1, 5 * BOXES), jnp.float32), pltpu.SemaphoreType.DMA((6,))],
        spaces=[pltpu.HBM] * 2,
    )
    return adjoint.reshape(state_shape), gradient


def solution(mesh):
    in_specs = (
        P(None, "gx", "gy", "gz"),
        P("gx", "gy", "gz"),
        P(None, "gx", "gy", "gz"),
        P("gx", "gy", "gz"),
        P("gx", "gy", "gz"),
        P("gx", "gy", "gz"),
        P(),
        P(),
        P(),
    )
    out_specs = (P(None, "gx", "gy", "gz"), P(("gx", "gy", "gz"), None))
    return jax.shard_map(body, mesh=mesh, in_specs=in_specs, out_specs=out_specs, check_vma=False)
```

```python
import functools

import jax
import jax.numpy as jnp
from jax import lax
from jax.experimental import pallas as pl
from jax.experimental.pallas import tpu as pltpu
from jax.sharding import PartitionSpec as P

CX = 8
CY = 8
CZ = 128
BZ = 16
BOXES = CZ // BZ
ROWS = CX * CY

AXES = ("gx", "gy", "gz")

step_length = 0.14
third = 1.0 / 3.0
two_thirds = 2.0 / 3.0

BASE = 5 * BOXES

TILE = (CY, CZ)
FLAT = (ROWS, CZ)
STATE = (5,) + FLAT


def pairings(sizes, axis, near_axis):
    size = sizes[axis]
    first, second = [], []
    for x in range(sizes[0]):
        for y in range(sizes[1]):
            for z in range(sizes[2]):
                here = [x, y, z]
                index = (x * sizes[1] + y) * sizes[2] + z
                place = here[axis]
                other = list(here)
                other[axis] = place ^ 1
                first.append((index, (other[0] * sizes[1] + other[1]) * sizes[2] + other[2]))
                other = list(here)
                if 0 < place < size - 1 or near_axis == axis:
                    other[axis] = (place + (1 if place % 2 else -1)) % size
                else:
                    other[near_axis] = here[near_axis] ^ 1
                second.append((index, (other[0] * sizes[1] + other[1]) * sizes[2] + other[2]))
    return first, second if size > 2 else None


def first_round(sizes):
    x, y, z = pairings(sizes, 0, 1), pairings(sizes, 1, 1), pairings(sizes, 2, 1)
    if sizes[0] > 2:
        plane = sizes[1] * sizes[2]
        first, second = dict(z[0]), dict(x[1])
        for index in range(plane):
            first[index], second[index] = second[index], first[index]
        x, z = (x[0], sorted(second.items())), (sorted(first.items()), z[1])
    return x, y, z


def at_start():
    return lax.axis_index(AXES[0]) == 0


class ZFields:
    def __init__(self, x_second, z_first):
        self.x_second, self.z_first = x_second, z_first

    def __getitem__(self, index):
        return jnp.where(at_start(), self.x_second[index], self.z_first[index])


def positions():
    return [lax.axis_index(axis) for axis in AXES]


def tile_at(x):
    return slice(x * CY, (x + 1) * CY)


def row_at(y):
    return pl.ds(y, CX, stride=CY)


def partials_of(adjoint, speed, density, stiffness, inverse, direction):
    components = [speed * component for component in adjoint]
    row = 1 + direction
    components[row] = components[row] + (density * adjoint[0] + stiffness * adjoint[4])
    components[4] = components[4] + adjoint[row] * inverse
    return components


def faces_at(state, scaled, rows, direction):
    adjoint = [state[component, rows, :] for component in range(5)]
    return partials_of(
        adjoint,
        scaled[direction, rows, :],
        scaled[3, rows, :],
        scaled[4, rows, :],
        scaled[5, rows, :],
        direction,
    )


def pack_lanes(fields):
    lanes = (lax.broadcasted_iota(jnp.int32, TILE, 1) + (CZ - BASE)) % CZ // 2
    tiles = []
    for index, field in enumerate(fields):
        for x in range(CX):
            k = index * CX + x
            tile = field[x]
            tiles.append(None if tile is None else pltpu.roll(tile, (BASE + 2 * k + 1) % CZ, 1))
    bit = 1
    while len(tiles) > 1:
        upper = (lanes & bit) != 0
        pairs = []
        for at in range(0, len(tiles), 2):
            low, high = tiles[at], tiles[at + 1] if at + 1 < len(tiles) else None
            if low is None or high is None:
                pairs.append(high if low is None else low)
            else:
                pairs.append(jnp.where(upper, high, low))
        tiles, bit = pairs, 2 * bit
    return tiles[0]


def put_pair(low, high, position, outs):
    even = position % 2 == 0
    for index, (below, above) in enumerate(zip(low, high)):
        outs[0][index] = jnp.where(even, above, below)
        if outs[1] is not None:
            outs[1][index] = jnp.where(even, below, above)


def outer_faces(state, scaled):
    x_low = faces_at(state, scaled, tile_at(0), 0)
    x_high = faces_at(state, scaled, tile_at(CX - 1), 0)
    y_low = faces_at(state, scaled, row_at(0), 1)
    y_high = faces_at(state, scaled, row_at(CY - 1), 1)
    z_tiles = [faces_at(state, scaled, tile_at(x), 2) for x in range(CX)]
    z_fields = [[z_tiles[x][component] for x in range(CX)] for component in range(5)]
    return x_low, x_high, y_low, y_high, z_fields


def put_messages(state, scaled, source, outs):
    here = positions()
    x_low, x_high, y_low, y_high, z_fields = outer_faces(state, scaled)
    if source is not None:
        x_low.append(source[tile_at(0), :])
        x_high.append(source[tile_at(CX - 1), :])
        y_low.append(source[row_at(0), :])
        y_high.append(source[row_at(CY - 1), :])
        z_fields.append([source[tile_at(x), :] for x in range(CX)])
    outs[2][0][0] = pack_lanes(z_fields)
    for index in range(1, outs[2][0].shape[0]):
        outs[2][0][index] = jnp.zeros(TILE, jnp.float32)
    put_pair(x_low, x_high, here[0], outs[0])
    put_pair(y_low, y_high, here[1], outs[1])


def sort_pair(first, second, position, size):
    even = position % 2 == 0
    zero = jnp.zeros_like(first)
    if second is None:
        return jnp.where(even, zero, first), jnp.where(even, first, zero)
    below = jnp.where(position == 0, zero, jnp.where(even, second, first))
    above = jnp.where(position == size - 1, zero, jnp.where(even, first, second))
    return below, above


def sorted_field(refs, index, position, size):
    first, second = refs
    return sort_pair(first[index], None if second is None else second[index], position, size)


def sorted_lanes(refs, position, size):
    return sorted_field(refs, 0, position, size)


def add_halo(base, received, weight, sizes, out, finish=None, z_halo=None):
    here = positions()
    lanes = lax.broadcasted_iota(jnp.int32, TILE, 1)
    edges = (lanes == 0) | (lanes == CZ - 1)
    if z_halo is None:
        z_below, z_above = sorted_lanes(received[2], here[2], sizes[2])
        z_halo = jnp.where(
            lanes % 2 == 0, pltpu.roll(z_above, CZ - 1, 1), -pltpu.roll(z_below, 1, 1)
        )
    z_halo = weight * z_halo
    for component in range(5):
        x_below, x_above = sorted_field(received[0], component, here[0], sizes[0])
        y_below, y_above = sorted_field(received[1], component, here[1], sizes[1])
        for x in range(CX):
            k = component * CX + x
            value = base[component, tile_at(x), :]
            value = value + jnp.where(edges, pltpu.roll(z_halo, (CZ - 1 - BASE - 2 * k) % CZ, 1), 0.0)
            if x == 0:
                value = value - weight * x_below
            if x == CX - 1:
                value = value + weight * x_above
            out[component, tile_at(x), :] = value
        out[component, row_at(0), :] = out[component, row_at(0), :] - weight * y_below
        out[component, row_at(CY - 1), :] = out[component, row_at(CY - 1), :] + weight * y_above
        if finish is not None:
            finish(component)


ORDERS = (
    ((1, 0), (0, 1), (0, 0), (2, 0), (2, 1), (1, 1)),
    ((1, 0), (0, 0), (0, 1), (1, 1)),
    ((0, 0), (1, 1), (0, 1), (2, 0), (2, 1), (1, 0)),
)


def message_keys(sizes, sent, stage):
    keys = [key for key in ORDERS[stage] if key[1] == 0 or sizes[key[0]] > 2]
    return [key for key in keys if not (sent and key == (2, 1))]


def split(refs, sizes, stage, sent=False):
    refs, out = list(refs), [[None, None] for axis in range(3)]
    for axis, which in message_keys(sizes, sent, stage):
        out[axis][which] = refs.pop(0)
    if stage == 0 and not sent and sizes[0] > 2:
        out[2][0] = ZFields(out[0][1], out[2][0])
    return out, refs


def first_kernel(sizes, level, adjoint, density, velocity, stiffness, sponge, source, *refs):
    adjoint_now, sponge_now, source_now, scaled, base, *refs = refs
    outs, scratch = split(refs, sizes, 0, True)
    level_now, density_now, velocity_now, stiffness_now, arrived = scratch
    targets = (
        level_now, density_now, velocity_now, stiffness_now, adjoint_now, sponge_now, source_now
    )
    copies = [
        pltpu.make_async_copy(there, here, arrived.at[index])
        for index, (there, here) in enumerate(
            zip((level, density, velocity, stiffness, adjoint, sponge, source), targets)
        )
    ]
    for copy in copies:
        copy.start()
    level_copy, density_copy, velocity_copy, stiffness_copy, *other_copies = copies
    level_copy.wait()
    here = positions()
    own_level = level_now[here[0], here[2], here[1]]
    half_inverse = 0.5 * lax.shift_left(jnp.int32(1), own_level).astype(jnp.float32)
    density_copy.wait()
    scaled[3] = half_inverse * density_now[...]
    scaled[5] = half_inverse / density_now[...]
    velocity_copy.wait()
    for direction in range(3):
        scaled[direction] = half_inverse * velocity_now[direction]
    stiffness_copy.wait()
    scaled[4] = half_inverse * stiffness_now[...]
    for copy in other_copies:
        copy.wait()
    tiles = own_part((0.0, 1.0), scaled, sponge_now, None, adjoint_now, base)
    x_low = tiles[0][0] + [source_now[tile_at(0), :]]
    x_high = tiles[CX - 1][0] + [source_now[tile_at(CX - 1), :]]
    y_low = faces_at(adjoint_now, scaled, row_at(0), 1) + [source_now[row_at(0), :]]
    y_high = faces_at(adjoint_now, scaled, row_at(CY - 1), 1) + [source_now[row_at(CY - 1), :]]
    put_pair(x_low, x_high, here[0], outs[0])
    put_pair(y_low, y_high, here[1], outs[1])
    along = [
        [[tiles[x][direction][component] for x in range(CX)] for component in range(5)]
        for direction in range(3)
    ]
    along[2].append([source_now[tile_at(x), :] for x in range(CX)])
    for index, fields in enumerate(
        (
            along[2],
            [[base[component, tile_at(x), :] for x in range(CX)] for component in range(5)],
            [[tile if x in (0, CX - 1) else None for x, tile in enumerate(f)] for f in along[0]],
            along[1],
            [[scaled[row, tile_at(x), :] for x in range(CX)] for row in range(2, 6)],
        )
    ):
        outs[2][0][index] = pack_lanes(fields)
    if sizes[0] > 2:

        @pl.when(at_start())
        def _():
            for index in range(5):
                outs[0][1][index] = outs[2][0][index]


def own_kernel(weights, scaled, sponge, start, state, out):
    own_part(weights, scaled, sponge, start, state, out)


def own_part(weights, scaled, sponge, start, state, out):
    keep, blend = weights
    rows = lax.broadcasted_iota(jnp.int32, TILE, 0)
    lanes = lax.broadcasted_iota(jnp.int32, TILE, 1)
    tiles = [
        [faces_at(state, scaled, tile_at(x), direction) for direction in range(3)]
        for x in range(CX)
    ]
    for x in range(CX):
        damp = sponge[tile_at(x), :]
        for component in range(5):
            total = None
            if x < CX - 1:
                total = tiles[x + 1][0][component]
            if x > 0:
                before = tiles[x - 1][0][component]
                total = -before if total is None else total - before
            part = tiles[x][1][component]
            total = total + jnp.where(rows == CY - 1, 0.0, pltpu.roll(part, CY - 1, 0))
            total = total - jnp.where(rows == 0, 0.0, pltpu.roll(part, 1, 0))
            part = tiles[x][2][component]
            total = total + jnp.where(lanes == CZ - 1, 0.0, pltpu.roll(part, CZ - 1, 1))
            total = total - jnp.where(lanes == 0, 0.0, pltpu.roll(part, 1, 1))
            value = state[component, tile_at(x), :]
            value = blend * (value + step_length * (total - damp * value))
            if keep:
                value = value + keep * start[component, tile_at(x), :]
            out[component, tile_at(x), :] = value
    return tiles


def shape_kernel(sizes, source, scaled, sponge, start, *refs):
    sources, (shapes, sums, faces) = split(refs, sizes, 0)
    rows = lax.broadcasted_iota(jnp.int32, TILE, 0)
    lanes = lax.broadcasted_iota(jnp.int32, TILE, 1)
    outer = step_length * two_thirds
    inner = outer * step_length
    totals = [None] * 5
    for x in range(CX):
        at = tile_at(x)
        shape = source[at, :]
        along_x = jnp.zeros(TILE, jnp.float32)
        if x > 0:
            along_x = along_x + source[tile_at(x - 1), :]
        if x < CX - 1:
            along_x = along_x - source[tile_at(x + 1), :]
        along_y = jnp.where(rows == 0, 0.0, pltpu.roll(shape, 1, 0)) - jnp.where(
            rows == CY - 1, 0.0, pltpu.roll(shape, CY - 1, 0)
        )
        before = inner * jnp.where(lanes == 0, 0.0, pltpu.roll(shape, 1, 1))
        after = inner * jnp.where(lanes == CZ - 1, 0.0, pltpu.roll(shape, CZ - 1, 1))
        along_x, along_y = inner * along_x, inner * along_y
        own = outer * shape * (1.0 - step_length * sponge[at, :])
        own = own + scaled[0, at, :] * along_x + scaled[1, at, :] * along_y
        for index, value in enumerate(
            (own, scaled[2, at, :] * before, scaled[2, at, :] * after, along_x, along_y, before, after)
        ):
            shapes[index, at, :] = value
        weighted = (step_length * third) * shape
        for component in range(5):
            value = weighted * start[component, at, :]
            totals[component] = value if totals[component] is None else totals[component] + value
    for component in range(5):
        sums[component] = totals[component]
    here = positions()
    x_below, x_above = sorted_field(sources[0], 5, here[0], sizes[0])
    y_below, y_above = sorted_field(sources[1], 5, here[1], sizes[1])
    z_below, z_above = sorted_lanes(sources[2], here[2], sizes[2])
    aligned_above = jnp.zeros(TILE, jnp.float32)
    aligned_below = jnp.zeros(TILE, jnp.float32)
    for component in range(5):
        group = (lanes >= BASE) & ((lanes - BASE) // (2 * CX) == component)
        shift = 2 * CX * (component - 5)
        aligned_above = jnp.where(
            group & (lanes % 2 == 0), pltpu.roll(z_above, (shift - 1) % CZ, 1), aligned_above
        )
        aligned_below = jnp.where(
            group & (lanes % 2 == 1), pltpu.roll(z_below, (shift + 1) % CZ, 1), aligned_below
        )
    for index, (sign, face) in enumerate(
        (
            (-inner, x_above),
            (inner, x_below),
            (-inner, y_above),
            (inner, y_below),
            (-inner, aligned_above),
            (inner, aligned_below),
        )
    ):
        faces[index] = sign * face


def stage_kernel(sizes, weight, base, scaled, routes, *refs):
    received, (section, *outs) = split(refs, sizes, 0)
    add_halo(base, received, weight, sizes, section)
    outs = split(outs, sizes, 1, True)[0]
    here = positions()
    x_low, x_high, y_low, y_high, z_fields = outer_faces(section, scaled)
    lanes = lax.broadcasted_iota(jnp.int32, TILE, 1)
    rows = lax.broadcasted_iota(jnp.int32, TILE, 0)
    place = (lanes + (CZ - BASE)) % CZ // 2 % CX
    x_below, x_above = sorted_field(received[2], 2, here[2], sizes[2])
    y_below, y_above = sorted_field(received[2], 3, here[2], sizes[2])
    far = 2 * (CX - 1)
    x_high.append(jnp.where(place == 0, both_layers(x_below, x_above, -far), 0.0))
    x_low.append(jnp.where(place == CX - 1, both_layers(x_below, x_above, far), 0.0))
    y_layers = both_layers(y_below, y_above, 0)
    y_high.append(jnp.where(rows == 0, pltpu.roll(y_layers, 1, 0), 0.0))
    y_low.append(jnp.where(rows == CY - 1, pltpu.roll(y_layers, CY - 1, 0), 0.0))
    put_pair(x_low, x_high, here[0], outs[0])
    put_pair(y_low, y_high, here[1], outs[1])


def both_layers(below, above, shift):
    lanes = lax.broadcasted_iota(jnp.int32, TILE, 1)
    return jnp.where(
        lanes % 2 == 0,
        pltpu.roll(above, (shift - 1) % CZ, 1),
        pltpu.roll(below, (shift + 1) % CZ, 1),
    )


def layer_partials(state, layer):
    group = 2 * CX
    return (
        layer[0] * state
        + layer[1] * pltpu.roll(state, 3 * group, 1)
        + layer[2] * pltpu.roll(state, CZ - group, 1)
        + layer[3] * pltpu.roll(state, group, 1)
    )


def layer_kernel(sizes, own, *refs):
    received, (layer, known) = split(refs, sizes, 0)
    here = positions()
    lanes = lax.broadcasted_iota(jnp.int32, TILE, 1)
    even = lanes % 2 == 0
    inside = (lanes >= BASE) & (lanes < BASE + 5 * 2 * CX)
    group = (lanes - BASE) // (2 * CX)
    below, above = sorted_field(received[2], 4, here[2], sizes[2])
    packed = jnp.where(even, 1.0, -1.0) * both_layers(below, above, 0)
    speed = jnp.zeros(TILE, jnp.float32)
    for component in range(5):
        speed = jnp.where(group == component, pltpu.roll(packed, 2 * CX * component, 1), speed)
    layer[0] = jnp.where(inside, speed, 0.0)
    layer[1] = jnp.where(inside & (group == 3), pltpu.roll(packed, 2 * CX * 2, 1), 0.0)
    layer[2] = jnp.where(inside & (group == 3), pltpu.roll(packed, 2 * CX, 1), 0.0)
    layer[3] = jnp.where(inside & (group == 4), pltpu.roll(packed, 2 * CX, 1), 0.0)
    below, above = sorted_field(received[2], 1, here[2], sizes[2])
    state = both_layers(below, above, 0)
    state = state + step_length * jnp.where(even, -own[0], own[0])
    known[...] = layer_partials(jnp.where(inside, state, 0.0), layer)


def sublane_total(tile):
    for shift in (4, 2, 1):
        tile = tile + pltpu.roll(tile, shift, 0)
    return tile


def three_parts(value):
    parts = []
    for _ in range(3):
        part = value.astype(jnp.bfloat16)
        parts.append(part)
        value = value - part.astype(jnp.float32)
    return parts


def product(value, matrix):
    count = value.shape[0]
    assert count % 16 == 0
    stacked = jnp.concatenate(three_parts(value), axis=0)
    result = jnp.dot(stacked, matrix, preferred_element_type=jnp.float32)
    return result[:count] + result[count : 2 * count] + result[2 * count :]


def target_kernel(sizes, patches, owners, routes, gather):
    here = positions()
    shape = routes.shape
    rows = lax.broadcasted_iota(jnp.int32, shape, 0)
    lanes = lax.broadcasted_iota(jnp.int32, shape, 1) % (CY * CY)
    chosen = jnp.zeros(shape, jnp.bool_)
    for index, offset in enumerate(OFFSETS):
        if offset is None:
            continue
        place = [
            jnp.clip(here[axis] + offset[axis], 0, sizes[axis] - 1) for axis in range(3)
        ]
        target = owners[patches[place[0], place[2], place[1]]]
        chosen = chosen | ((lanes // CY == index) & (rows == target))
    routes[...] = jnp.where(chosen, 1.0, 0.0).astype(jnp.bfloat16)
    rows = lax.broadcasted_iota(jnp.int32, (CZ, CZ), 0)
    lanes = lax.broadcasted_iota(jnp.int32, (CZ, CZ), 1)
    for component in range(5):
        ones = lanes == BOXES * component + rows // BZ
        gather[component * CZ : (component + 1) * CZ, :] = jnp.where(ones, 1.0, 0.0).astype(
            jnp.bfloat16
        )
    for index, box in enumerate((0, BOXES - 1)):
        ones = (lanes == BOXES * ((rows - BASE) // (2 * CX)) + box) & (rows >= BASE)
        ones = ones & (rows < BASE + 5 * 2 * CX)
        start = (5 + index) * CZ
        gather[start : start + CZ, :] = jnp.where(ones, 1.0, 0.0).astype(jnp.bfloat16)


OFFSETS = (
    (0, 0, 0),
    (1, 0, 0),
    (-1, 0, 0),
    (0, 1, 0),
    (0, -1, 0),
    None,
    (0, 0, 1),
    (0, 0, -1),
)


def gradient_kernel(
    sizes, weight, base, scaled, shapes, sums, faces, routes, gather, layer, known, *refs
):
    received, (section, table, *rest) = split(refs, sizes, 1)
    outs, (rows_out, sent) = split(rest, sizes, 2, True)
    here = positions()
    x_below, x_above = sorted_field(received[0], 5, here[0], sizes[0])
    y_below, y_above = sorted_field(received[1], 5, here[1], sizes[1])
    late = step_length * ((x_above - x_below) + (y_above - y_below))
    z_halo = known[...] + layer_partials(late, layer)
    add_halo(base, received, weight, sizes, section, z_halo=z_halo)
    x_low, x_high, y_low, y_high, z_fields = outer_faces(section, scaled)
    packed = pack_lanes(z_fields)
    main = [sums[component] for component in range(5)]
    before = [None] * 5
    after = [None] * 5

    def accumulate(totals, component, value):
        old = totals[component]
        totals[component] = value if old is None else old + value

    for x in range(CX):
        at = tile_at(x)
        state = [section[component, at, :] for component in range(5)]
        own, lane_before, lane_after, along_x, along_y, shape_before, shape_after = (
            shapes[index, at, :] for index in range(7)
        )
        push = scaled[3, at, :] * state[0] + scaled[4, at, :] * state[4]
        drawn = [scaled[5, at, :] * state[1 + direction] for direction in range(3)]
        for component in range(5):
            accumulate(main, component, own * state[component])
            accumulate(before, component, lane_before * state[component])
            accumulate(after, component, lane_after * state[component])
        accumulate(main, 1, along_x * push)
        accumulate(main, 2, along_y * push)
        accumulate(before, 3, shape_before * push)
        accumulate(after, 3, shape_after * push)
        accumulate(main, 4, along_x * drawn[0] + along_y * drawn[1])
        accumulate(before, 4, shape_before * drawn[2])
        accumulate(after, 4, shape_after * drawn[2])
    columns = []
    zero = jnp.zeros(TILE, jnp.float32)
    for f in range(5):
        own = main[f] + pltpu.roll(before[f], CZ - 1, 1) - pltpu.roll(after[f], 1, 1)
        columns.append(
            jnp.concatenate(
                [own, faces[0] * x_high[f], faces[1] * x_low[f], faces[2] * y_high[f], faces[3] * y_low[f], zero],
                axis=0,
            )
        )
    blocks = product(jnp.concatenate(columns, axis=1), gather[: 5 * CZ, :])
    above = jnp.concatenate([faces[4] * packed, zero], axis=1)
    below = jnp.concatenate([zero, faces[5] * packed], axis=1)
    z_blocks = product(jnp.concatenate([above, below], axis=0), gather[5 * CZ :, :])
    blocks = jnp.concatenate([blocks, z_blocks], axis=0)
    rows_out[...] = jnp.dot(
        routes[...],
        jnp.concatenate(three_parts(blocks), axis=0),
        preferred_element_type=jnp.float32,
    )
    copy = pltpu.make_async_copy(rows_out, table, sent)
    copy.start()
    put_pair(x_low, x_high, here[0], outs[0])
    put_pair(y_low, y_high, here[1], outs[1])
    outs[2][0][0] = packed
    copy.wait()


def last_kernel(sizes, base, table, *refs):
    received, (out, gradient, done, block, sent) = split(refs, sizes, 2)
    totals = [None] * 4
    for device in range(table.shape[0]):
        part = table[device : device + 1, :]
        old = totals[device % 4]
        totals[device % 4] = part if old is None else old + part
    total = (totals[0] + totals[1]) + (totals[2] + totals[3])
    block[...] = total[:, : 5 * BOXES]
    copies = [pltpu.make_async_copy(block, gradient, sent.at[5])]
    copies[0].start()

    def send(component):
        copy = pltpu.make_async_copy(done.at[component], out.at[component], sent.at[component])
        copy.start()
        copies.append(copy)

    add_halo(base, received, two_thirds * step_length, sizes, done, send)
    for copy in copies:
        copy.wait()


VMEM = pl.BlockSpec(memory_space=pltpu.VMEM)
SMEM = pl.BlockSpec(memory_space=pltpu.SMEM)
HBM = pl.BlockSpec(memory_space=pltpu.HBM)


def call(kernel, in_specs, operands, out_shapes, scratch=(), spaces=None, dtype=jnp.float32):
    spaces = spaces or [pltpu.VMEM] * len(out_shapes)
    operands = [
        pltpu.with_memory_space_constraint(operand, pltpu.HBM) if spec is HBM else operand
        for spec, operand in zip(in_specs, operands)
    ]
    return pl.pallas_call(
        kernel,
        out_shape=[space(shape, dtype) for space, shape in zip(spaces, out_shapes)],
        in_specs=in_specs,
        out_specs=[pl.BlockSpec(memory_space=space) for space in spaces],
        scratch_shapes=list(scratch),
        compiler_params=pltpu.CompilerParams(vmem_limit_bytes=16 * 1024 * 1024),
        cost_estimate=pl.CostEstimate(flops=2000000, bytes_accessed=1000000, transcendentals=0),
    )(*operands)


def body(
    terminal_adjoint,
    density,
    velocity,
    stiffness,
    sponge,
    source_shape,
    brick_level,
    brick_patch,
    patch_owner,
):
    sizes = tuple(lax.axis_size(axis) for axis in AXES)
    later = (pairings(sizes, 0, 1), pairings(sizes, 1, 1), pairings(sizes, 2, 1))
    permutations = (first_round(sizes), later, later)
    devices = patch_owner.shape[0]
    state_shape = terminal_adjoint.shape
    start = terminal_adjoint.reshape(STATE)
    density, stiffness, sponge, source = (
        array.reshape(FLAT) for array in (density, stiffness, sponge, source_shape)
    )
    velocity = velocity.reshape((3,) + FLAT)
    level = jnp.transpose(brick_level, (0, 2, 1))
    patches = jnp.transpose(brick_patch, (0, 2, 1))

    def message_shapes(fields, stage):
        return [
            ({0: 5, 2: 1}.get(stage) if key[0] == 2 else fields,) + TILE
            for key in message_keys(sizes, True, stage)
        ]

    def exchange(messages, stage):
        sends = dict(zip(message_keys(sizes, True, stage), messages))
        sends[2, 1] = sends.get((2, 0))
        return [
            lax.ppermute(sends[key], AXES, permutations[stage][key[0]][key[1]])
            for key in message_keys(sizes, False, stage)
        ]

    flat = pltpu.VMEM(FLAT, jnp.float32)
    state = pltpu.VMEM(STATE, jnp.float32)
    start, sponge, source, scaled, base, *sent = call(
        functools.partial(first_kernel, sizes),
        [HBM] * 7,
        (level, start, density, velocity, stiffness, sponge, source),
        [STATE, FLAT, FLAT, (6,) + FLAT, STATE] + message_shapes(6, 0),
        scratch=[
            pltpu.SMEM(level.shape, jnp.int32),
            flat,
            pltpu.VMEM((3,) + FLAT, jnp.float32),
            flat,
            pltpu.SemaphoreType.DMA((7,)),
        ],
    )
    received_one = exchange(sent, 0)
    own_layers = dict(zip(message_keys(sizes, True, 0), sent))[2, 0]
    routes, gather = call(
        functools.partial(target_kernel, sizes),
        [SMEM] * 2,
        (patches, patch_owner),
        [(devices, 3 * CY * CY), (7 * CZ, CZ)],
        dtype=jnp.bfloat16,
    )
    operands = (base, scaled, routes, *received_one)
    section, *sent = call(
        functools.partial(stage_kernel, sizes, step_length),
        [VMEM] * len(operands),
        operands,
        [STATE] + message_shapes(6, 1),
    )
    received = exchange(sent, 1)
    operands = (own_layers, *received_one)
    layer, known = call(
        functools.partial(layer_kernel, sizes),
        [VMEM] * len(operands),
        operands,
        [(4,) + TILE, TILE],
    )
    (base,) = call(
        functools.partial(own_kernel, (0.75, 0.25)),
        [VMEM] * 4,
        (scaled, sponge, start, section),
        [STATE],
    )
    operands = (source, scaled, sponge, start, *received_one)
    shapes, sums, faces = call(
        functools.partial(shape_kernel, sizes),
        [VMEM] * len(operands),
        operands,
        [(7,) + FLAT, (5,) + TILE, (6,) + TILE],
    )
    operands = (base, scaled, shapes, sums, faces, routes, gather, layer, known, *received)
    section, table, *sent = call(
        functools.partial(gradient_kernel, sizes, 0.25 * step_length),
        [VMEM] * len(operands),
        operands,
        [STATE, (devices, CZ)] + message_shapes(5, 2),
        scratch=[pltpu.VMEM((devices, CZ), jnp.float32), pltpu.SemaphoreType.DMA],
        spaces=[pltpu.VMEM, pltpu.HBM] + [pltpu.VMEM] * len(message_shapes(5, 2)),
    )
    table = lax.all_to_all(table.reshape(devices, 1, CZ), AXES, 0, 0, tiled=True)
    received = exchange(sent, 2)
    (base,) = call(
        functools.partial(own_kernel, (third, two_thirds)),
        [VMEM] * 4,
        (scaled, sponge, start, section),
        [STATE],
    )
    operands = (base, table.reshape(devices, CZ), *received)
    adjoint, gradient = call(
        functools.partial(last_kernel, sizes),
        [VMEM] * len(operands),
        operands,
        [STATE, (1, 5 * BOXES)],
        scratch=[state, pltpu.VMEM((1, 5 * BOXES), jnp.float32), pltpu.SemaphoreType.DMA((6,))],
        spaces=[pltpu.HBM] * 2,
    )
    return adjoint.reshape(state_shape), gradient


def solution(mesh):
    in_specs = (
        P(None, "gx", "gy", "gz"),
        P("gx", "gy", "gz"),
        P(None, "gx", "gy", "gz"),
        P("gx", "gy", "gz"),
        P("gx", "gy", "gz"),
        P("gx", "gy", "gz"),
        P(),
        P(),
        P(),
    )
    out_specs = (P(None, "gx", "gy", "gz"), P(("gx", "gy", "gz"), None))
    return jax.shard_map(body, mesh=mesh, in_specs=in_specs, out_specs=out_specs, check_vma=False)
```

```python
import functools

import jax
import jax.numpy as jnp
from jax import lax
from jax.experimental import pallas as pl
from jax.experimental.pallas import tpu as pltpu
from jax.sharding import PartitionSpec as P

CX = 8
CY = 8
CZ = 128
BZ = 16
BOXES = CZ // BZ
ROWS = CX * CY

AXES = ("gx", "gy", "gz")

step_length = 0.14
third = 1.0 / 3.0
two_thirds = 2.0 / 3.0

BASE = 5 * BOXES

TILE = (CY, CZ)
FLAT = (ROWS, CZ)
STATE = (5,) + FLAT


def pairings(sizes, axis, near_axis):
    size = sizes[axis]
    first, second = [], []
    for x in range(sizes[0]):
        for y in range(sizes[1]):
            for z in range(sizes[2]):
                here = [x, y, z]
                index = (x * sizes[1] + y) * sizes[2] + z
                place = here[axis]
                other = list(here)
                other[axis] = place ^ 1
                first.append((index, (other[0] * sizes[1] + other[1]) * sizes[2] + other[2]))
                other = list(here)
                if 0 < place < size - 1 or near_axis == axis:
                    other[axis] = (place + (1 if place % 2 else -1)) % size
                else:
                    other[near_axis] = here[near_axis] ^ 1
                second.append((index, (other[0] * sizes[1] + other[1]) * sizes[2] + other[2]))
    return first, second if size > 2 else None


def first_round(sizes):
    x, y, z = pairings(sizes, 0, 1), pairings(sizes, 1, 1), pairings(sizes, 2, 1)
    if sizes[0] > 2:
        plane = sizes[1] * sizes[2]
        first, second = dict(z[0]), dict(x[1])
        for index in range(plane):
            first[index], second[index] = second[index], first[index]
        x, z = (x[0], sorted(second.items())), (sorted(first.items()), z[1])
    return x, y, z


def at_start():
    return lax.axis_index(AXES[0]) == 0


class ZFields:
    def __init__(self, x_second, z_first):
        self.x_second, self.z_first = x_second, z_first

    def __getitem__(self, index):
        return jnp.where(at_start(), self.x_second[index], self.z_first[index])


def positions():
    return [lax.axis_index(axis) for axis in AXES]


def tile_at(x):
    return slice(x * CY, (x + 1) * CY)


def row_at(y):
    return pl.ds(y, CX, stride=CY)


def partials_of(adjoint, speed, density, stiffness, inverse, direction):
    components = [speed * component for component in adjoint]
    row = 1 + direction
    components[row] = components[row] + (density * adjoint[0] + stiffness * adjoint[4])
    components[4] = components[4] + adjoint[row] * inverse
    return components


def faces_at(state, scaled, rows, direction):
    adjoint = [state[component, rows, :] for component in range(5)]
    return partials_of(
        adjoint,
        scaled[direction, rows, :],
        scaled[3, rows, :],
        scaled[4, rows, :],
        scaled[5, rows, :],
        direction,
    )


def pack_lanes(fields):
    lanes = (lax.broadcasted_iota(jnp.int32, TILE, 1) + (CZ - BASE)) % CZ // 2
    tiles = []
    for index, field in enumerate(fields):
        for x in range(CX):
            k = index * CX + x
            tile = field[x]
            tiles.append(None if tile is None else pltpu.roll(tile, (BASE + 2 * k + 1) % CZ, 1))
    bit = 1
    while len(tiles) > 1:
        upper = (lanes & bit) != 0
        pairs = []
        for at in range(0, len(tiles), 2):
            low, high = tiles[at], tiles[at + 1] if at + 1 < len(tiles) else None
            if low is None or high is None:
                pairs.append(high if low is None else low)
            else:
                pairs.append(jnp.where(upper, high, low))
        tiles, bit = pairs, 2 * bit
    return tiles[0]


def put_pair(low, high, position, outs):
    even = position % 2 == 0
    for index, (below, above) in enumerate(zip(low, high)):
        outs[0][index] = jnp.where(even, above, below)
        if outs[1] is not None:
            outs[1][index] = jnp.where(even, below, above)


def outer_faces(state, scaled):
    x_low = faces_at(state, scaled, tile_at(0), 0)
    x_high = faces_at(state, scaled, tile_at(CX - 1), 0)
    y_low = faces_at(state, scaled, row_at(0), 1)
    y_high = faces_at(state, scaled, row_at(CY - 1), 1)
    z_tiles = [faces_at(state, scaled, tile_at(x), 2) for x in range(CX)]
    z_fields = [[z_tiles[x][component] for x in range(CX)] for component in range(5)]
    return x_low, x_high, y_low, y_high, z_fields


def put_messages(state, scaled, source, outs):
    here = positions()
    x_low, x_high, y_low, y_high, z_fields = outer_faces(state, scaled)
    if source is not None:
        x_low.append(source[tile_at(0), :])
        x_high.append(source[tile_at(CX - 1), :])
        y_low.append(source[row_at(0), :])
        y_high.append(source[row_at(CY - 1), :])
        z_fields.append([source[tile_at(x), :] for x in range(CX)])
    outs[2][0][0] = pack_lanes(z_fields)
    for index in range(1, outs[2][0].shape[0]):
        outs[2][0][index] = jnp.zeros(TILE, jnp.float32)
    put_pair(x_low, x_high, here[0], outs[0])
    put_pair(y_low, y_high, here[1], outs[1])


def sort_pair(first, second, position, size):
    even = position % 2 == 0
    zero = jnp.zeros_like(first)
    if second is None:
        return jnp.where(even, zero, first), jnp.where(even, first, zero)
    below = jnp.where(position == 0, zero, jnp.where(even, second, first))
    above = jnp.where(position == size - 1, zero, jnp.where(even, first, second))
    return below, above


def sorted_field(refs, index, position, size):
    first, second = refs
    return sort_pair(first[index], None if second is None else second[index], position, size)


def sorted_lanes(refs, position, size):
    return sorted_field(refs, 0, position, size)


def add_halo(base, received, weight, sizes, out, finish=None, z_halo=None):
    here = positions()
    lanes = lax.broadcasted_iota(jnp.int32, TILE, 1)
    edges = (lanes == 0) | (lanes == CZ - 1)
    if z_halo is None:
        z_below, z_above = sorted_lanes(received[2], here[2], sizes[2])
        z_halo = jnp.where(
            lanes % 2 == 0, pltpu.roll(z_above, CZ - 1, 1), -pltpu.roll(z_below, 1, 1)
        )
    z_halo = weight * z_halo
    for component in range(5):
        x_below, x_above = sorted_field(received[0], component, here[0], sizes[0])
        y_below, y_above = sorted_field(received[1], component, here[1], sizes[1])
        for x in range(CX):
            k = component * CX + x
            value = base[component, tile_at(x), :]
            value = value + jnp.where(edges, pltpu.roll(z_halo, (CZ - 1 - BASE - 2 * k) % CZ, 1), 0.0)
            if x == 0:
                value = value - weight * x_below
            if x == CX - 1:
                value = value + weight * x_above
            out[component, tile_at(x), :] = value
        out[component, row_at(0), :] = out[component, row_at(0), :] - weight * y_below
        out[component, row_at(CY - 1), :] = out[component, row_at(CY - 1), :] + weight * y_above
        if finish is not None:
            finish(component)


ORDERS = (
    ((1, 0), (0, 1), (0, 0), (1, 1), (2, 0), (2, 1)),
    ((1, 0), (0, 0), (0, 1), (1, 1)),
    ((0, 0), (1, 1), (2, 0), (2, 1), (1, 0), (0, 1)),
)


def message_keys(sizes, sent, stage):
    keys = [key for key in ORDERS[stage] if key[1] == 0 or sizes[key[0]] > 2]
    return [key for key in keys if not (sent and key == (2, 1))]


def split(refs, sizes, stage, sent=False):
    refs, out = list(refs), [[None, None] for axis in range(3)]
    for axis, which in message_keys(sizes, sent, stage):
        out[axis][which] = refs.pop(0)
    if stage == 0 and not sent and sizes[0] > 2:
        out[2][0] = ZFields(out[0][1], out[2][0])
    return out, refs


def first_kernel(sizes, level, adjoint, density, velocity, stiffness, sponge, source, *refs):
    adjoint_now, sponge_now, source_now, scaled, base, *refs = refs
    outs, scratch = split(refs, sizes, 0, True)
    level_now, density_now, velocity_now, stiffness_now, arrived = scratch
    targets = (
        level_now, density_now, velocity_now, stiffness_now, adjoint_now, sponge_now, source_now
    )
    copies = [
        pltpu.make_async_copy(there, here, arrived.at[index])
        for index, (there, here) in enumerate(
            zip((level, density, velocity, stiffness, adjoint, sponge, source), targets)
        )
    ]
    for copy in copies:
        copy.start()
    level_copy, density_copy, velocity_copy, stiffness_copy, *other_copies = copies
    level_copy.wait()
    here = positions()
    own_level = level_now[here[0], here[2], here[1]]
    half_inverse = 0.5 * lax.shift_left(jnp.int32(1), own_level).astype(jnp.float32)
    density_copy.wait()
    scaled[3] = half_inverse * density_now[...]
    scaled[5] = half_inverse / density_now[...]
    velocity_copy.wait()
    for direction in range(3):
        scaled[direction] = half_inverse * velocity_now[direction]
    stiffness_copy.wait()
    scaled[4] = half_inverse * stiffness_now[...]
    for copy in other_copies:
        copy.wait()
    tiles = own_part((0.0, 1.0), scaled, sponge_now, None, adjoint_now, base)
    x_low = tiles[0][0] + [source_now[tile_at(0), :]]
    x_high = tiles[CX - 1][0] + [source_now[tile_at(CX - 1), :]]
    y_low = faces_at(adjoint_now, scaled, row_at(0), 1) + [source_now[row_at(0), :]]
    y_high = faces_at(adjoint_now, scaled, row_at(CY - 1), 1) + [source_now[row_at(CY - 1), :]]
    put_pair(x_low, x_high, here[0], outs[0])
    put_pair(y_low, y_high, here[1], outs[1])
    along = [
        [[tiles[x][direction][component] for x in range(CX)] for component in range(5)]
        for direction in range(3)
    ]
    along[2].append([source_now[tile_at(x), :] for x in range(CX)])
    for index, fields in enumerate(
        (
            along[2],
            [[base[component, tile_at(x), :] for x in range(CX)] for component in range(5)],
            [[tile if x in (0, CX - 1) else None for x, tile in enumerate(f)] for f in along[0]],
            along[1],
            [[scaled[row, tile_at(x), :] for x in range(CX)] for row in range(2, 6)],
        )
    ):
        outs[2][0][index] = pack_lanes(fields)
    if sizes[0] > 2:

        @pl.when(at_start())
        def _():
            for index in range(5):
                outs[0][1][index] = outs[2][0][index]


def own_kernel(weights, scaled, sponge, start, state, out):
    own_part(weights, scaled, sponge, start, state, out)


def own_part(weights, scaled, sponge, start, state, out):
    keep, blend = weights
    rows = lax.broadcasted_iota(jnp.int32, TILE, 0)
    lanes = lax.broadcasted_iota(jnp.int32, TILE, 1)
    tiles = [
        [faces_at(state, scaled, tile_at(x), direction) for direction in range(3)]
        for x in range(CX)
    ]
    for x in range(CX):
        damp = sponge[tile_at(x), :]
        for component in range(5):
            total = None
            if x < CX - 1:
                total = tiles[x + 1][0][component]
            if x > 0:
                before = tiles[x - 1][0][component]
                total = -before if total is None else total - before
            part = tiles[x][1][component]
            total = total + jnp.where(rows == CY - 1, 0.0, pltpu.roll(part, CY - 1, 0))
            total = total - jnp.where(rows == 0, 0.0, pltpu.roll(part, 1, 0))
            part = tiles[x][2][component]
            total = total + jnp.where(lanes == CZ - 1, 0.0, pltpu.roll(part, CZ - 1, 1))
            total = total - jnp.where(lanes == 0, 0.0, pltpu.roll(part, 1, 1))
            value = state[component, tile_at(x), :]
            value = blend * (value + step_length * (total - damp * value))
            if keep:
                value = value + keep * start[component, tile_at(x), :]
            out[component, tile_at(x), :] = value
    return tiles


def shape_kernel(sizes, source, scaled, sponge, start, *refs):
    sources, (shapes, sums, faces) = split(refs, sizes, 0)
    rows = lax.broadcasted_iota(jnp.int32, TILE, 0)
    lanes = lax.broadcasted_iota(jnp.int32, TILE, 1)
    outer = step_length * two_thirds
    inner = outer * step_length
    totals = [None] * 5
    for x in range(CX):
        at = tile_at(x)
        shape = source[at, :]
        along_x = jnp.zeros(TILE, jnp.float32)
        if x > 0:
            along_x = along_x + source[tile_at(x - 1), :]
        if x < CX - 1:
            along_x = along_x - source[tile_at(x + 1), :]
        along_y = jnp.where(rows == 0, 0.0, pltpu.roll(shape, 1, 0)) - jnp.where(
            rows == CY - 1, 0.0, pltpu.roll(shape, CY - 1, 0)
        )
        before = inner * jnp.where(lanes == 0, 0.0, pltpu.roll(shape, 1, 1))
        after = inner * jnp.where(lanes == CZ - 1, 0.0, pltpu.roll(shape, CZ - 1, 1))
        along_x, along_y = inner * along_x, inner * along_y
        own = outer * shape * (1.0 - step_length * sponge[at, :])
        own = own + scaled[0, at, :] * along_x + scaled[1, at, :] * along_y
        for index, value in enumerate(
            (own, scaled[2, at, :] * before, scaled[2, at, :] * after, along_x, along_y, before, after)
        ):
            shapes[index, at, :] = value
        weighted = (step_length * third) * shape
        for component in range(5):
            value = weighted * start[component, at, :]
            totals[component] = value if totals[component] is None else totals[component] + value
    for component in range(5):
        sums[component] = totals[component]
    here = positions()
    x_below, x_above = sorted_field(sources[0], 5, here[0], sizes[0])
    y_below, y_above = sorted_field(sources[1], 5, here[1], sizes[1])
    z_below, z_above = sorted_lanes(sources[2], here[2], sizes[2])
    aligned_above = jnp.zeros(TILE, jnp.float32)
    aligned_below = jnp.zeros(TILE, jnp.float32)
    for component in range(5):
        group = (lanes >= BASE) & ((lanes - BASE) // (2 * CX) == component)
        shift = 2 * CX * (component - 5)
        aligned_above = jnp.where(
            group & (lanes % 2 == 0), pltpu.roll(z_above, (shift - 1) % CZ, 1), aligned_above
        )
        aligned_below = jnp.where(
            group & (lanes % 2 == 1), pltpu.roll(z_below, (shift + 1) % CZ, 1), aligned_below
        )
    for index, (sign, face) in enumerate(
        (
            (-inner, x_above),
            (inner, x_below),
            (-inner, y_above),
            (inner, y_below),
            (-inner, aligned_above),
            (inner, aligned_below),
        )
    ):
        faces[index] = sign * face


def stage_kernel(sizes, weight, base, scaled, routes, *refs):
    received, (section, *outs) = split(refs, sizes, 0)
    add_halo(base, received, weight, sizes, section)
    outs = split(outs, sizes, 1, True)[0]
    here = positions()
    x_low, x_high, y_low, y_high, z_fields = outer_faces(section, scaled)
    lanes = lax.broadcasted_iota(jnp.int32, TILE, 1)
    rows = lax.broadcasted_iota(jnp.int32, TILE, 0)
    place = (lanes + (CZ - BASE)) % CZ // 2 % CX
    x_below, x_above = sorted_field(received[2], 2, here[2], sizes[2])
    y_below, y_above = sorted_field(received[2], 3, here[2], sizes[2])
    far = 2 * (CX - 1)
    x_high.append(jnp.where(place == 0, both_layers(x_below, x_above, -far), 0.0))
    x_low.append(jnp.where(place == CX - 1, both_layers(x_below, x_above, far), 0.0))
    y_layers = both_layers(y_below, y_above, 0)
    y_high.append(jnp.where(rows == 0, pltpu.roll(y_layers, 1, 0), 0.0))
    y_low.append(jnp.where(rows == CY - 1, pltpu.roll(y_layers, CY - 1, 0), 0.0))
    put_pair(x_low, x_high, here[0], outs[0])
    put_pair(y_low, y_high, here[1], outs[1])


def both_layers(below, above, shift):
    lanes = lax.broadcasted_iota(jnp.int32, TILE, 1)
    return jnp.where(
        lanes % 2 == 0,
        pltpu.roll(above, (shift - 1) % CZ, 1),
        pltpu.roll(below, (shift + 1) % CZ, 1),
    )


def layer_partials(state, layer):
    group = 2 * CX
    return (
        layer[0] * state
        + layer[1] * pltpu.roll(state, 3 * group, 1)
        + layer[2] * pltpu.roll(state, CZ - group, 1)
        + layer[3] * pltpu.roll(state, group, 1)
    )


def layer_kernel(sizes, own, *refs):
    received, (layer, known) = split(refs, sizes, 0)
    here = positions()
    lanes = lax.broadcasted_iota(jnp.int32, TILE, 1)
    even = lanes % 2 == 0
    inside = (lanes >= BASE) & (lanes < BASE + 5 * 2 * CX)
    group = (lanes - BASE) // (2 * CX)
    below, above = sorted_field(received[2], 4, here[2], sizes[2])
    packed = jnp.where(even, 1.0, -1.0) * both_layers(below, above, 0)
    speed = jnp.zeros(TILE, jnp.float32)
    for component in range(5):
        speed = jnp.where(group == component, pltpu.roll(packed, 2 * CX * component, 1), speed)
    layer[0] = jnp.where(inside, speed, 0.0)
    layer[1] = jnp.where(inside & (group == 3), pltpu.roll(packed, 2 * CX * 2, 1), 0.0)
    layer[2] = jnp.where(inside & (group == 3), pltpu.roll(packed, 2 * CX, 1), 0.0)
    layer[3] = jnp.where(inside & (group == 4), pltpu.roll(packed, 2 * CX, 1), 0.0)
    below, above = sorted_field(received[2], 1, here[2], sizes[2])
    state = both_layers(below, above, 0)
    state = state + step_length * jnp.where(even, -own[0], own[0])
    known[...] = layer_partials(jnp.where(inside, state, 0.0), layer)


def sublane_total(tile):
    for shift in (4, 2, 1):
        tile = tile + pltpu.roll(tile, shift, 0)
    return tile


def three_parts(value):
    parts = []
    for _ in range(3):
        part = value.astype(jnp.bfloat16)
        parts.append(part)
        value = value - part.astype(jnp.float32)
    return parts


def product(value, matrix):
    count = value.shape[0]
    assert count % 16 == 0
    stacked = jnp.concatenate(three_parts(value), axis=0)
    result = jnp.dot(stacked, matrix, preferred_element_type=jnp.float32)
    return result[:count] + result[count : 2 * count] + result[2 * count :]


def target_kernel(sizes, patches, owners, routes, gather):
    here = positions()
    shape = routes.shape
    rows = lax.broadcasted_iota(jnp.int32, shape, 0)
    lanes = lax.broadcasted_iota(jnp.int32, shape, 1) % (CY * CY)
    chosen = jnp.zeros(shape, jnp.bool_)
    for index, offset in enumerate(OFFSETS):
        if offset is None:
            continue
        place = [
            jnp.clip(here[axis] + offset[axis], 0, sizes[axis] - 1) for axis in range(3)
        ]
        target = owners[patches[place[0], place[2], place[1]]]
        chosen = chosen | ((lanes // CY == index) & (rows == target))
    routes[...] = jnp.where(chosen, 1.0, 0.0).astype(jnp.bfloat16)
    rows = lax.broadcasted_iota(jnp.int32, (CZ, CZ), 0)
    lanes = lax.broadcasted_iota(jnp.int32, (CZ, CZ), 1)
    for component in range(5):
        ones = lanes == BOXES * component + rows // BZ
        gather[component * CZ : (component + 1) * CZ, :] = jnp.where(ones, 1.0, 0.0).astype(
            jnp.bfloat16
        )
    for index, box in enumerate((0, BOXES - 1)):
        ones = (lanes == BOXES * ((rows - BASE) // (2 * CX)) + box) & (rows >= BASE)
        ones = ones & (rows < BASE + 5 * 2 * CX)
        start = (5 + index) * CZ
        gather[start : start + CZ, :] = jnp.where(ones, 1.0, 0.0).astype(jnp.bfloat16)


OFFSETS = (
    (0, 0, 0),
    (1, 0, 0),
    (-1, 0, 0),
    (0, 1, 0),
    (0, -1, 0),
    None,
    (0, 0, 1),
    (0, 0, -1),
)


def gradient_kernel(
    sizes, weight, base, scaled, shapes, sums, faces, routes, gather, layer, known, *refs
):
    received, (section, table, *rest) = split(refs, sizes, 1)
    outs, (rows_out, sent) = split(rest, sizes, 2, True)
    here = positions()
    x_below, x_above = sorted_field(received[0], 5, here[0], sizes[0])
    y_below, y_above = sorted_field(received[1], 5, here[1], sizes[1])
    late = step_length * ((x_above - x_below) + (y_above - y_below))
    z_halo = known[...] + layer_partials(late, layer)
    add_halo(base, received, weight, sizes, section, z_halo=z_halo)
    x_low, x_high, y_low, y_high, z_fields = outer_faces(section, scaled)
    packed = pack_lanes(z_fields)
    main = [sums[component] for component in range(5)]
    before = [None] * 5
    after = [None] * 5

    def accumulate(totals, component, value):
        old = totals[component]
        totals[component] = value if old is None else old + value

    for x in range(CX):
        at = tile_at(x)
        state = [section[component, at, :] for component in range(5)]
        own, lane_before, lane_after, along_x, along_y, shape_before, shape_after = (
            shapes[index, at, :] for index in range(7)
        )
        push = scaled[3, at, :] * state[0] + scaled[4, at, :] * state[4]
        drawn = [scaled[5, at, :] * state[1 + direction] for direction in range(3)]
        for component in range(5):
            accumulate(main, component, own * state[component])
            accumulate(before, component, lane_before * state[component])
            accumulate(after, component, lane_after * state[component])
        accumulate(main, 1, along_x * push)
        accumulate(main, 2, along_y * push)
        accumulate(before, 3, shape_before * push)
        accumulate(after, 3, shape_after * push)
        accumulate(main, 4, along_x * drawn[0] + along_y * drawn[1])
        accumulate(before, 4, shape_before * drawn[2])
        accumulate(after, 4, shape_after * drawn[2])
    columns = []
    zero = jnp.zeros(TILE, jnp.float32)
    for f in range(5):
        own = main[f] + pltpu.roll(before[f], CZ - 1, 1) - pltpu.roll(after[f], 1, 1)
        columns.append(
            jnp.concatenate(
                [own, faces[0] * x_high[f], faces[1] * x_low[f], faces[2] * y_high[f], faces[3] * y_low[f], zero],
                axis=0,
            )
        )
    blocks = product(jnp.concatenate(columns, axis=1), gather[: 5 * CZ, :])
    above = jnp.concatenate([faces[4] * packed, zero], axis=1)
    below = jnp.concatenate([zero, faces[5] * packed], axis=1)
    z_blocks = product(jnp.concatenate([above, below], axis=0), gather[5 * CZ :, :])
    blocks = jnp.concatenate([blocks, z_blocks], axis=0)
    rows_out[...] = jnp.dot(
        routes[...],
        jnp.concatenate(three_parts(blocks), axis=0),
        preferred_element_type=jnp.float32,
    )
    copy = pltpu.make_async_copy(rows_out, table, sent)
    copy.start(priority=1)
    put_pair(x_low, x_high, here[0], outs[0])
    put_pair(y_low, y_high, here[1], outs[1])
    outs[2][0][0] = packed
    copy.wait()


def last_kernel(sizes, base, table, *refs):
    received, (out, gradient, done, block, sent) = split(refs, sizes, 2)
    totals = [None] * 4
    for device in range(table.shape[0]):
        part = table[device : device + 1, :]
        old = totals[device % 4]
        totals[device % 4] = part if old is None else old + part
    total = (totals[0] + totals[1]) + (totals[2] + totals[3])
    block[...] = total[:, : 5 * BOXES]
    copies = [pltpu.make_async_copy(block, gradient, sent.at[5])]
    copies[0].start()

    def send(component):
        copy = pltpu.make_async_copy(done.at[component], out.at[component], sent.at[component])
        copy.start()
        copies.append(copy)

    add_halo(base, received, two_thirds * step_length, sizes, done, send)
    for copy in copies:
        copy.wait()


VMEM = pl.BlockSpec(memory_space=pltpu.VMEM)
SMEM = pl.BlockSpec(memory_space=pltpu.SMEM)
HBM = pl.BlockSpec(memory_space=pltpu.HBM)


def call(kernel, in_specs, operands, out_shapes, scratch=(), spaces=None, dtype=jnp.float32):
    spaces = spaces or [pltpu.VMEM] * len(out_shapes)
    operands = [
        pltpu.with_memory_space_constraint(operand, pltpu.HBM) if spec is HBM else operand
        for spec, operand in zip(in_specs, operands)
    ]
    return pl.pallas_call(
        kernel,
        out_shape=[space(shape, dtype) for space, shape in zip(spaces, out_shapes)],
        in_specs=in_specs,
        out_specs=[pl.BlockSpec(memory_space=space) for space in spaces],
        scratch_shapes=list(scratch),
        compiler_params=pltpu.CompilerParams(vmem_limit_bytes=16 * 1024 * 1024),
        cost_estimate=pl.CostEstimate(flops=2000000, bytes_accessed=1000000, transcendentals=0),
    )(*operands)


def body(
    terminal_adjoint,
    density,
    velocity,
    stiffness,
    sponge,
    source_shape,
    brick_level,
    brick_patch,
    patch_owner,
):
    sizes = tuple(lax.axis_size(axis) for axis in AXES)
    later = (pairings(sizes, 0, 1), pairings(sizes, 1, 1), pairings(sizes, 2, 1))
    permutations = (first_round(sizes), later, later)
    devices = patch_owner.shape[0]
    state_shape = terminal_adjoint.shape
    start = terminal_adjoint.reshape(STATE)
    density, stiffness, sponge, source = (
        array.reshape(FLAT) for array in (density, stiffness, sponge, source_shape)
    )
    velocity = velocity.reshape((3,) + FLAT)
    level = jnp.transpose(brick_level, (0, 2, 1))
    patches = jnp.transpose(brick_patch, (0, 2, 1))

    def message_shapes(fields, stage):
        return [
            ({0: 5, 2: 1}.get(stage) if key[0] == 2 else fields,) + TILE
            for key in message_keys(sizes, True, stage)
        ]

    def exchange(messages, stage):
        sends = dict(zip(message_keys(sizes, True, stage), messages))
        sends[2, 1] = sends.get((2, 0))
        return [
            lax.ppermute(sends[key], AXES, permutations[stage][key[0]][key[1]])
            for key in message_keys(sizes, False, stage)
        ]

    flat = pltpu.VMEM(FLAT, jnp.float32)
    state = pltpu.VMEM(STATE, jnp.float32)
    start, sponge, source, scaled, base, *sent = call(
        functools.partial(first_kernel, sizes),
        [HBM] * 7,
        (level, start, density, velocity, stiffness, sponge, source),
        [STATE, FLAT, FLAT, (6,) + FLAT, STATE] + message_shapes(6, 0),
        scratch=[
            pltpu.SMEM(level.shape, jnp.int32),
            flat,
            pltpu.VMEM((3,) + FLAT, jnp.float32),
            flat,
            pltpu.SemaphoreType.DMA((7,)),
        ],
    )
    received_one = exchange(sent, 0)
    own_layers = dict(zip(message_keys(sizes, True, 0), sent))[2, 0]
    routes, gather = call(
        functools.partial(target_kernel, sizes),
        [SMEM] * 2,
        (patches, patch_owner),
        [(devices, 3 * CY * CY), (7 * CZ, CZ)],
        dtype=jnp.bfloat16,
    )
    operands = (base, scaled, routes, *received_one)
    section, *sent = call(
        functools.partial(stage_kernel, sizes, step_length),
        [VMEM] * len(operands),
        operands,
        [STATE] + message_shapes(6, 1),
    )
    received = exchange(sent, 1)
    operands = (own_layers, *received_one)
    layer, known = call(
        functools.partial(layer_kernel, sizes),
        [VMEM] * len(operands),
        operands,
        [(4,) + TILE, TILE],
    )
    (base,) = call(
        functools.partial(own_kernel, (0.75, 0.25)),
        [VMEM] * 4,
        (scaled, sponge, start, section),
        [STATE],
    )
    operands = (source, scaled, sponge, start, *received_one)
    shapes, sums, faces = call(
        functools.partial(shape_kernel, sizes),
        [VMEM] * len(operands),
        operands,
        [(7,) + FLAT, (5,) + TILE, (6,) + TILE],
    )
    operands = (base, scaled, shapes, sums, faces, routes, gather, layer, known, *received)
    section, table, *sent = call(
        functools.partial(gradient_kernel, sizes, 0.25 * step_length),
        [VMEM] * len(operands),
        operands,
        [STATE, (devices, CZ)] + message_shapes(5, 2),
        scratch=[pltpu.VMEM((devices, CZ), jnp.float32), pltpu.SemaphoreType.DMA],
        spaces=[pltpu.VMEM, pltpu.HBM] + [pltpu.VMEM] * len(message_shapes(5, 2)),
    )
    table = lax.all_to_all(table.reshape(devices, 1, CZ), AXES, 0, 0, tiled=True)
    received = exchange(sent, 2)
    (base,) = call(
        functools.partial(own_kernel, (third, two_thirds)),
        [VMEM] * 4,
        (scaled, sponge, start, section),
        [STATE],
    )
    operands = (base, table.reshape(devices, CZ), *received)
    adjoint, gradient = call(
        functools.partial(last_kernel, sizes),
        [VMEM] * len(operands),
        operands,
        [STATE, (1, 5 * BOXES)],
        scratch=[state, pltpu.VMEM((1, 5 * BOXES), jnp.float32), pltpu.SemaphoreType.DMA((6,))],
        spaces=[pltpu.HBM] * 2,
    )
    return adjoint.reshape(state_shape), gradient


def solution(mesh):
    in_specs = (
        P(None, "gx", "gy", "gz"),
        P("gx", "gy", "gz"),
        P(None, "gx", "gy", "gz"),
        P("gx", "gy", "gz"),
        P("gx", "gy", "gz"),
        P("gx", "gy", "gz"),
        P(),
        P(),
        P(),
    )
    out_specs = (P(None, "gx", "gy", "gz"), P(("gx", "gy", "gz"), None))
    return jax.shard_map(body, mesh=mesh, in_specs=in_specs, out_specs=out_specs, check_vma=False)
```
